32 devices in a mesh: lat: 4 (over z), lon: 8 (over y, x, core).
Axes of the slice: x: 2, y: 2, z: 4, core: 2. Of those that a mesh axis runs over, the one named last changes fastest.
Arguments:
- tracers: float32 [2, 48, 512, 1024], P(None, None, 'lat', 'lon'), may hold values from -6 to 6
- east_courant: float32 [48, 512, 1024], P(None, 'lat', 'lon'), may hold values from -0.4 to 0.4
- north_courant: float32 [48, 512, 1024], P(None, 'lat', 'lon'), may hold values from -0.4 to 0.4
- diffusivity: float32 [48, 512, 1024], P(None, 'lat', 'lon'), may hold values from 0.05 to 20
- land_sea: int32 [512, 1024], P('lat', 'lon'), may hold values 0 or 1
- fluxes: float32 [6, 262144], P(None, ('lat', 'lon')), may hold values from -6 to 6
- source_cell: int32 [32, 4, 6144], P(('lat', 'lon')), may hold values from 0 to 8191, as said below
- link_weight: float32 [32, 4, 6144], P(('lat', 'lon')), may hold values from 0.05 to 0.3
- target_cell: int32 [32, 4, 6144], P(('lat', 'lon')), may hold values from 0 to 16383, as said below
Outputs:
- stepped: float32 [2, 48, 512, 1024], P(None, None, 'lat', 'lon')
The draws below stay inside these ranges and needn't reach their ends.
Inputs may be any that keep to these rules, and one draw needn't show every extreme that they name: source_cell[s, n, c] lies in n * 2048 to (n+1) * 2048 - 1; several links may name the same cells. target_cell[d, n, c] has its row in (1 - n // 2) * 64 to that plus 128 // 2 - 1 and its column in (1 - n % 2) * 64 to that plus 128 // 2 - 1.
All inputs are finite; a program needn't handle non-finite values. No bound on the sum of `land_sea` on one device may be relied on, other than what follows from the above.
Results may differ from the reference program's by a relative error of at most 0.00005.
Values sent between devices are 32-bit elements; how exact they have to be, the bound alone decides.
No kernel may reach another device: no remote copies, remote signals or barrier semaphores. Data moves between devices by JAX's collectives and lax.ppermute only.
A program may use at most 192 MiB of HBM per device.

```python
import math
import jax
import jax.numpy as jnp

FIELDS = 6
LEVELS = 48
CLAT = 128
CLON = 128
ATM_DEV = 8192
CAP = 6144
NLAT = 512
NLON = 1024
ATM_CELLS = 262144
N_LAT = 4
N_LON = 8
DEVICES = 32


def draw_source_cell(key, part):
    quarter = ATM_DEV // 4
    offset = jax.random.randint(key, (DEVICES, 4, CAP), 0, quarter, dtype=jnp.int32)
    base = (jnp.arange(4, dtype=jnp.int32) * quarter)[None, :, None]
    cells = offset + base
    cells = cells.at[:, 3, 0].set(ATM_DEV - 1)
    cells = cells.at[:, 0, 0].set(0)
    return cells


def draw_target_cell(key, part):
    half_rows = CLAT // 2
    half_cols = CLON // 2
    row_key = jax.random.fold_in(key, 11)
    col_key = jax.random.fold_in(key, 23)
    rows = jax.random.randint(row_key, (DEVICES, 4, CAP), 0, half_rows, dtype=jnp.int32)
    cols = jax.random.randint(col_key, (DEVICES, 4, CAP), 0, half_cols, dtype=jnp.int32)
    intersection = jnp.arange(4, dtype=jnp.int32)[None, :, None]
    rows = rows + (1 - intersection // 2) * half_rows
    cols = cols + (1 - intersection % 2) * half_cols
    cells = rows * CLON + cols
    cells = cells.at[:, 0, 0].set(CLAT * CLON - 1)
    cells = cells.at[:, 3, 0].set(0)
    return cells


def place_ends(array, own_key, least, largest):
    shape = array.shape
    index_at = [jax.random.randint(jax.random.fold_in(own_key, axis), (), 0, shape[axis]) for axis in range(len(shape))]
    array = array.at[tuple(index_at)].set(least)
    longest = shape.index(max(shape))
    index_at[longest] = (index_at[longest] + 1) % shape[longest]
    return array.at[tuple(index_at)].set(largest)


def steps_of(own_key, extent, shards, smallest, top_value):
    factor_of, own = 1.0, jax.random.fold_in(own_key, 6)
    for axis_at, blocks in shards:
        draws = jnp.exp(jax.random.uniform(jax.random.fold_in(own, axis_at), (blocks,), jnp.float32, smallest / len(shards), top_value / len(shards)))
        factor_of = factor_of * jnp.repeat(draws, extent[axis_at] // blocks).reshape([-1 if axis == axis_at else 1 for axis in range(len(extent))])
    return factor_of


def normal_values(key, extent, deviation, bound, cuts=(), held_as=jnp.bfloat16):
    drawn = jax.random.normal(key, extent, jnp.float32) * deviation
    if len(cuts) > 0:
        drawn = steps_of(key, extent, cuts, -0.22, 0.18) * drawn
    return jnp.clip(drawn, min=-bound, max=bound).astype(held_as)


def setup_inputs(seed: int = 0) -> dict:
    keys = jax.random.split(jax.random.key(seed), 10)
    return {
        "tracers": normal_values(keys[0], (2, LEVELS, NLAT, NLON), 1.0, 6.0, ((2, 4), (3, 8)), jnp.float32),
        "east_courant": jnp.clip(jax.random.uniform(keys[1], (LEVELS, NLAT, NLON), jnp.float32, -0.4, 0.4) * steps_of(keys[1], (LEVELS, NLAT, NLON), ((1, 4), (2, 8)), -0.4, 0.0), -0.4, 0.4),
        "north_courant": jnp.clip(jax.random.uniform(keys[2], (LEVELS, NLAT, NLON), jnp.float32, -0.4, 0.4) * steps_of(keys[2], (LEVELS, NLAT, NLON), ((1, 4), (2, 8)), -0.4, 0.0), -0.4, 0.4),
        "diffusivity": jnp.clip(jnp.exp(math.log(20.0) - 5.9914645 * jax.random.uniform(keys[3], (LEVELS, NLAT, NLON), jnp.float32) ** steps_of(keys[3], (LEVELS, NLAT, NLON), ((1, 4), (2, 8)), -0.2, 0.2)), 0.05, 20.0),
        "land_sea": place_ends((jax.random.randint(keys[4], (NLAT, NLON), 0, 4) < 3).astype(jnp.int32), jax.random.fold_in(keys[4], 1), 0, 1),
        "fluxes": normal_values(keys[5], (FIELDS, ATM_CELLS), 1.0, 6.0, ((1, 32),), jnp.float32),
        "source_cell": draw_source_cell(jax.random.fold_in(keys[9], 71), 0),
        "link_weight": jnp.clip(0.05 + 0.25 * jax.random.uniform(keys[7], (DEVICES, 4, CAP), jnp.float32) ** steps_of(keys[7], (DEVICES, 4, CAP), ((0, 32),), -0.2, 0.2), 0.05, 0.3),
        "target_cell": draw_target_cell(jax.random.fold_in(keys[9], 71), 0),
    }


def face(lower_two, lower_one, upper_one, upper_two):
    return (7.0 * (lower_one + upper_one) - (lower_two + upper_two)) / 12.0

def column_solve(right_side, mixing):
    levels = mixing.shape[0]
    above = jnp.zeros_like(mixing[0])
    prior_upper = jnp.zeros_like(mixing[0])
    prior_value = jnp.zeros_like(right_side[:, 0])
    uppers = []
    values = []
    for level in range(levels):
        below = mixing[level]
        pivot = 1.0 + above + below + above * prior_upper
        value = (right_side[:, level] + above * prior_value) / pivot
        prior_upper = -below / pivot
        prior_value = value
        uppers.append(prior_upper)
        values.append(value)
        above = below
    result = [None] * levels
    result[levels - 1] = values[levels - 1]
    for level in range(levels - 2, -1, -1):
        result[level] = values[level] - uppers[level] * result[level + 1]
    return jnp.stack(result, 1)

def forcing(advected, surface, diffusivity):
    levels = advected.shape[1]
    depth = jnp.arange(levels, dtype=jnp.float32)
    absorb = jnp.exp(-4.0 * depth / levels) - jnp.exp(-4.0 * (depth + 1.0) / levels)
    decay = jnp.exp(-4.0 * depth / levels)
    keep = (jnp.arange(levels) < levels - 1).astype(jnp.float32)
    heat_part = advected[0] + 0.5 * surface[2][None] * absorb[:, None, None]
    heat_part = heat_part.at[0].add(0.5 * surface[0])
    salt_part = advected[1].at[0].add(0.5 * (surface[1] + surface[5]))
    forced = jnp.stack([heat_part, salt_part], 0)
    stress = jnp.sqrt(surface[3] * surface[3] + surface[4] * surface[4])
    mixing = (diffusivity + 2.0 * stress[None] * decay[:, None, None]) * keep[:, None, None]
    return (forced, mixing)

def reference(tracers, east_courant, north_courant, diffusivity, land_sea, fluxes, source_cell, link_weight, target_cell):
    devices = N_LAT * N_LON
    owner = jnp.arange(devices, dtype=jnp.int32)[:, None]
    intersection = jnp.arange(4, dtype=jnp.int32)[None, :]
    lat_off = intersection // 2
    lon_off = intersection % 2
    owner_lat = owner // N_LON
    owner_lon = owner % N_LON
    sender_lat = owner_lat - lat_off
    exists = (sender_lat >= 0).astype(jnp.float32)
    sender = sender_lat % N_LAT * N_LON + (owner_lon - lon_off) % N_LON
    picked_cell = source_cell[sender, intersection]
    picked_weight = link_weight[sender, intersection] * exists[:, :, None]
    global_cell = (picked_cell + (sender * ATM_DEV)[:, :, None]).reshape(-1)
    values = jnp.take(fluxes, global_cell, axis=1) * picked_weight.reshape(-1)[None]
    row = (owner_lat * CLAT)[:, :, None] + target_cell // CLON
    col = (owner_lon * CLON)[:, :, None] + target_cell % CLON
    flat = (row * NLON + col).reshape(-1)
    surface = jnp.zeros((FIELDS, NLAT * NLON), jnp.float32).at[:, flat].add(values)
    surface = surface.reshape(FIELDS, NLAT, NLON)
    east_val = face(jnp.roll(tracers, 1, 3), tracers, jnp.roll(tracers, -1, 3), jnp.roll(tracers, -2, 3))
    east_flux = east_courant[None] * east_val
    west_flux = jnp.roll(east_flux, 1, 3)
    padded = jnp.pad(tracers, ((0, 0), (0, 0), (2, 2), (0, 0)))
    north_val = face(padded[:, :, 1:NLAT + 1], padded[:, :, 2:NLAT + 2], padded[:, :, 3:NLAT + 3], padded[:, :, 4:NLAT + 4])
    north_flux = north_courant[None] * north_val
    south_flux = jnp.concatenate([jnp.zeros_like(north_flux[:, :, :1]), north_flux[:, :, :-1]], 2)
    advected = tracers - (east_flux - west_flux) - (north_flux - south_flux)
    forced, mixing = forcing(advected, surface, diffusivity)
    solved = column_solve(forced, mixing)
    return jnp.where((land_sea == 1)[None, None], solved, tracers)
```

```python
import functools

import jax
import jax.numpy as jnp
from jax import lax
from jax.experimental import pallas as pl
from jax.experimental.pallas import tpu as pltpu
from jax.sharding import PartitionSpec as P

F32 = jnp.float32
BF16 = jnp.bfloat16
LANES = 128
SUB = 8
TABLE_ROWS = 16


def lane_of(shape):
    return lax.broadcasted_iota(jnp.int32, shape, len(shape) - 1)


def prep_kernel(
    links,
    tracers,
    east_courant,
    north_last,
    fluxes,
    source,
    weight,
    east_msg,
    west_msg,
    north_msg,
    south_msg,
    corner_msg,
    own_msg,
):
    step = pl.program_id(0)
    steps = pl.num_programs(0)
    levels = tracers.shape[1]
    block = tracers.shape[2]
    rows_all = steps * block
    lane = lane_of((SUB, LANES))
    pair = lane // 2
    half = levels // 2
    for rb in range(block // SUB):
        at = pl.ds(rb * SUB, SUB)
        for t in range(2):
            tail = jnp.zeros((SUB, LANES), F32)
            head = jnp.zeros((SUB, LANES), F32)
            for k in range(levels):
                moved = pltpu.roll(tracers[t, k, at, :], 2 * k + 2, 1)
                tail = jnp.where(pair == k, moved, tail)
                head = jnp.where(pair == k + 1, moved, head)
            for j in range(half):
                moved = pltpu.roll(east_courant[t * half + j, at, :], (2 * levels + j + 1) % LANES, 1)
                tail = jnp.where(lane == 2 * levels + j, moved, tail)
            start = pl.multiple_of(t * rows_all + step * block + rb * SUB, SUB)
            east_msg[pl.ds(start, SUB), :] = tail
            west_msg[pl.ds(start, SUB), :] = head

    @pl.when(step == 0)
    def _():
        quarter = fluxes.shape[1] // 4
        places = ((own_msg, 0), (east_msg, 2 * rows_all), (north_msg, 5 * levels), (corner_msg, 0))
        for n, (msg, base) in enumerate(places):
            for f in range(5):
                for u in range(TABLE_ROWS):
                    cut = pl.ds(n * quarter + u * LANES, LANES)
                    row = fluxes[f : f + 1, cut]
                    if f == 1:
                        row = row + fluxes[5:6, cut]
                    msg[pl.ds(base + f * TABLE_ROWS + u, 1), :] = row
            base = base + 5 * TABLE_ROWS
            for c in range(links // LANES):
                cut = pl.ds(c * LANES, LANES)
                msg[pl.ds(base + c, 1), :] = source[n : n + 1, cut].astype(F32)
                msg[pl.ds(base + links // LANES + c, 1), :] = weight[n : n + 1, cut]
        for t in range(2):
            for k in range(levels):
                south_msg[pl.ds(2 * (t * levels + k), 2), :] = tracers[t, k, 0:2, :]

    @pl.when(step == steps - 1)
    def _():
        for t in range(2):
            for k in range(levels):
                north_msg[pl.ds(2 * (t * levels + k), 2), :] = tracers[t, k, block - 2 : block, :]
        for k in range(levels):
            north_msg[pl.ds(4 * levels + k, 1), :] = north_last[k, SUB - 1 : SUB, :]


def prep(tracers, east_courant, north_courant, fluxes, source, weight):
    _, levels, rows, cols = tracers.shape
    links = source.shape[1]
    block = 16
    remap = 5 * TABLE_ROWS + 2 * (links // LANES)
    heights = (2 * rows + remap, 2 * rows, 5 * levels + remap, 4 * levels, remap, remap)
    whole = lambda shape: pl.BlockSpec(shape, lambda i: (0,) * len(shape))
    return pl.pallas_call(
        functools.partial(prep_kernel, links),
        grid=(rows // block,),
        in_specs=[
            pl.BlockSpec((2, levels, block, cols), lambda i: (0, 0, i, 0)),
            pl.BlockSpec((levels, block, cols), lambda i: (0, i, 0)),
            pl.BlockSpec((levels, SUB, cols), lambda i: (0, rows // SUB - 1, 0)),
            whole(fluxes.shape),
            whole(source.shape),
            whole(weight.shape),
        ],
        out_specs=[whole((h, LANES)) for h in heights],
        out_shape=[jax.ShapeDtypeStruct((h, LANES), F32) for h in heights],
        compiler_params=pltpu.CompilerParams(vmem_limit_bytes=32 << 20),
        name="prep",
    )(tracers, east_courant, north_courant, fluxes, source, weight)


def gather_links(msg, base, n, links, picked):
    rows = links // LANES
    for g in range(rows // SUB):
        cells = msg[pl.ds(base + 5 * TABLE_ROWS + g * SUB, SUB), :].astype(jnp.int32)
        weights = msg[pl.ds(base + 5 * TABLE_ROWS + rows + g * SUB, SUB), :]
        low = cells % LANES
        high = (cells // LANES) % TABLE_ROWS
        for f in range(5):
            total = jnp.zeros((SUB, LANES), F32)
            for u in range(TABLE_ROWS):
                row = jnp.broadcast_to(msg[pl.ds(base + f * TABLE_ROWS + u, 1), :], (SUB, LANES))
                found = jnp.take_along_axis(row, low, axis=1, mode="promise_in_bounds")
                total = jnp.where(high == u, found, total)
            picked[f, pl.ds(n * rows + g * SUB, SUB), :] = total * weights


def scatter_links(picked, target, n, links, rows, cols):
    half_rows = rows // 2
    half_cols = cols // 2
    count = links // LANES
    wide = 4 * half_cols
    short = half_rows // 4
    tall_iota = lax.broadcasted_iota(jnp.int32, (wide, LANES), 0)
    short_iota = lax.broadcasted_iota(jnp.int32, (short, LANES), 0)
    total = jnp.zeros((10 * short, wide), F32)
    group = 8
    for g in range(count // group):
        lefts = []
        rights = []
        for c in range(g * group, (g + 1) * group):
            cell = target[n : n + 1, c * LANES : (c + 1) * LANES]
            row = cell // cols - (1 - n // 2) * half_rows
            col = cell % cols - (1 - n % 2) * half_cols
            short_at = jnp.broadcast_to(row % short, (short, LANES)) == short_iota
            wide_at = jnp.broadcast_to(row // short * half_cols + col, (wide, LANES)) == tall_iota
            rights.append(jnp.where(wide_at, 1.0, 0.0).astype(BF16))
            pieces = []
            for f in range(5):
                value = picked[f, pl.ds(n * count + c, 1), :]
                high = value.astype(BF16).astype(F32)
                low = value - high
                for part in (high, low):
                    spread = jnp.broadcast_to(part, (short, LANES))
                    pieces.append(jnp.where(short_at, spread, 0.0).astype(BF16))
            lefts.append(jnp.concatenate(pieces, 0))
        left = jnp.concatenate(lefts, 1)
        right = jnp.concatenate(rights, 1)
        total = total + lax.dot_general(
            left, right, (((1,), (1,)), ((), ())), preferred_element_type=F32
        )
    return total


def main_kernel(
    links,
    chunk_rows,
    tables,
    tracers,
    east_courant,
    north_courant,
    diffusivity,
    land,
    target,
    own_tail,
    own_head,
    from_west,
    from_east,
    from_south,
    from_north,
    from_corner,
    own_remap,
    out,
    cells,
    east,
    north,
    diff,
    values,
    gains,
    flux,
    picked,
    surface,
    left_fix,
    right_fix,
    in_sem,
    out_sem,
):
    _, levels, rows, cols = tracers.shape
    chunks = rows // chunk_rows
    lane = lane_of((SUB, LANES))

    def loads(c):
        part = pl.ds(c * chunk_rows, chunk_rows)
        return [
            pltpu.make_async_copy(
                tracers.at[:, :, part, :],
                cells.at[:, :, pl.ds(SUB + c * chunk_rows, chunk_rows), :],
                in_sem.at[0, c],
            ),
            pltpu.make_async_copy(
                east_courant.at[:, part, :], east.at[:, part, :], in_sem.at[1, c]
            ),
            pltpu.make_async_copy(
                north_courant.at[:, part, :], north.at[:, part, :], in_sem.at[2, c]
            ),
            pltpu.make_async_copy(
                diffusivity.at[:, part, :], diff.at[:, part, :], in_sem.at[3, c]
            ),
        ]

    def store(c):
        part = pl.ds(c * chunk_rows, chunk_rows)
        return pltpu.make_async_copy(
            values.at[:, :, part, :], out.at[:, :, part, :], out_sem.at[c]
        )

    copies = [loads(c) for c in range(chunks)]
    for group in copies:
        for copy in group:
            copy.start()

    places = (
        (own_remap, 0),
        (from_west, 2 * rows),
        (from_south, 5 * levels),
        (from_corner, 0),
    )
    quads = []
    for n, (msg, base) in enumerate(places):
        gather_links(msg, base, n, links, picked)
        quads.append(scatter_links(picked, target, n, links, rows, cols))
    short = rows // 8
    for pair in range(2):
        left = quads[2 * pair + 1]
        right = quads[2 * pair]
        for f in range(5):
            at = 2 * f * short
            one = left[at : at + short] + left[at + short : at + 2 * short]
            two = right[at : at + short] + right[at + short : at + 2 * short]
            for g in range(4):
                half = slice(g // 2 * LANES, g // 2 * LANES + LANES)
                a = one[:, half]
                b = two[:, half]
                if g % 2:
                    a = pltpu.roll(a, LANES // 2, 1)
                else:
                    b = pltpu.roll(b, LANES // 2, 1)
                merged = jnp.where(lane_of((short, LANES)) < LANES // 2, a, b)
                base = (1 - pair) * (rows // 2) + g * short
                surface[f, base : base + short, :] = merged
    for rb in range(rows // SUB):
        at = pl.ds(rb * SUB, SUB)
        s3 = surface[3, at, :]
        s4 = surface[4, at, :]
        surface[3, at, :] = 2.0 * jnp.sqrt(s3 * s3 + s4 * s4)

    even = lane % 2 == 0
    half = levels // 2
    spread = 2 * levels + (lane // 2) % half
    lower = lane // 2 < half
    for rb in range(rows // SUB):
        at = pl.ds(rb * SUB, SUB)
        next_at = pl.ds(rows + rb * SUB, SUB)
        first = jnp.take_along_axis(from_west[at, :], spread, axis=1, mode="promise_in_bounds")
        second = jnp.take_along_axis(from_west[next_at, :], spread, axis=1, mode="promise_in_bounds")
        courant = jnp.where(lower, first, second)
        for t in range(2):
            place = pl.ds(t * rows + rb * SUB, SUB)
            head = own_head[place, :]
            gap = from_east[place, :] - head
            right_fix[t, at, :] = jnp.where(even, -gap, 7.0 * pltpu.roll(gap, 1, 1) - gap)
            west = from_west[place, :]
            west_face = 7.0 * (pltpu.roll(west, LANES - 1, 1) + pltpu.roll(head, LANES - 2, 1)) - (
                west + pltpu.roll(head, LANES - 3, 1)
            )
            left_fix[t, at, :] = jnp.where(even, courant * west_face, own_tail[place, :] - west)

    def halo_rows(k, carry):
        for t in range(2):
            unit = t * levels + k
            below = from_south[pl.ds(2 * unit, 2), :]
            cells[t, k, SUB - 2 : SUB, :] = below
            cells[t, k, SUB + rows : SUB + rows + 2, :] = from_north[pl.ds(2 * unit, 2), :]
            low_two = below[0:1]
            low_one = below[1:2]
            up_one = cells[t, k, SUB : SUB + 1, :]
            up_two = cells[t, k, SUB + 1 : SUB + 2, :]
            courant = from_south[pl.ds(4 * levels + k, 1), :]
            flux[t, k, SUB - 1 : SUB, :] = courant * (7.0 * (low_one + up_one) - (low_two + up_two))
        return carry

    for copy in copies[0]:
        copy.wait()
    lax.fori_loop(0, levels, halo_rows, 0)

    at_right = lane >= LANES - 2
    at_left = lane == 0
    at_last = lane == LANES - 1
    blocks = chunk_rows // SUB

    def advect(t, k, r0):
        here = cells[t, k, SUB + r0 : 2 * SUB + r0, :]
        up_one = pltpu.roll(here, LANES - 1, 1)
        up_two = pltpu.roll(here, LANES - 2, 1)
        low_one = pltpu.roll(here, 1, 1)
        fix_right = pltpu.roll(right_fix[t, r0 : r0 + SUB, :], (2 * LANES - 4 - 2 * k) % LANES, 1)
        fix_left = pltpu.roll(left_fix[t, r0 : r0 + SUB, :], (LANES - 1 - 2 * k) % LANES, 1)
        face = 7.0 * (here + up_one) - (low_one + up_two)
        face = face + jnp.where(at_right, fix_right, jnp.where(at_left, fix_left, 0.0))
        east_flux = east[k, r0 : r0 + SUB, :] * face
        west_flux = pltpu.roll(jnp.where(at_last, fix_left, east_flux), 1, 1)
        low_one = cells[t, k, SUB + r0 - 1 : 2 * SUB + r0 - 1, :]
        up_one = cells[t, k, SUB + r0 + 1 : 2 * SUB + r0 + 1, :]
        up_two = cells[t, k, SUB + r0 + 2 : 2 * SUB + r0 + 2, :]
        face = 7.0 * (here + up_one) - (low_one + up_two)
        north_flux = north[k, r0 : r0 + SUB, :] * face
        flux[t, k, SUB + r0 : 2 * SUB + r0, :] = north_flux
        south_flux = flux[t, k, SUB + r0 - 1 : 2 * SUB + r0 - 1, :]
        change = (east_flux - west_flux) + (north_flux - south_flux)
        return here - change * (1.0 / 12.0)

    for c in range(chunks):
        if c + 1 < chunks:
            for copy in copies[c + 1]:
                copy.wait()
        base = c * chunk_rows

        def forward(k, carry, last=False):
            new = []
            for i in range(blocks):
                r0 = base + i * SUB
                above, lead, heat, salt = carry[4 * i : 4 * i + 4]
                heat_in = advect(0, k, r0) + surface[2, r0 : r0 + SUB, :] * tables[0, k]
                salt_in = advect(1, k, r0)
                if last:
                    inverse = 1.0 / lead
                    below = above
                else:
                    below = diff[k, r0 : r0 + SUB, :] + surface[3, r0 : r0 + SUB, :] * tables[1, k]
                    pivot = lead + below
                    rough = pl.reciprocal(pivot, approx=True)
                    inverse = rough * (2.0 - pivot * rough)
                heat = (heat_in + above * heat) * inverse
                salt = (salt_in + above * salt) * inverse
                values[0, k, r0 : r0 + SUB, :] = heat
                values[1, k, r0 : r0 + SUB, :] = salt
                if not last:
                    gains[k, i * SUB : (i + 1) * SUB, :] = below * inverse
                    lead = 1.0 + below * (lead * inverse)
                new += [below, lead, heat, salt]
            return tuple(new)

        carry = []
        for i in range(blocks):
            r0 = base + i * SUB
            one = jnp.ones((SUB, LANES), F32)
            carry += [one, one, 0.5 * surface[0, r0 : r0 + SUB, :], 0.5 * surface[1, r0 : r0 + SUB, :]]
        carry = lax.fori_loop(0, levels - 1, forward, tuple(carry))
        carry = forward(levels - 1, carry, True)

        def finish(k, i, heat, salt):
            r0 = base + i * SUB
            wet = land[r0 : r0 + SUB, :] == 1
            values[0, k, r0 : r0 + SUB, :] = jnp.where(wet, heat, cells[0, k, SUB + r0 : 2 * SUB + r0, :])
            values[1, k, r0 : r0 + SUB, :] = jnp.where(wet, salt, cells[1, k, SUB + r0 : 2 * SUB + r0, :])

        def backward(step, carry):
            k = levels - 2 - step
            new = []
            for i in range(blocks):
                r0 = base + i * SUB
                heat, salt = carry[2 * i : 2 * i + 2]
                gain = gains[k, i * SUB : (i + 1) * SUB, :]
                heat = values[0, k, r0 : r0 + SUB, :] + gain * heat
                salt = values[1, k, r0 : r0 + SUB, :] + gain * salt
                finish(k, i, heat, salt)
                new += [heat, salt]
            return tuple(new)

        ends = []
        for i in range(blocks):
            heat, salt = carry[4 * i + 2 : 4 * i + 4]
            finish(levels - 1, i, heat, salt)
            ends += [heat, salt]
        lax.fori_loop(0, levels - 1, backward, tuple(ends))
        store(c).start()
    for c in range(chunks):
        store(c).wait()


def step_blocks(
    tracers, east_courant, north_courant, diffusivity, land, target, messages, chunk_rows=32
):
    _, levels, rows, cols = tracers.shape
    links = target.shape[1]
    depth = jnp.arange(levels, dtype=F32)
    decay = jnp.exp(-4.0 * depth / levels)
    absorb = decay - jnp.exp(-4.0 * (depth + 1.0) / levels)
    tables = jnp.stack([0.5 * absorb, decay])
    chunks = rows // chunk_rows
    hbm = pl.BlockSpec(memory_space=pl.ANY)
    vmem = pl.BlockSpec(memory_space=pltpu.VMEM)
    own_tail, own_head = messages[0], messages[1]
    return pl.pallas_call(
        functools.partial(main_kernel, links, chunk_rows),
        in_specs=[pl.BlockSpec(memory_space=pltpu.SMEM)] + [hbm] * 4 + [vmem] * 10,
        out_specs=hbm,
        out_shape=jax.ShapeDtypeStruct(tracers.shape, F32),
        scratch_shapes=[
            pltpu.VMEM((2, levels, rows + 2 * SUB, cols), F32),
            pltpu.VMEM((levels, rows, cols), F32),
            pltpu.VMEM((levels, rows, cols), F32),
            pltpu.VMEM((levels, rows, cols), F32),
            pltpu.VMEM((2, levels, rows, cols), F32),
            pltpu.VMEM((levels, chunk_rows, cols), F32),
            pltpu.VMEM((2, levels, rows + SUB, cols), F32),
            pltpu.VMEM((5, 4 * links // LANES, LANES), F32),
            pltpu.VMEM((5, rows, cols), F32),
            pltpu.VMEM((2, rows, cols), F32),
            pltpu.VMEM((2, rows, cols), F32),
            pltpu.SemaphoreType.DMA((4, chunks)),
            pltpu.SemaphoreType.DMA((chunks,)),
        ],
        compiler_params=pltpu.CompilerParams(vmem_limit_bytes=56 << 20),
        name="step",
    )(tables, tracers, east_courant, north_courant, diffusivity, land, target, *messages)


def ring(axis, by):
    length = lax.axis_size(axis)
    return [(i, (i + by) % length) for i in range(length)]


def line(axis, by):
    length = lax.axis_size(axis)
    return [(i, i + by) for i in range(length) if 0 <= i + by < length]


def diagonal():
    lats = lax.axis_size("lat")
    lons = lax.axis_size("lon")
    return [
        (i * lons + j, (i + 1) * lons + (j + 1) % lons) for i in range(lats - 1) for j in range(lons)
    ]


def local(
    tracers,
    east_courant,
    north_courant,
    diffusivity,
    land_sea,
    fluxes,
    source_cell,
    link_weight,
    target_cell,
):
    east, west, north, south, corner, own = prep(
        tracers, east_courant, north_courant, fluxes, source_cell[0], link_weight[0]
    )
    from_corner = lax.ppermute(corner, ("lat", "lon"), diagonal())
    from_west = lax.ppermute(east, "lon", ring("lon", 1))
    from_east = lax.ppermute(west, "lon", ring("lon", -1))
    from_south = lax.ppermute(north, "lat", line("lat", 1))
    from_north = lax.ppermute(south, "lat", line("lat", -1))
    messages = (east, west, from_west, from_east, from_south, from_north, from_corner, own)
    return step_blocks(
        tracers, east_courant, north_courant, diffusivity, land_sea, target_cell[0], messages
    )


def solution(mesh):
    in_specs = (
        P(None, None, "lat", "lon"),
        P(None, "lat", "lon"),
        P(None, "lat", "lon"),
        P(None, "lat", "lon"),
        P("lat", "lon"),
        P(None, ("lat", "lon")),
        P(("lat", "lon"), None, None),
        P(("lat", "lon"), None, None),
        P(("lat", "lon"), None, None),
    )
    out_specs = P(None, None, "lat", "lon")
    return jax.shard_map(local, mesh=mesh, in_specs=in_specs, out_specs=out_specs, check_vma=False)
```

```python
import functools

import jax
import jax.numpy as jnp
from jax import lax
from jax.experimental import pallas as pl
from jax.experimental.pallas import tpu as pltpu
from jax.sharding import PartitionSpec as P

F32 = jnp.float32
BF16 = jnp.bfloat16
LANES = 128
SUB = 8
TABLE_ROWS = 16
EDGE_VMEM = 60 << 20
COLUMN_VMEM = 8 << 20
STEP_VMEM = 24 << 20


def lane_of(shape):
    return lax.broadcasted_iota(jnp.int32, shape, len(shape) - 1)


def edge_kernel(
    links,
    tracers,
    north_courant,
    fluxes,
    source,
    weight,
    east_links,
    north_msg,
    south_msg,
    corner_msg,
    own_msg,
    first_rows,
    last_rows,
    last_north,
    flux_in,
    source_in,
    weight_in,
    sem,
):
    _, levels, rows, _ = tracers.shape
    copies = [
        pltpu.make_async_copy(fluxes, flux_in, sem.at[0]),
        pltpu.make_async_copy(source, source_in, sem.at[1]),
        pltpu.make_async_copy(weight, weight_in, sem.at[2]),
        pltpu.make_async_copy(tracers.at[:, :, pl.ds(0, SUB), :], first_rows, sem.at[3]),
        pltpu.make_async_copy(tracers.at[:, :, pl.ds(rows - SUB, SUB), :], last_rows, sem.at[4]),
        pltpu.make_async_copy(north_courant.at[:, pl.ds(rows - SUB, SUB), :], last_north, sem.at[5]),
    ]
    for copy in copies:
        copy.start()
    for copy in copies[:3]:
        copy.wait()
    quarter = fluxes.shape[1] // 4
    places = ((own_msg, 0), (east_links, 0), (north_msg, 5 * levels), (corner_msg, 0))
    for n, (msg, base) in enumerate(places):
        for f in range(5):
            for u in range(TABLE_ROWS):
                cut = pl.ds(n * quarter + u * LANES, LANES)
                row = flux_in[f : f + 1, cut]
                if f == 1:
                    row = row + flux_in[5:6, cut]
                msg[pl.ds(base + f * TABLE_ROWS + u, 1), :] = row
        base = base + 5 * TABLE_ROWS
        for c in range(links // LANES):
            cut = pl.ds(c * LANES, LANES)
            msg[pl.ds(base + c, 1), :] = source_in[n : n + 1, cut].astype(F32)
            msg[pl.ds(base + links // LANES + c, 1), :] = weight_in[n : n + 1, cut]
    for copy in copies[3:]:
        copy.wait()
    for t in range(2):
        for k in range(levels):
            at = pl.ds(2 * (t * levels + k), 2)
            south_msg[at, :] = first_rows[t, k, 0:2, :]
            north_msg[at, :] = last_rows[t, k, SUB - 2 : SUB, :]
    for k in range(levels):
        north_msg[pl.ds(4 * levels + k, 1), :] = last_north[k, SUB - 1 : SUB, :]


def edges(tracers, north_courant, fluxes, source, weight):
    _, levels, _, cols = tracers.shape
    links = source.shape[1]
    remap = remap_rows(links)
    heights = (remap, 5 * levels + remap, 4 * levels, remap, remap)
    hbm = pl.BlockSpec(memory_space=pl.ANY)
    vmem = pl.BlockSpec(memory_space=pltpu.VMEM)
    return pl.pallas_call(
        functools.partial(edge_kernel, links),
        in_specs=[hbm] * 5,
        out_specs=[vmem] * 5,
        out_shape=[jax.ShapeDtypeStruct((h, LANES), F32) for h in heights],
        scratch_shapes=[
            pltpu.VMEM((2, levels, SUB, cols), F32),
            pltpu.VMEM((2, levels, SUB, cols), F32),
            pltpu.VMEM((levels, SUB, cols), F32),
            pltpu.VMEM(fluxes.shape, F32),
            pltpu.VMEM(source.shape, jnp.int32),
            pltpu.VMEM(weight.shape, F32),
            pltpu.SemaphoreType.DMA((6,)),
        ],
        compiler_params=pltpu.CompilerParams(vmem_limit_bytes=EDGE_VMEM),
        name="edges",
    )(tracers, north_courant, fluxes, source, weight)


def column_kernel(tracers, east_courant, east_links, east_msg, west_msg):
    _, levels, rows, _ = tracers.shape
    lane = lane_of((SUB, LANES))
    pair = lane // 2
    half = levels // 2

    def block(rb, carry):
        at = pl.ds(pl.multiple_of(rb * SUB, SUB), SUB)
        for t in range(2):
            tail = jnp.zeros((SUB, LANES), F32)
            head = jnp.zeros((SUB, LANES), F32)
            for k in range(levels):
                moved = pltpu.roll(tracers[t, k, at, :], 2 * k + 2, 1)
                tail = jnp.where(pair == k, moved, tail)
                head = jnp.where(pair == k + 1, moved, head)
            for j in range(half):
                moved = pltpu.roll(east_courant[t * half + j, at, :], (2 * levels + j + 1) % LANES, 1)
                tail = jnp.where(lane == 2 * levels + j, moved, tail)
            place = pl.ds(pl.multiple_of(t * rows + rb * SUB, SUB), SUB)
            east_msg[place, :] = tail
            west_msg[place, :] = head
        return carry

    lax.fori_loop(0, rows // SUB, block, 0)
    east_msg[2 * rows :, :] = east_links[...]


def columns(tracers, east_courant, east_links):
    rows = tracers.shape[2]
    vmem = pl.BlockSpec(memory_space=pltpu.VMEM)
    return pl.pallas_call(
        column_kernel,
        in_specs=[vmem] * 3,
        out_specs=[vmem] * 2,
        out_shape=[
            jax.ShapeDtypeStruct((2 * rows + east_links.shape[0], LANES), F32),
            jax.ShapeDtypeStruct((2 * rows, LANES), F32),
        ],
        compiler_params=pltpu.CompilerParams(vmem_limit_bytes=COLUMN_VMEM),
        name="columns",
    )(tracers, east_courant, east_links)


def remap_rows(links):
    return 5 * TABLE_ROWS + 2 * (links // LANES)


def gather_links(msg, base, n, links, picked):
    rows = links // LANES
    for g in range(rows // SUB):
        cells = msg[pl.ds(base + 5 * TABLE_ROWS + g * SUB, SUB), :].astype(jnp.int32)
        weights = msg[pl.ds(base + 5 * TABLE_ROWS + rows + g * SUB, SUB), :]
        low = cells % LANES
        high = (cells // LANES) % TABLE_ROWS
        for f in range(5):
            total = jnp.zeros((SUB, LANES), F32)
            for u in range(TABLE_ROWS):
                row = jnp.broadcast_to(msg[pl.ds(base + f * TABLE_ROWS + u, 1), :], (SUB, LANES))
                found = jnp.take_along_axis(row, low, axis=1, mode="promise_in_bounds")
                total = jnp.where(high == u, found, total)
            picked[f, pl.ds(n * rows + g * SUB, SUB), :] = total * weights


def scatter_links(picked, target, n, links, rows, cols):
    half_rows = rows // 2
    half_cols = cols // 2
    count = links // LANES
    wide = 4 * half_cols
    short = half_rows // 4
    tall_iota = lax.broadcasted_iota(jnp.int32, (wide, LANES), 0)
    short_iota = lax.broadcasted_iota(jnp.int32, (short, LANES), 0)
    total = jnp.zeros((10 * short, wide), F32)
    group = 8
    for g in range(count // group):
        lefts = []
        rights = []
        for c in range(g * group, (g + 1) * group):
            cell = target[n : n + 1, c * LANES : (c + 1) * LANES]
            row = cell // cols - (1 - n // 2) * half_rows
            col = cell % cols - (1 - n % 2) * half_cols
            short_at = jnp.broadcast_to(row % short, (short, LANES)) == short_iota
            wide_at = jnp.broadcast_to(row // short * half_cols + col, (wide, LANES)) == tall_iota
            rights.append(jnp.where(wide_at, 1.0, 0.0).astype(BF16))
            pieces = []
            for f in range(5):
                value = picked[f, pl.ds(n * count + c, 1), :]
                high = value.astype(BF16).astype(F32)
                low = value - high
                for part in (high, low):
                    spread = jnp.broadcast_to(part, (short, LANES))
                    pieces.append(jnp.where(short_at, spread, 0.0).astype(BF16))
            lefts.append(jnp.concatenate(pieces, 0))
        left = jnp.concatenate(lefts, 1)
        right = jnp.concatenate(rights, 1)
        total = total + lax.dot_general(
            left, right, (((1,), (1,)), ((), ())), preferred_element_type=F32
        )
    return total


def remap_kernel(links, rows, cols, numbers, bases, target, *refs):
    count = len(numbers)
    quads = refs[count]
    picked = refs[count + 1]
    for i, (n, base) in enumerate(zip(numbers, bases)):
        gather_links(refs[i], base, n, links, picked)
        quads[i] = scatter_links(picked, target, n, links, rows, cols)


def remap(target, blocks, rows, cols):
    links = target.shape[1]
    numbers = tuple(n for n, _, _ in blocks)
    bases = tuple(base for _, _, base in blocks)
    vmem = pl.BlockSpec(memory_space=pltpu.VMEM)
    return pl.pallas_call(
        functools.partial(remap_kernel, links, rows, cols, numbers, bases),
        in_specs=[vmem] * (1 + len(blocks)),
        out_specs=vmem,
        out_shape=jax.ShapeDtypeStruct((len(blocks), 10 * rows // 8, 2 * cols), F32),
        scratch_shapes=[pltpu.VMEM((5, 4 * links // LANES, LANES), F32)],
        compiler_params=pltpu.CompilerParams(vmem_limit_bytes=16 << 20),
        name="remap",
    )(target, *[msg for _, msg, _ in blocks])


def main_kernel(
    links,
    chunk_rows,
    tables,
    tracers,
    east,
    north,
    diff,
    land,
    target,
    own_tail,
    own_head,
    from_west,
    from_east,
    from_south,
    from_north,
    earlier,
    out,
    values,
    gains,
    before,
    picked,
    surface,
    left_fix,
    right_fix,
    out_sem,
):
    _, levels, rows, cols = tracers.shape
    chunks = rows // chunk_rows
    lane = lane_of((SUB, LANES))
    sub = lax.broadcasted_iota(jnp.int32, (SUB, LANES), 0)

    def store(c):
        part = pl.ds(c * chunk_rows, chunk_rows)
        return pltpu.make_async_copy(
            values.at[:, :, part, :], out.at[:, :, part, :], out_sem.at[c]
        )

    gather_links(from_west, 2 * rows, 1, links, picked)
    eastern = scatter_links(picked, target, 1, links, rows, cols)
    quads = [earlier[0], eastern, earlier[1], earlier[2]]
    short = rows // 8
    for pair in range(2):
        left = quads[2 * pair + 1]
        right = quads[2 * pair]
        for f in range(5):
            at = 2 * f * short
            one = left[at : at + short] + left[at + short : at + 2 * short]
            two = right[at : at + short] + right[at + short : at + 2 * short]
            for g in range(4):
                half = slice(g // 2 * LANES, g // 2 * LANES + LANES)
                a = one[:, half]
                b = two[:, half]
                if g % 2:
                    a = pltpu.roll(a, LANES // 2, 1)
                else:
                    b = pltpu.roll(b, LANES // 2, 1)
                merged = jnp.where(lane_of((short, LANES)) < LANES // 2, a, b)
                base = (1 - pair) * (rows // 2) + g * short
                surface[f, base : base + short, :] = merged
    for rb in range(rows // SUB):
        at = pl.ds(rb * SUB, SUB)
        s3 = surface[3, at, :]
        s4 = surface[4, at, :]
        surface[3, at, :] = 2.0 * jnp.sqrt(s3 * s3 + s4 * s4)

    even = lane % 2 == 0
    half = levels // 2
    spread = 2 * levels + (lane // 2) % half
    lower = lane // 2 < half
    for rb in range(rows // SUB):
        at = pl.ds(rb * SUB, SUB)
        next_at = pl.ds(rows + rb * SUB, SUB)
        first = jnp.take_along_axis(from_west[at, :], spread, axis=1, mode="promise_in_bounds")
        second = jnp.take_along_axis(from_west[next_at, :], spread, axis=1, mode="promise_in_bounds")
        courant = jnp.where(lower, first, second)
        for t in range(2):
            place = pl.ds(t * rows + rb * SUB, SUB)
            head = own_head[place, :]
            gap = from_east[place, :] - head
            right_fix[t, at, :] = jnp.where(even, -gap, 7.0 * pltpu.roll(gap, 1, 1) - gap)
            west = from_west[place, :]
            west_face = 7.0 * (pltpu.roll(west, LANES - 1, 1) + pltpu.roll(head, LANES - 2, 1)) - (
                west + pltpu.roll(head, LANES - 3, 1)
            )
            left_fix[t, at, :] = jnp.where(even, courant * west_face, own_tail[place, :] - west)

    def south_face(k, carry):
        for t in range(2):
            unit = t * levels + k
            below = from_south[pl.ds(2 * unit, 2), :]
            inside = tracers[t, k, 0:2, :]
            courant = from_south[pl.ds(4 * levels + k, 1), :]
            face = 7.0 * (below[1:2] + inside[0:1]) - (below[0:1] + inside[1:2])
            before[t, k, 0:1, :] = courant * face
        return carry

    lax.fori_loop(0, levels, south_face, 0)

    at_right = lane >= LANES - 2
    at_left = lane == 0
    at_last = lane == LANES - 1
    blocks = chunk_rows // SUB

    def halo_row(msg, index):
        return jnp.broadcast_to(msg[pl.ds(index, 1), :], (SUB, LANES))

    def advect(t, k, base):
        unit = t * levels + k
        south = before[t, k]
        result = []
        for i in range(blocks):
            r0 = base + i * SUB
            here = tracers[t, k, r0 : r0 + SUB, :]
            up_one = pltpu.roll(here, LANES - 1, 1)
            up_two = pltpu.roll(here, LANES - 2, 1)
            low_one = pltpu.roll(here, 1, 1)
            fix_right = pltpu.roll(right_fix[t, r0 : r0 + SUB, :], (2 * LANES - 4 - 2 * k) % LANES, 1)
            fix_left = pltpu.roll(left_fix[t, r0 : r0 + SUB, :], (LANES - 1 - 2 * k) % LANES, 1)
            face = 7.0 * (here + up_one) - (low_one + up_two)
            face = face + jnp.where(at_right, fix_right, jnp.where(at_left, fix_left, 0.0))
            east_flux = east[k, r0 : r0 + SUB, :] * face
            west_flux = pltpu.roll(jnp.where(at_last, fix_left, east_flux), 1, 1)
            if r0 == 0:
                low_one = jnp.where(sub == 0, halo_row(from_south, 2 * unit + 1), pltpu.roll(here, 1, 0))
            else:
                low_one = tracers[t, k, r0 - 1 : r0 - 1 + SUB, :]
            if r0 + SUB == rows:
                near = halo_row(from_north, 2 * unit)
                far = halo_row(from_north, 2 * unit + 1)
                up_one = jnp.where(sub == SUB - 1, near, pltpu.roll(here, SUB - 1, 0))
                up_two = jnp.where(
                    sub == SUB - 1, far, jnp.where(sub == SUB - 2, near, pltpu.roll(here, SUB - 2, 0))
                )
            else:
                up_one = tracers[t, k, r0 + 1 : r0 + 1 + SUB, :]
                up_two = tracers[t, k, r0 + 2 : r0 + 2 + SUB, :]
            face = 7.0 * (here + up_one) - (low_one + up_two)
            north_flux = north[k, r0 : r0 + SUB, :] * face
            moved = pltpu.roll(north_flux, 1, 0)
            south_flux = jnp.where(sub == 0, south, moved)
            south = moved
            change = (east_flux - west_flux) + (north_flux - south_flux)
            result.append(here - change * (1.0 / 12.0))
        before[t, k] = south
        return result

    for c in range(chunks):
        base = c * chunk_rows

        def forward(k, carry, last=False):
            new = []
            heat_all = advect(0, k, base)
            salt_all = advect(1, k, base)
            for i in range(blocks):
                r0 = base + i * SUB
                above, lead, heat, salt = carry[4 * i : 4 * i + 4]
                heat_in = heat_all[i] + surface[2, r0 : r0 + SUB, :] * tables[0, k]
                salt_in = salt_all[i]
                if last:
                    inverse = 1.0 / lead
                    below = above
                else:
                    below = diff[k, r0 : r0 + SUB, :] + surface[3, r0 : r0 + SUB, :] * tables[1, k]
                    pivot = lead + below
                    rough = pl.reciprocal(pivot, approx=True)
                    inverse = rough * (2.0 - pivot * rough)
                heat = (heat_in + above * heat) * inverse
                salt = (salt_in + above * salt) * inverse
                values[0, k, r0 : r0 + SUB, :] = heat
                values[1, k, r0 : r0 + SUB, :] = salt
                if not last:
                    gains[k, i * SUB : (i + 1) * SUB, :] = below * inverse
                    lead = 1.0 + below * (lead * inverse)
                new += [below, lead, heat, salt]
            return tuple(new)

        carry = []
        for i in range(blocks):
            r0 = base + i * SUB
            one = jnp.ones((SUB, LANES), F32)
            carry += [one, one, 0.5 * surface[0, r0 : r0 + SUB, :], 0.5 * surface[1, r0 : r0 + SUB, :]]
        carry = lax.fori_loop(0, levels - 1, forward, tuple(carry))
        carry = forward(levels - 1, carry, True)

        def finish(k, i, heat, salt):
            r0 = base + i * SUB
            wet = land[r0 : r0 + SUB, :] == 1
            values[0, k, r0 : r0 + SUB, :] = jnp.where(wet, heat, tracers[0, k, r0 : r0 + SUB, :])
            values[1, k, r0 : r0 + SUB, :] = jnp.where(wet, salt, tracers[1, k, r0 : r0 + SUB, :])

        def backward(step, carry):
            k = levels - 2 - step
            new = []
            for i in range(blocks):
                r0 = base + i * SUB
                heat, salt = carry[2 * i : 2 * i + 2]
                gain = gains[k, i * SUB : (i + 1) * SUB, :]
                heat = values[0, k, r0 : r0 + SUB, :] + gain * heat
                salt = values[1, k, r0 : r0 + SUB, :] + gain * salt
                finish(k, i, heat, salt)
                new += [heat, salt]
            return tuple(new)

        ends = []
        for i in range(blocks):
            heat, salt = carry[4 * i + 2 : 4 * i + 4]
            finish(levels - 1, i, heat, salt)
            ends += [heat, salt]
        lax.fori_loop(0, levels - 1, backward, tuple(ends))
        store(c).start()
    for c in range(chunks):
        store(c).wait()


def step_blocks(
    tracers, east_courant, north_courant, diffusivity, land, target, messages, chunk_rows=64
):
    _, levels, rows, cols = tracers.shape
    links = target.shape[1]
    depth = jnp.arange(levels, dtype=F32)
    decay = jnp.exp(-4.0 * depth / levels)
    absorb = decay - jnp.exp(-4.0 * (depth + 1.0) / levels)
    tables = jnp.stack([0.5 * absorb, decay])
    chunks = rows // chunk_rows
    hbm = pl.BlockSpec(memory_space=pl.ANY)
    vmem = pl.BlockSpec(memory_space=pltpu.VMEM)
    return pl.pallas_call(
        functools.partial(main_kernel, links, chunk_rows),
        in_specs=[pl.BlockSpec(memory_space=pltpu.SMEM)] + [vmem] * (6 + len(messages)),
        out_specs=hbm,
        out_shape=jax.ShapeDtypeStruct(tracers.shape, F32),
        scratch_shapes=[
            pltpu.VMEM((2, levels, rows, cols), F32),
            pltpu.VMEM((levels, chunk_rows, cols), F32),
            pltpu.VMEM((2, levels, SUB, cols), F32),
            pltpu.VMEM((5, 4 * links // LANES, LANES), F32),
            pltpu.VMEM((5, rows, cols), F32),
            pltpu.VMEM((2, rows, cols), F32),
            pltpu.VMEM((2, rows, cols), F32),
            pltpu.SemaphoreType.DMA((chunks,)),
        ],
        compiler_params=pltpu.CompilerParams(vmem_limit_bytes=STEP_VMEM),
        name="step",
    )(tables, tracers, east_courant, north_courant, diffusivity, land, target, *messages)


def ring(axis, by):
    length = lax.axis_size(axis)
    return [(i, (i + by) % length) for i in range(length)]


def line(axis, by):
    length = lax.axis_size(axis)
    return [(i, i + by) for i in range(length) if 0 <= i + by < length]


def diagonal():
    lats = lax.axis_size("lat")
    lons = lax.axis_size("lon")
    return [
        (i * lons + j, (i + 1) * lons + (j + 1) % lons) for i in range(lats - 1) for j in range(lons)
    ]


def local(
    tracers,
    east_courant,
    north_courant,
    diffusivity,
    land_sea,
    fluxes,
    source_cell,
    link_weight,
    target_cell,
):
    _, levels, rows, cols = tracers.shape
    target = target_cell[0]
    east_links, north, south, corner, own = edges(
        tracers, north_courant, fluxes, source_cell[0], link_weight[0]
    )
    from_corner = lax.ppermute(corner, ("lat", "lon"), diagonal())
    from_south = lax.ppermute(north, "lat", line("lat", 1))
    from_north = lax.ppermute(south, "lat", line("lat", -1))
    east, west = columns(tracers, east_courant, east_links)
    from_west = lax.ppermute(east, "lon", ring("lon", 1))
    from_east = lax.ppermute(west, "lon", ring("lon", -1))
    earlier = remap(
        target, [(0, own, 0), (2, from_south, 5 * levels), (3, from_corner, 0)], rows, cols
    )
    messages = (east, west, from_west, from_east, from_south, from_north, earlier)
    return step_blocks(
        tracers, east_courant, north_courant, diffusivity, land_sea, target, messages
    )


def solution(mesh):
    in_specs = (
        P(None, None, "lat", "lon"),
        P(None, "lat", "lon"),
        P(None, "lat", "lon"),
        P(None, "lat", "lon"),
        P("lat", "lon"),
        P(None, ("lat", "lon")),
        P(("lat", "lon"), None, None),
        P(("lat", "lon"), None, None),
        P(("lat", "lon"), None, None),
    )
    out_specs = P(None, None, "lat", "lon")
    return jax.shard_map(local, mesh=mesh, in_specs=in_specs, out_specs=out_specs, check_vma=False)
```

```python
import functools

import jax
import jax.numpy as jnp
import numpy as np
from jax import lax
from jax.experimental import pallas as pl
from jax.experimental.pallas import tpu as pltpu
from jax.sharding import PartitionSpec as P

F32 = jnp.float32
BF16 = jnp.bfloat16
LANES = 128
SUB = 8
TABLE_ROWS = 16
PARTS = 4
PACK = 16
LEVELS = 6
FORWARD = 4
BACKWARD = 4


def lane_of(shape):
    return lax.broadcasted_iota(jnp.int32, shape, len(shape) - 1)


def remap_rows(links):
    return 5 * TABLE_ROWS + 2 * (links // LANES)


def load_kernel(
    links,
    tracers,
    east_courant,
    north_courant,
    fluxes,
    source,
    weight,
    cells,
    east,
    own,
    east_msg,
    west_msg,
    north_msg,
    south_msg,
    corner_msg,
    own_msg,
    flux_in,
    source_in,
    weight_in,
    last_north,
    sem,
):
    _, levels, rows, _ = tracers.shape
    part = levels // PARTS
    half = levels // 2
    small = [
        pltpu.make_async_copy(fluxes, flux_in, sem.at[0]),
        pltpu.make_async_copy(source, source_in, sem.at[1]),
        pltpu.make_async_copy(weight, weight_in, sem.at[2]),
        pltpu.make_async_copy(north_courant.at[:, pl.ds(rows - SUB, SUB), :], last_north, sem.at[3]),
    ]
    large = []
    for q in range(PARTS):
        at = pl.ds(q * part, part)
        large.append(
            [
                pltpu.make_async_copy(tracers.at[0, at], cells.at[0, at], sem.at[4 + 3 * q]),
                pltpu.make_async_copy(tracers.at[1, at], cells.at[1, at], sem.at[5 + 3 * q]),
                pltpu.make_async_copy(east_courant.at[at], east.at[at], sem.at[6 + 3 * q]),
            ]
        )
    for copy in small:
        copy.start()
    for group in large:
        for copy in group:
            copy.start()
    for copy in small:
        copy.wait()
    quarter = fluxes.shape[1] // 4
    places = ((own_msg, 0), (east_msg, 2 * rows), (north_msg, 5 * levels), (corner_msg, 0))
    for n, (msg, base) in enumerate(places):
        for f in range(5):
            for u in range(TABLE_ROWS):
                cut = pl.ds(n * quarter + u * LANES, LANES)
                row = flux_in[f : f + 1, cut]
                if f == 1:
                    row = row + flux_in[5:6, cut]
                msg[pl.ds(base + f * TABLE_ROWS + u, 1), :] = row
        base = base + 5 * TABLE_ROWS
        for c in range(links // LANES):
            cut = pl.ds(c * LANES, LANES)
            msg[pl.ds(base + c, 1), :] = source_in[n : n + 1, cut].astype(F32)
            msg[pl.ds(base + links // LANES + c, 1), :] = weight_in[n : n + 1, cut]
    for k in range(levels):
        north_msg[pl.ds(4 * levels + k, 1), :] = last_north[k, SUB - 1 : SUB, :]

    lane = lane_of((SUB, LANES))
    group = lane // 4
    for q in range(PARTS):
        for copy in large[q]:
            copy.wait()
        side = q * part // half
        offset = q * part % half

        def pack(rb, carry):
            at = pl.ds(pl.multiple_of(rb * SUB, SUB), SUB)
            for slot, ref in ((side, cells.at[0]), (2 + side, cells.at[1]), (4 + side, east)):
                packed = own[slot, at, :] if offset else jnp.zeros((SUB, LANES), F32)
                for j in range(part):
                    moved = pltpu.roll(ref[q * part + j, at, :], 4 * (offset + j) + 2, 1)
                    packed = jnp.where(group == offset + j, moved, packed)
                own[slot, at, :] = packed
            return carry

        lax.fori_loop(0, rows // SUB, pack, 0, unroll=PACK)
        for t in range(2):
            for k in range(q * part, (q + 1) * part):
                at = pl.ds(2 * (t * levels + k), 2)
                south_msg[at, :] = cells[t, k, 0:2, :]
                north_msg[at, :] = cells[t, k, rows - 2 : rows, :]

    early = lane % 4 < 2
    spare = lane >= 2 * levels
    last_column = (4 * lane + 1) % LANES

    def messages(rb, carry):
        at = pl.ds(pl.multiple_of(rb * SUB, SUB), SUB)
        for t in range(2):
            first = own[2 * t, at, :]
            second = own[2 * t + 1, at, :]
            courant = jnp.take_along_axis(own[4 + t, at, :], last_column, axis=1, mode="promise_in_bounds")
            tails = jnp.where(early, first, pltpu.roll(second, 2, 1))
            place = pl.ds(pl.multiple_of(t * rows + rb * SUB, SUB), SUB)
            east_msg[place, :] = jnp.where(spare, courant, tails)
            west_msg[place, :] = jnp.where(early, pltpu.roll(first, LANES - 2, 1), second)
        return carry

    lax.fori_loop(0, rows // SUB, messages, 0, unroll=4)


def in_hbm(*arrays):
    return [pltpu.with_memory_space_constraint(a, pltpu.HBM) for a in arrays]


def load(tracers, east_courant, north_courant, fluxes, source, weight):
    _, levels, rows, cols = tracers.shape
    links = source.shape[1]
    remap = remap_rows(links)
    hbm = pl.BlockSpec(memory_space=pltpu.HBM)
    vmem = pl.BlockSpec(memory_space=pltpu.VMEM)
    shapes = [
        tracers.shape,
        east_courant.shape,
        (6, rows, cols),
        (2 * rows + remap, LANES),
        (2 * rows, LANES),
        (5 * levels + remap, LANES),
        (4 * levels, LANES),
        (remap, LANES),
        (remap, LANES),
    ]
    return pl.pallas_call(
        functools.partial(load_kernel, links),
        in_specs=[hbm] * 6,
        out_specs=[vmem] * len(shapes),
        out_shape=[pltpu.VMEM(shape, F32) for shape in shapes],
        scratch_shapes=[
            pltpu.VMEM(fluxes.shape, F32),
            pltpu.VMEM(source.shape, jnp.int32),
            pltpu.VMEM(weight.shape, F32),
            pltpu.VMEM((levels, SUB, cols), F32),
            pltpu.SemaphoreType.DMA((4 + 3 * PARTS,)),
        ],
        compiler_params=pltpu.CompilerParams(vmem_limit_bytes=16 << 20),
        name="load",
    )(*in_hbm(tracers, east_courant, north_courant, fluxes, source, weight))


def stencil_weights(cols):
    i = lax.broadcasted_iota(jnp.int32, (2 * cols, 2 * cols), 0) % cols
    j = lax.broadcasted_iota(jnp.int32, (2 * cols, 2 * cols), 1)
    face = j % cols - j // cols
    gap = i - face
    near = (gap == 0) | (gap == 1)
    far = (gap == -1) | (gap == 2)
    return jnp.where(near, 7.0, jnp.where(far, -1.0, 0.0)).astype(BF16)


def interior_kernel(
    cells,
    east,
    north_courant,
    diffusivity,
    from_south,
    from_north,
    advected,
    diff,
    weights,
    north,
    sem,
):
    _, levels, rows, cols = cells.shape
    weights[...] = stencil_weights(cols)
    part = levels // PARTS
    sub = lax.broadcasted_iota(jnp.int32, (SUB, LANES), 0)
    blocks = rows // SUB
    copies = []
    for q in range(PARTS):
        at = pl.ds(q * part, part)
        copies.append(pltpu.make_async_copy(north_courant.at[at], north.at[at], sem.at[q]))
    last = pltpu.make_async_copy(diffusivity, diff, sem.at[PARTS])
    for copy in copies:
        copy.start()
    last.start()

    def halo_row(msg, index):
        return jnp.broadcast_to(msg[pl.ds(index, 1), :], (SUB, LANES))

    def level(k, carry):
        west_courant = [pltpu.roll(east[k, i * SUB : (i + 1) * SUB, :], 1, 1) for i in range(blocks)]
        for t in range(2):
            unit = t * levels + k
            whole = cells[t, k]
            high = whole.astype(BF16)
            low = (whole - high.astype(F32)).astype(BF16)
            faces = jnp.dot(
                jnp.concatenate([high, low], 1), weights[...], preferred_element_type=F32
            )
            below = from_south[pl.ds(2 * unit, 2), :]
            inside = cells[t, k, 0:2, :]
            courant = from_south[pl.ds(4 * levels + k, 1), :]
            south = courant * (7.0 * (below[1:2] + inside[0:1]) - (below[0:1] + inside[1:2]))
            south = jnp.broadcast_to(south, (SUB, LANES))
            for i in range(blocks):
                r0 = i * SUB
                here = cells[t, k, r0 : r0 + SUB, :]
                east_flux = east[k, r0 : r0 + SUB, :] * faces[r0 : r0 + SUB, :cols]
                west_flux = west_courant[i] * faces[r0 : r0 + SUB, cols:]
                if i == 0:
                    low_one = jnp.where(
                        sub == 0, halo_row(from_south, 2 * unit + 1), pltpu.roll(here, 1, 0)
                    )
                else:
                    low_one = cells[t, k, r0 - 1 : r0 - 1 + SUB, :]
                if i == blocks - 1:
                    near = halo_row(from_north, 2 * unit)
                    far = halo_row(from_north, 2 * unit + 1)
                    up_one = jnp.where(sub == SUB - 1, near, pltpu.roll(here, SUB - 1, 0))
                    up_two = pltpu.roll(here, SUB - 2, 0)
                    up_two = jnp.where(
                        sub == SUB - 1, far, jnp.where(sub == SUB - 2, near, up_two)
                    )
                else:
                    up_one = cells[t, k, r0 + 1 : r0 + 1 + SUB, :]
                    up_two = cells[t, k, r0 + 2 : r0 + 2 + SUB, :]
                face = 7.0 * (here + up_one) - (low_one + up_two)
                north_flux = north[k, r0 : r0 + SUB, :] * face
                moved = pltpu.roll(north_flux, 1, 0)
                south_flux = jnp.where(sub == 0, south, moved)
                south = moved
                change = (east_flux - west_flux) + (north_flux - south_flux)
                advected[t, k, r0 : r0 + SUB, :] = here - change * (1.0 / 12.0)
        return carry

    for q in range(PARTS):
        copies[q].wait()
        lax.fori_loop(q * part, (q + 1) * part, level, 0, unroll=LEVELS)
    last.wait()


def interior(cells, east, north_courant, diffusivity, from_south, from_north):
    _, levels, rows, cols = cells.shape
    hbm = pl.BlockSpec(memory_space=pltpu.HBM)
    vmem = pl.BlockSpec(memory_space=pltpu.VMEM)
    return pl.pallas_call(
        interior_kernel,
        in_specs=[vmem] * 2 + [hbm] * 2 + [vmem] * 2,
        out_specs=[vmem] * 2,
        out_shape=[pltpu.VMEM(cells.shape, F32), pltpu.VMEM(diffusivity.shape, F32)],
        scratch_shapes=[
            pltpu.VMEM((2 * cols, 2 * cols), BF16),
            pltpu.VMEM(north_courant.shape, F32),
            pltpu.SemaphoreType.DMA((PARTS + 1,)),
        ],
        compiler_params=pltpu.CompilerParams(vmem_limit_bytes=16 << 20),
        name="interior",
    )(cells, east, *in_hbm(north_courant, diffusivity), from_south, from_north)


def gather_links(msg, base, n, links, picked):
    rows = links // LANES
    for g in range(rows // SUB):
        cells = msg[pl.ds(base + 5 * TABLE_ROWS + g * SUB, SUB), :].astype(jnp.int32)
        weights = msg[pl.ds(base + 5 * TABLE_ROWS + rows + g * SUB, SUB), :]
        low = cells % LANES
        high = (cells // LANES) % TABLE_ROWS
        for f in range(5):
            total = jnp.zeros((SUB, LANES), F32)
            for u in range(TABLE_ROWS):
                row = jnp.broadcast_to(msg[pl.ds(base + f * TABLE_ROWS + u, 1), :], (SUB, LANES))
                found = jnp.take_along_axis(row, low, axis=1, mode="promise_in_bounds")
                total = jnp.where(high == u, found, total)
            picked[f, pl.ds(n * rows + g * SUB, SUB), :] = total * weights


def scatter_links(picked, target, n, links, rows, cols):
    half_rows = rows // 2
    half_cols = cols // 2
    count = links // LANES
    wide = 4 * half_cols
    short = half_rows // 4
    tall_iota = lax.broadcasted_iota(jnp.int32, (wide, LANES), 0)
    short_iota = lax.broadcasted_iota(jnp.int32, (short, LANES), 0)
    total = jnp.zeros((10 * short, wide), F32)
    group = 8
    for g in range(count // group):
        lefts = []
        rights = []
        for c in range(g * group, (g + 1) * group):
            cell = target[n : n + 1, c * LANES : (c + 1) * LANES]
            row = cell // cols - (1 - n // 2) * half_rows
            col = cell % cols - (1 - n % 2) * half_cols
            short_at = jnp.broadcast_to(row % short, (short, LANES)) == short_iota
            wide_at = jnp.broadcast_to(row // short * half_cols + col, (wide, LANES)) == tall_iota
            rights.append(jnp.where(wide_at, 1.0, 0.0).astype(BF16))
            pieces = []
            for f in range(5):
                value = picked[f, pl.ds(n * count + c, 1), :]
                high = value.astype(BF16).astype(F32)
                low = value - high
                for part in (high, low):
                    spread = jnp.broadcast_to(part, (short, LANES))
                    pieces.append(jnp.where(short_at, spread, 0.0).astype(BF16))
            lefts.append(jnp.concatenate(pieces, 0))
        left = jnp.concatenate(lefts, 1)
        right = jnp.concatenate(rights, 1)
        total = total + lax.dot_general(
            left, right, (((1,), (1,)), ((), ())), preferred_element_type=F32
        )
    return total


def remap_kernel(links, rows, cols, numbers, bases, target, *refs):
    count = len(numbers)
    quads = refs[count]
    picked = refs[count + 1]
    for i, (n, base) in enumerate(zip(numbers, bases)):
        gather_links(refs[i], base, n, links, picked)
        quads[i] = scatter_links(picked, target, n, links, rows, cols)


def remap(target, blocks, rows, cols):
    links = target.shape[1]
    numbers = tuple(n for n, _, _ in blocks)
    bases = tuple(base for _, _, base in blocks)
    vmem = pl.BlockSpec(memory_space=pltpu.VMEM)
    return pl.pallas_call(
        functools.partial(remap_kernel, links, rows, cols, numbers, bases),
        in_specs=[vmem] * (1 + len(blocks)),
        out_specs=vmem,
        out_shape=jax.ShapeDtypeStruct((len(blocks), 10 * rows // 8, 2 * cols), F32),
        scratch_shapes=[pltpu.VMEM((5, 4 * links // LANES, LANES), F32)],
        compiler_params=pltpu.CompilerParams(vmem_limit_bytes=16 << 20),
        name="remap",
    )(target, *[msg for _, msg, _ in blocks])


def main_kernel(
    links,
    chunk_rows,
    tables,
    cells,
    advected,
    diff,
    land,
    target,
    own,
    from_west,
    from_east,
    earlier,
    out,
    values,
    gains,
    picked,
    surface,
    fix,
    out_sem,
):
    _, levels, rows, cols = cells.shape
    chunks = rows // chunk_rows
    lane = lane_of((SUB, LANES))

    def store(c):
        part = pl.ds(c * chunk_rows, chunk_rows)
        return pltpu.make_async_copy(
            values.at[:, :, part, :], out.at[:, :, part, :], out_sem.at[c]
        )

    gather_links(from_west, 2 * rows, 1, links, picked)
    eastern = scatter_links(picked, target, 1, links, rows, cols)
    quads = [earlier[0], eastern, earlier[1], earlier[2]]
    short = rows // 8
    for pair in range(2):
        left = quads[2 * pair + 1]
        right = quads[2 * pair]
        for f in range(5):
            at = 2 * f * short
            one = left[at : at + short] + left[at + short : at + 2 * short]
            two = right[at : at + short] + right[at + short : at + 2 * short]
            for g in range(4):
                half = slice(g // 2 * LANES, g // 2 * LANES + LANES)
                a = one[:, half]
                b = two[:, half]
                if g % 2:
                    a = pltpu.roll(a, LANES // 2, 1)
                else:
                    b = pltpu.roll(b, LANES // 2, 1)
                merged = jnp.where(lane_of((short, LANES)) < LANES // 2, a, b)
                base = (1 - pair) * (rows // 2) + g * short
                surface[f, base : base + short, :] = merged
    for rb in range(rows // SUB):
        at = pl.ds(rb * SUB, SUB)
        s3 = surface[3, at, :]
        s4 = surface[4, at, :]
        surface[3, at, :] = 2.0 * jnp.sqrt(s3 * s3 + s4 * s4)

    half = levels // 2
    place_in_group = lane % 4
    spread = (2 * levels + lane // 4) % LANES
    for side in range(2):

        def mend(rb, carry):
            at = pl.ds(pl.multiple_of(rb * SUB, SUB), SUB)
            msg_at = pl.ds(pl.multiple_of(side * rows + rb * SUB, SUB), SUB)
            courant = own[4 + side, at, :]
            courant_before = pltpu.roll(courant, 1, 1)
            west_courant = jnp.take_along_axis(
                from_west[msg_at, :], spread, axis=1, mode="promise_in_bounds"
            )
            for t in range(2):
                msg_at = pl.ds(pl.multiple_of(t * rows + rb * SUB, SUB), SUB)
                west = from_west[msg_at, :]
                right = from_east[msg_at, :]
                if side:
                    west = pltpu.roll(west, LANES - 2, 1)
                    right = pltpu.roll(right, LANES - 2, 1)
                inner = own[2 * t + side, at, :]
                inner_next = pltpu.roll(inner, LANES - 1, 1)
                west_one = pltpu.roll(west, 1, 1)
                west_two = pltpu.roll(west, 2, 1)
                product = courant * right
                second = courant * (7.0 * pltpu.roll(right, 1, 1)) - product + pltpu.roll(product, 1, 1)
                third = (
                    courant_before * (7.0 * inner - inner_next)
                    - courant * west_one
                    - west_courant * (7.0 * (west_one + inner) - (west_two + inner_next))
                )
                fourth = courant_before * west_two
                change = jnp.where(
                    place_in_group < 2,
                    jnp.where(place_in_group == 0, -product, second),
                    jnp.where(place_in_group == 2, third, fourth),
                )
                fix[t, side, at, :] = change * (-1.0 / 12.0)
            return carry

        lax.fori_loop(0, rows // SUB, mend, 0, unroll=4)

    at_edge = (lane >= LANES - 2) | (lane < 2)
    blocks = chunk_rows // SUB

    def advect(t, k, base):
        side = k // half
        shift = (2 * LANES - 2 - 4 * (k % half)) % LANES
        result = []
        for i in range(blocks):
            at = pl.ds(base + i * SUB, SUB)
            edge = pltpu.roll(fix[t, side, at, :], shift, 1)
            result.append(advected[t, k, at, :] + jnp.where(at_edge, edge, 0.0))
        return result

    for c in range(chunks):
        base = c * chunk_rows

        def forward(k, carry, last=False):
            new = []
            heat_all = advect(0, k, base)
            salt_all = advect(1, k, base)
            for i in range(blocks):
                r0 = base + i * SUB
                above, lead, heat, salt = carry[4 * i : 4 * i + 4]
                heat_in = heat_all[i] + surface[2, r0 : r0 + SUB, :] * tables[0, k]
                salt_in = salt_all[i]
                if last:
                    inverse = 1.0 / lead
                    below = above
                else:
                    below = diff[k, r0 : r0 + SUB, :] + surface[3, r0 : r0 + SUB, :] * tables[1, k]
                    pivot = lead + below
                    rough = pl.reciprocal(pivot, approx=True)
                    inverse = rough * (2.0 - pivot * rough)
                heat = (heat_in + above * heat) * inverse
                salt = (salt_in + above * salt) * inverse
                values[0, k, r0 : r0 + SUB, :] = heat
                values[1, k, r0 : r0 + SUB, :] = salt
                if not last:
                    gains[k, i * SUB : (i + 1) * SUB, :] = below * inverse
                    lead = 1.0 + below * (lead * inverse)
                new += [below, lead, heat, salt]
            return tuple(new)

        carry = []
        for i in range(blocks):
            r0 = base + i * SUB
            one = jnp.ones((SUB, LANES), F32)
            carry += [one, one, 0.5 * surface[0, r0 : r0 + SUB, :], 0.5 * surface[1, r0 : r0 + SUB, :]]
        spare = (levels - 1) % FORWARD
        carry = lax.fori_loop(0, levels - 1 - spare, forward, tuple(carry), unroll=FORWARD)
        for k in range(levels - 1 - spare, levels - 1):
            carry = forward(k, carry)
        carry = forward(levels - 1, carry, True)

        def finish(k, i, heat, salt):
            r0 = base + i * SUB
            wet = land[r0 : r0 + SUB, :] == 1
            values[0, k, r0 : r0 + SUB, :] = jnp.where(wet, heat, cells[0, k, r0 : r0 + SUB, :])
            values[1, k, r0 : r0 + SUB, :] = jnp.where(wet, salt, cells[1, k, r0 : r0 + SUB, :])

        def backward(step, carry):
            k = levels - 2 - step
            new = []
            for i in range(blocks):
                r0 = base + i * SUB
                heat, salt = carry[2 * i : 2 * i + 2]
                gain = gains[k, i * SUB : (i + 1) * SUB, :]
                heat = values[0, k, r0 : r0 + SUB, :] + gain * heat
                salt = values[1, k, r0 : r0 + SUB, :] + gain * salt
                finish(k, i, heat, salt)
                new += [heat, salt]
            return tuple(new)

        ends = []
        for i in range(blocks):
            heat, salt = carry[4 * i + 2 : 4 * i + 4]
            finish(levels - 1, i, heat, salt)
            ends += [heat, salt]
        spare = (levels - 1) % BACKWARD
        carry = lax.fori_loop(0, levels - 1 - spare, backward, tuple(ends), unroll=BACKWARD)
        for k in range(levels - 1 - spare, levels - 1):
            carry = backward(k, carry)
        store(c).start()
    for c in range(chunks):
        store(c).wait()


def step(cells, advected, diff, land, target, own, from_west, from_east, earlier, chunk_rows=64):
    _, levels, rows, cols = cells.shape
    links = target.shape[1]
    depth = np.arange(levels)
    decay = np.exp(-4.0 * depth / levels)
    absorb = decay - np.exp(-4.0 * (depth + 1.0) / levels)
    tables = jnp.asarray(np.stack([0.5 * absorb, decay]), F32)
    chunks = rows // chunk_rows
    hbm = pl.BlockSpec(memory_space=pl.ANY)
    vmem = pl.BlockSpec(memory_space=pltpu.VMEM)
    return pl.pallas_call(
        functools.partial(main_kernel, links, chunk_rows),
        in_specs=[pl.BlockSpec(memory_space=pltpu.SMEM)] + [vmem] * 9,
        out_specs=hbm,
        out_shape=jax.ShapeDtypeStruct(cells.shape, F32),
        scratch_shapes=[
            pltpu.VMEM((2, levels, rows, cols), F32),
            pltpu.VMEM((levels, chunk_rows, cols), F32),
            pltpu.VMEM((5, 4 * links // LANES, LANES), F32),
            pltpu.VMEM((5, rows, cols), F32),
            pltpu.VMEM((2, 2, rows, cols), F32),
            pltpu.SemaphoreType.DMA((chunks,)),
        ],
        compiler_params=pltpu.CompilerParams(vmem_limit_bytes=16 << 20),
        name="step",
    )(tables, cells, advected, diff, land, target, own, from_west, from_east, earlier)


def ring(axis, by):
    length = lax.axis_size(axis)
    return [(i, (i + by) % length) for i in range(length)]


def line(axis, by):
    length = lax.axis_size(axis)
    return [(i, i + by) for i in range(length) if 0 <= i + by < length]


def diagonal():
    lats = lax.axis_size("lat")
    lons = lax.axis_size("lon")
    return [
        (i * lons + j, (i + 1) * lons + (j + 1) % lons) for i in range(lats - 1) for j in range(lons)
    ]


def local(
    tracers,
    east_courant,
    north_courant,
    diffusivity,
    land_sea,
    fluxes,
    source_cell,
    link_weight,
    target_cell,
):
    _, levels, rows, cols = tracers.shape
    target = target_cell[0]
    cells, east, own, to_east, to_west, to_north, to_south, corner, own_links = load(
        tracers, east_courant, north_courant, fluxes, source_cell[0], link_weight[0]
    )
    from_corner = lax.ppermute(corner, ("lat", "lon"), diagonal())
    from_south = lax.ppermute(to_north, "lat", line("lat", 1))
    from_north = lax.ppermute(to_south, "lat", line("lat", -1))
    from_west = lax.ppermute(to_east, "lon", ring("lon", 1))
    from_east = lax.ppermute(to_west, "lon", ring("lon", -1))
    advected, diff = interior(cells, east, north_courant, diffusivity, from_south, from_north)
    earlier = remap(
        target, [(0, own_links, 0), (2, from_south, 5 * levels), (3, from_corner, 0)], rows, cols
    )
    return step(cells, advected, diff, land_sea, target, own, from_west, from_east, earlier)


def solution(mesh):
    in_specs = (
        P(None, None, "lat", "lon"),
        P(None, "lat", "lon"),
        P(None, "lat", "lon"),
        P(None, "lat", "lon"),
        P("lat", "lon"),
        P(None, ("lat", "lon")),
        P(("lat", "lon"), None, None),
        P(("lat", "lon"), None, None),
        P(("lat", "lon"), None, None),
    )
    out_specs = P(None, None, "lat", "lon")
    return jax.shard_map(local, mesh=mesh, in_specs=in_specs, out_specs=out_specs, check_vma=False)
```

```python
import functools

import jax
import jax.numpy as jnp
import numpy as np
from jax import lax
from jax.experimental import pallas as pl
from jax.experimental.pallas import tpu as pltpu
from jax.sharding import PartitionSpec as P

F32 = jnp.float32
BF16 = jnp.bfloat16
LANES = 128
SUB = 8
TABLE_ROWS = 16
PARTS = 4
PACK = 16
LEVELS = 6
FORWARD = 4
BACKWARD = 4


def lane_of(shape):
    return lax.broadcasted_iota(jnp.int32, shape, len(shape) - 1)


def remap_rows(links):
    return 5 * TABLE_ROWS + 2 * (links // LANES)


def load_kernel(
    links,
    tracers,
    east_courant,
    north_courant,
    fluxes,
    source,
    weight,
    cells,
    east,
    own,
    east_msg,
    west_msg,
    north_msg,
    south_msg,
    corner_msg,
    own_msg,
    own_rows,
    flux_in,
    source_in,
    weight_in,
    first_north,
    last_north,
    sem,
):
    _, levels, rows, _ = tracers.shape
    lat = lax.axis_index("lat")
    has_north = (lat < lax.axis_size("lat") - 1).astype(F32)
    has_south = (lat > 0).astype(F32)
    part = levels // PARTS
    half = levels // 2
    small = [
        pltpu.make_async_copy(fluxes, flux_in, sem.at[0]),
        pltpu.make_async_copy(source, source_in, sem.at[1]),
        pltpu.make_async_copy(weight, weight_in, sem.at[2]),
        pltpu.make_async_copy(north_courant.at[:, pl.ds(rows - SUB, SUB), :], last_north, sem.at[3]),
        pltpu.make_async_copy(north_courant.at[:, pl.ds(0, SUB), :], first_north, sem.at[4 + 3 * PARTS]),
    ]
    large = []
    for q in range(PARTS):
        at = pl.ds(q * part, part)
        large.append(
            [
                pltpu.make_async_copy(tracers.at[0, at], cells.at[0, at], sem.at[4 + 3 * q]),
                pltpu.make_async_copy(tracers.at[1, at], cells.at[1, at], sem.at[5 + 3 * q]),
                pltpu.make_async_copy(east_courant.at[at], east.at[at], sem.at[6 + 3 * q]),
            ]
        )
    for copy in small:
        copy.start()
    for group in large:
        for copy in group:
            copy.start()
    for copy in small:
        copy.wait()
    quarter = fluxes.shape[1] // 4
    places = ((own_msg, 0), (east_msg, 2 * rows), (north_msg, 5 * levels), (corner_msg, 0))
    for n, (msg, base) in enumerate(places):
        for f in range(5):
            for u in range(TABLE_ROWS):
                cut = pl.ds(n * quarter + u * LANES, LANES)
                row = flux_in[f : f + 1, cut]
                if f == 1:
                    row = row + flux_in[5:6, cut]
                msg[pl.ds(base + f * TABLE_ROWS + u, 1), :] = row
        base = base + 5 * TABLE_ROWS
        for c in range(links // LANES):
            cut = pl.ds(c * LANES, LANES)
            msg[pl.ds(base + c, 1), :] = source_in[n : n + 1, cut].astype(F32)
            row = weight_in[n : n + 1, cut]
            msg[pl.ds(base + links // LANES + c, 1), :] = row * has_north if n >= 2 else row
    for k in range(levels):
        north_msg[pl.ds(4 * levels + k, 1), :] = last_north[k, SUB - 1 : SUB, :] * has_north
        own_rows[pl.ds(k, 1), :] = first_north[k, 0:1, :]
        own_rows[pl.ds(levels + k, 1), :] = last_north[k, SUB - 2 : SUB - 1, :]
        own_rows[pl.ds(2 * levels + k, 1), :] = last_north[k, SUB - 1 : SUB, :]

    lane = lane_of((SUB, LANES))
    group = lane // 4
    for q in range(PARTS):
        for copy in large[q]:
            copy.wait()
        side = q * part // half
        offset = q * part % half

        def pack(rb, carry):
            at = pl.ds(pl.multiple_of(rb * SUB, SUB), SUB)
            for slot, ref in ((side, cells.at[0]), (2 + side, cells.at[1]), (4 + side, east)):
                packed = own[slot, at, :] if offset else jnp.zeros((SUB, LANES), F32)
                for j in range(part):
                    moved = pltpu.roll(ref[q * part + j, at, :], 4 * (offset + j) + 2, 1)
                    packed = jnp.where(group == offset + j, moved, packed)
                own[slot, at, :] = packed
            return carry

        lax.fori_loop(0, rows // SUB, pack, 0, unroll=PACK)
        for t in range(2):
            for k in range(q * part, (q + 1) * part):
                for j in range(2):
                    at = pl.ds((2 * t + j) * levels + k, 1)
                    low = cells[t, k, j : j + 1, :]
                    high = cells[t, k, rows - 2 + j : rows - 1 + j, :]
                    south_msg[at, :] = low * has_south
                    north_msg[at, :] = high * has_north
                    own_rows[pl.ds((3 + 2 * t + j) * levels + k, 1), :] = low

    early = lane % 4 < 2
    spare = lane >= 2 * levels
    last_column = (4 * lane + 1) % LANES

    def messages(rb, carry):
        at = pl.ds(pl.multiple_of(rb * SUB, SUB), SUB)
        for t in range(2):
            first = own[2 * t, at, :]
            second = own[2 * t + 1, at, :]
            courant = jnp.take_along_axis(own[4 + t, at, :], last_column, axis=1, mode="promise_in_bounds")
            tails = jnp.where(early, first, pltpu.roll(second, 2, 1))
            place = pl.ds(pl.multiple_of(t * rows + rb * SUB, SUB), SUB)
            east_msg[place, :] = jnp.where(spare, courant, tails)
            west_msg[place, :] = jnp.where(early, pltpu.roll(first, LANES - 2, 1), second)
        return carry

    lax.fori_loop(0, rows // SUB, messages, 0, unroll=4)


def in_hbm(*arrays):
    return [pltpu.with_memory_space_constraint(a, pltpu.HBM) for a in arrays]


def load(tracers, east_courant, north_courant, fluxes, source, weight):
    _, levels, rows, cols = tracers.shape
    links = source.shape[1]
    remap = remap_rows(links)
    hbm = pl.BlockSpec(memory_space=pltpu.HBM)
    vmem = pl.BlockSpec(memory_space=pltpu.VMEM)
    shapes = [
        tracers.shape,
        east_courant.shape,
        (6, rows, cols),
        (2 * rows + remap, LANES),
        (2 * rows, LANES),
        (5 * levels + remap, LANES),
        (4 * levels, LANES),
        (remap, LANES),
        (remap, LANES),
        (7 * levels, LANES),
    ]
    return pl.pallas_call(
        functools.partial(load_kernel, links),
        in_specs=[hbm] * 6,
        out_specs=[vmem] * len(shapes),
        out_shape=[pltpu.VMEM(shape, F32) for shape in shapes],
        scratch_shapes=[
            pltpu.VMEM(fluxes.shape, F32),
            pltpu.VMEM(source.shape, jnp.int32),
            pltpu.VMEM(weight.shape, F32),
            pltpu.VMEM((levels, SUB, cols), F32),
            pltpu.VMEM((levels, SUB, cols), F32),
            pltpu.SemaphoreType.DMA((5 + 3 * PARTS,)),
        ],
        compiler_params=pltpu.CompilerParams(vmem_limit_bytes=16 << 20),
        name="load",
    )(*in_hbm(tracers, east_courant, north_courant, fluxes, source, weight))


def stencil_weights(cols):
    i = lax.broadcasted_iota(jnp.int32, (2 * cols, 2 * cols), 0) % cols
    j = lax.broadcasted_iota(jnp.int32, (2 * cols, 2 * cols), 1)
    face = j % cols - j // cols
    gap = i - face
    near = (gap == 0) | (gap == 1)
    far = (gap == -1) | (gap == 2)
    return jnp.where(near, 7.0, jnp.where(far, -1.0, 0.0)).astype(BF16)


def interior_kernel(
    cells,
    east,
    north_courant,
    diffusivity,
    advected,
    diff,
    weights,
    north,
    sem,
):
    _, levels, rows, cols = cells.shape
    weights[...] = stencil_weights(cols)
    part = levels // PARTS
    sub = lax.broadcasted_iota(jnp.int32, (SUB, LANES), 0)
    blocks = rows // SUB
    copies = []
    for q in range(PARTS):
        at = pl.ds(q * part, part)
        copies.append(pltpu.make_async_copy(north_courant.at[at], north.at[at], sem.at[q]))
    last = pltpu.make_async_copy(diffusivity, diff, sem.at[PARTS])
    for copy in copies:
        copy.start()
    last.start()

    def level(k, carry):
        west_courant = [pltpu.roll(east[k, i * SUB : (i + 1) * SUB, :], 1, 1) for i in range(blocks)]
        for t in range(2):
            whole = cells[t, k]
            high = whole.astype(BF16)
            low = (whole - high.astype(F32)).astype(BF16)
            faces = jnp.dot(
                jnp.concatenate([high, low], 1), weights[...], preferred_element_type=F32
            )
            south = jnp.zeros((SUB, LANES), F32)
            for i in range(blocks):
                r0 = i * SUB
                here = cells[t, k, r0 : r0 + SUB, :]
                east_flux = east[k, r0 : r0 + SUB, :] * faces[r0 : r0 + SUB, :cols]
                west_flux = west_courant[i] * faces[r0 : r0 + SUB, cols:]
                if i == 0:
                    low_one = jnp.where(sub == 0, 0.0, pltpu.roll(here, 1, 0))
                else:
                    low_one = cells[t, k, r0 - 1 : r0 - 1 + SUB, :]
                if i == blocks - 1:
                    up_one = jnp.where(sub == SUB - 1, 0.0, pltpu.roll(here, SUB - 1, 0))
                    up_two = jnp.where(sub >= SUB - 2, 0.0, pltpu.roll(here, SUB - 2, 0))
                else:
                    up_one = cells[t, k, r0 + 1 : r0 + 1 + SUB, :]
                    up_two = cells[t, k, r0 + 2 : r0 + 2 + SUB, :]
                face = 7.0 * (here + up_one) - (low_one + up_two)
                north_flux = north[k, r0 : r0 + SUB, :] * face
                moved = pltpu.roll(north_flux, 1, 0)
                south_flux = jnp.where(sub == 0, south, moved)
                south = moved
                change = (east_flux - west_flux) + (north_flux - south_flux)
                advected[t, k, r0 : r0 + SUB, :] = here - change * (1.0 / 12.0)
        return carry

    for q in range(PARTS):
        copies[q].wait()
        lax.fori_loop(q * part, (q + 1) * part, level, 0, unroll=LEVELS)
    last.wait()


def interior(cells, east, north_courant, diffusivity):
    _, levels, rows, cols = cells.shape
    hbm = pl.BlockSpec(memory_space=pltpu.HBM)
    vmem = pl.BlockSpec(memory_space=pltpu.VMEM)
    return pl.pallas_call(
        interior_kernel,
        in_specs=[vmem] * 2 + [hbm] * 2,
        out_specs=[vmem] * 2,
        out_shape=[pltpu.VMEM(cells.shape, F32), pltpu.VMEM(diffusivity.shape, F32)],
        scratch_shapes=[
            pltpu.VMEM((2 * cols, 2 * cols), BF16),
            pltpu.VMEM(north_courant.shape, F32),
            pltpu.SemaphoreType.DMA((PARTS + 1,)),
        ],
        compiler_params=pltpu.CompilerParams(vmem_limit_bytes=16 << 20),
        name="interior",
    )(cells, east, *in_hbm(north_courant, diffusivity))


def gather_links(msg, base, n, links, picked):
    rows = links // LANES
    for g in range(rows // SUB):
        cells = msg[pl.ds(base + 5 * TABLE_ROWS + g * SUB, SUB), :].astype(jnp.int32)
        weights = msg[pl.ds(base + 5 * TABLE_ROWS + rows + g * SUB, SUB), :]
        low = cells % LANES
        high = (cells // LANES) % TABLE_ROWS
        for f in range(5):
            total = jnp.zeros((SUB, LANES), F32)
            for u in range(TABLE_ROWS):
                row = jnp.broadcast_to(msg[pl.ds(base + f * TABLE_ROWS + u, 1), :], (SUB, LANES))
                found = jnp.take_along_axis(row, low, axis=1, mode="promise_in_bounds")
                total = jnp.where(high == u, found, total)
            picked[f, pl.ds(n * rows + g * SUB, SUB), :] = total * weights


def scatter_links(picked, target, n, links, rows, cols):
    half_rows = rows // 2
    half_cols = cols // 2
    count = links // LANES
    wide = 4 * half_cols
    short = half_rows // 4
    tall_iota = lax.broadcasted_iota(jnp.int32, (wide, LANES), 0)
    short_iota = lax.broadcasted_iota(jnp.int32, (short, LANES), 0)
    total = jnp.zeros((10 * short, wide), F32)
    group = 8
    for g in range(count // group):
        lefts = []
        rights = []
        for c in range(g * group, (g + 1) * group):
            cell = target[n : n + 1, c * LANES : (c + 1) * LANES]
            row = cell // cols - (1 - n // 2) * half_rows
            col = cell % cols - (1 - n % 2) * half_cols
            short_at = jnp.broadcast_to(row % short, (short, LANES)) == short_iota
            wide_at = jnp.broadcast_to(row // short * half_cols + col, (wide, LANES)) == tall_iota
            rights.append(jnp.where(wide_at, 1.0, 0.0).astype(BF16))
            pieces = []
            for f in range(5):
                value = picked[f, pl.ds(n * count + c, 1), :]
                high = value.astype(BF16).astype(F32)
                low = value - high
                for part in (high, low):
                    spread = jnp.broadcast_to(part, (short, LANES))
                    pieces.append(jnp.where(short_at, spread, 0.0).astype(BF16))
            lefts.append(jnp.concatenate(pieces, 0))
        left = jnp.concatenate(lefts, 1)
        right = jnp.concatenate(rights, 1)
        total = total + lax.dot_general(
            left, right, (((1,), (1,)), ((), ())), preferred_element_type=F32
        )
    return total


def remap_kernel(links, rows, cols, numbers, bases, target, *refs):
    count = len(numbers)
    quads = refs[count]
    picked = refs[count + 1]
    for i, (n, base) in enumerate(zip(numbers, bases)):
        gather_links(refs[i], base, n, links, picked)
        quads[i] = scatter_links(picked, target, n, links, rows, cols)


def remap(target, blocks, rows, cols):
    links = target.shape[1]
    numbers = tuple(n for n, _, _ in blocks)
    bases = tuple(base for _, _, base in blocks)
    vmem = pl.BlockSpec(memory_space=pltpu.VMEM)
    return pl.pallas_call(
        functools.partial(remap_kernel, links, rows, cols, numbers, bases),
        in_specs=[vmem] * (1 + len(blocks)),
        out_specs=vmem,
        out_shape=jax.ShapeDtypeStruct((len(blocks), 10 * rows // 8, 2 * cols), F32),
        scratch_shapes=[pltpu.VMEM((5, 4 * links // LANES, LANES), F32)],
        compiler_params=pltpu.CompilerParams(vmem_limit_bytes=16 << 20),
        name="remap",
    )(target, *[msg for _, msg, _ in blocks])


def main_kernel(
    links,
    chunk_rows,
    tables,
    cells,
    advected,
    diff,
    land,
    target,
    own,
    from_west,
    from_east,
    own_rows,
    from_south,
    from_north,
    earlier,
    out,
    values,
    gains,
    picked,
    surface,
    fix,
    row_fix,
    out_sem,
):
    _, levels, rows, cols = cells.shape
    chunks = rows // chunk_rows
    lane = lane_of((SUB, LANES))

    def store(c, q):
        part = pl.ds(c * chunk_rows, chunk_rows)
        at = pl.ds(q * (levels // PARTS), levels // PARTS)
        return pltpu.make_async_copy(
            values.at[:, at, part, :], out.at[:, at, part, :], out_sem.at[c, q]
        )

    gather_links(from_west, 2 * rows, 1, links, picked)
    eastern = scatter_links(picked, target, 1, links, rows, cols)
    quads = [earlier[0], eastern, earlier[1], earlier[2]]
    short = rows // 8
    for pair in range(2):
        left = quads[2 * pair + 1]
        right = quads[2 * pair]
        for f in range(5):
            at = 2 * f * short
            one = left[at : at + short] + left[at + short : at + 2 * short]
            two = right[at : at + short] + right[at + short : at + 2 * short]
            for g in range(4):
                half = slice(g // 2 * LANES, g // 2 * LANES + LANES)
                a = one[:, half]
                b = two[:, half]
                if g % 2:
                    a = pltpu.roll(a, LANES // 2, 1)
                else:
                    b = pltpu.roll(b, LANES // 2, 1)
                merged = jnp.where(lane_of((short, LANES)) < LANES // 2, a, b)
                base = (1 - pair) * (rows // 2) + g * short
                surface[f, base : base + short, :] = merged
    for rb in range(rows // SUB):
        at = pl.ds(rb * SUB, SUB)
        s3 = surface[3, at, :]
        s4 = surface[4, at, :]
        surface[3, at, :] = 2.0 * jnp.sqrt(s3 * s3 + s4 * s4)

    half = levels // 2
    place_in_group = lane % 4
    spread = (2 * levels + lane // 4) % LANES
    for side in range(2):

        def mend(rb, carry):
            at = pl.ds(pl.multiple_of(rb * SUB, SUB), SUB)
            msg_at = pl.ds(pl.multiple_of(side * rows + rb * SUB, SUB), SUB)
            courant = own[4 + side, at, :]
            courant_before = pltpu.roll(courant, 1, 1)
            west_courant = jnp.take_along_axis(
                from_west[msg_at, :], spread, axis=1, mode="promise_in_bounds"
            )
            for t in range(2):
                msg_at = pl.ds(pl.multiple_of(t * rows + rb * SUB, SUB), SUB)
                west = from_west[msg_at, :]
                right = from_east[msg_at, :]
                if side:
                    west = pltpu.roll(west, LANES - 2, 1)
                    right = pltpu.roll(right, LANES - 2, 1)
                inner = own[2 * t + side, at, :]
                inner_next = pltpu.roll(inner, LANES - 1, 1)
                west_one = pltpu.roll(west, 1, 1)
                west_two = pltpu.roll(west, 2, 1)
                product = courant * right
                second = courant * (7.0 * pltpu.roll(right, 1, 1)) - product + pltpu.roll(product, 1, 1)
                third = (
                    courant_before * (7.0 * inner - inner_next)
                    - courant * west_one
                    - west_courant * (7.0 * (west_one + inner) - (west_two + inner_next))
                )
                fourth = courant_before * west_two
                change = jnp.where(
                    place_in_group < 2,
                    jnp.where(place_in_group == 0, -product, second),
                    jnp.where(place_in_group == 2, third, fourth),
                )
                fix[t, side, at, :] = change * (-1.0 / 12.0)
            return carry

        lax.fori_loop(0, rows // SUB, mend, 0, unroll=4)

    def plane(msg, p):
        return msg[p * levels : (p + 1) * levels, :]

    for t in range(2):
        inner_one = plane(own_rows, 3 + 2 * t)
        inner_two = plane(own_rows, 4 + 2 * t)
        below_two = plane(from_south, 2 * t)
        below_one = plane(from_south, 2 * t + 1)
        above_one = plane(from_north, 2 * t)
        above_two = plane(from_north, 2 * t + 1)
        first = plane(own_rows, 0) * below_one
        entering = plane(from_south, 4) * (7.0 * (below_one + inner_one) - (below_two + inner_two))
        last = plane(own_rows, 1) * above_one
        top = plane(own_rows, 2) * (7.0 * above_one - above_two)
        for p, change in enumerate((-first - entering, first, -last, top + last)):
            row_fix[t, p] = change * (-1.0 / 12.0)

    at_edge = (lane >= LANES - 2) | (lane < 2)
    sub = lax.broadcasted_iota(jnp.int32, (SUB, LANES), 0)
    blocks = chunk_rows // SUB

    def row_pair(t, k, p, at):
        one = jnp.broadcast_to(row_fix[t, p, pl.ds(k, 1), :], (SUB, LANES))
        two = jnp.broadcast_to(row_fix[t, p + 1, pl.ds(k, 1), :], (SUB, LANES))
        return jnp.where(sub == at, one, jnp.where(sub == at + 1, two, 0.0))

    def advect(t, k, base):
        side = k // half
        shift = (2 * LANES - 2 - 4 * (k % half)) % LANES
        result = []
        for i in range(blocks):
            at = pl.ds(base + i * SUB, SUB)
            edge = pltpu.roll(fix[t, side, at, :], shift, 1)
            value = advected[t, k, at, :] + jnp.where(at_edge, edge, 0.0)
            if base + i * SUB == 0:
                value = value + row_pair(t, k, 0, 0)
            if base + (i + 1) * SUB == rows:
                value = value + row_pair(t, k, 2, SUB - 2)
            result.append(value)
        return result

    for c in range(chunks):
        base = c * chunk_rows

        def forward(k, carry, last=False):
            new = []
            heat_all = advect(0, k, base)
            salt_all = advect(1, k, base)
            for i in range(blocks):
                r0 = base + i * SUB
                above, lead, heat, salt = carry[4 * i : 4 * i + 4]
                heat_in = heat_all[i] + surface[2, r0 : r0 + SUB, :] * tables[0, k]
                salt_in = salt_all[i]
                if last:
                    inverse = 1.0 / lead
                    below = above
                else:
                    below = diff[k, r0 : r0 + SUB, :] + surface[3, r0 : r0 + SUB, :] * tables[1, k]
                    pivot = lead + below
                    rough = pl.reciprocal(pivot, approx=True)
                    inverse = rough * (2.0 - pivot * rough)
                heat = (heat_in + above * heat) * inverse
                salt = (salt_in + above * salt) * inverse
                values[0, k, r0 : r0 + SUB, :] = heat
                values[1, k, r0 : r0 + SUB, :] = salt
                if not last:
                    gains[k, i * SUB : (i + 1) * SUB, :] = below * inverse
                    lead = 1.0 + below * (lead * inverse)
                new += [below, lead, heat, salt]
            return tuple(new)

        carry = []
        for i in range(blocks):
            r0 = base + i * SUB
            one = jnp.ones((SUB, LANES), F32)
            carry += [one, one, 0.5 * surface[0, r0 : r0 + SUB, :], 0.5 * surface[1, r0 : r0 + SUB, :]]
        spare = (levels - 1) % FORWARD
        carry = lax.fori_loop(0, levels - 1 - spare, forward, tuple(carry), unroll=FORWARD)
        for k in range(levels - 1 - spare, levels - 1):
            carry = forward(k, carry)
        carry = forward(levels - 1, carry, True)

        def finish(k, i, heat, salt):
            r0 = base + i * SUB
            wet = land[r0 : r0 + SUB, :] == 1
            values[0, k, r0 : r0 + SUB, :] = jnp.where(wet, heat, cells[0, k, r0 : r0 + SUB, :])
            values[1, k, r0 : r0 + SUB, :] = jnp.where(wet, salt, cells[1, k, r0 : r0 + SUB, :])

        def backward(step, carry):
            k = levels - 2 - step
            new = []
            for i in range(blocks):
                r0 = base + i * SUB
                heat, salt = carry[2 * i : 2 * i + 2]
                gain = gains[k, i * SUB : (i + 1) * SUB, :]
                heat = values[0, k, r0 : r0 + SUB, :] + gain * heat
                salt = values[1, k, r0 : r0 + SUB, :] + gain * salt
                finish(k, i, heat, salt)
                new += [heat, salt]
            return tuple(new)

        ends = []
        for i in range(blocks):
            heat, salt = carry[4 * i + 2 : 4 * i + 4]
            finish(levels - 1, i, heat, salt)
            ends += [heat, salt]
        carry = backward(0, tuple(ends))
        done = 1
        for q in reversed(range(PARTS)):
            until = levels - 1 - q * (levels // PARTS)
            while (until - done) % BACKWARD:
                carry = backward(done, carry)
                done += 1
            carry = lax.fori_loop(done, until, backward, carry, unroll=BACKWARD)
            done = until
            store(c, q).start()
    for c in range(chunks):
        for q in range(PARTS):
            store(c, q).wait()


def step(cells, advected, diff, land, target, messages, chunk_rows=64):
    _, levels, rows, cols = cells.shape
    links = target.shape[1]
    depth = np.arange(levels)
    decay = np.exp(-4.0 * depth / levels)
    absorb = decay - np.exp(-4.0 * (depth + 1.0) / levels)
    tables = jnp.asarray(np.stack([0.5 * absorb, decay]), F32)
    chunks = rows // chunk_rows
    hbm = pl.BlockSpec(memory_space=pl.ANY)
    vmem = pl.BlockSpec(memory_space=pltpu.VMEM)
    return pl.pallas_call(
        functools.partial(main_kernel, links, chunk_rows),
        in_specs=[pl.BlockSpec(memory_space=pltpu.SMEM)] + [vmem] * (5 + len(messages)),
        out_specs=hbm,
        out_shape=jax.ShapeDtypeStruct(cells.shape, F32),
        scratch_shapes=[
            pltpu.VMEM((2, levels, rows, cols), F32),
            pltpu.VMEM((levels, chunk_rows, cols), F32),
            pltpu.VMEM((5, 4 * links // LANES, LANES), F32),
            pltpu.VMEM((5, rows, cols), F32),
            pltpu.VMEM((2, 2, rows, cols), F32),
            pltpu.VMEM((2, 4, levels, cols), F32),
            pltpu.SemaphoreType.DMA((chunks, PARTS)),
        ],
        compiler_params=pltpu.CompilerParams(vmem_limit_bytes=16 << 20),
        name="step",
    )(tables, cells, advected, diff, land, target, *messages)


def ring(axis, by):
    length = lax.axis_size(axis)
    return [(i, (i + by) % length) for i in range(length)]


def diagonal():
    lats = lax.axis_size("lat")
    lons = lax.axis_size("lon")
    return [
        (i * lons + j, (i + 1) % lats * lons + (j + 1) % lons) for i in range(lats) for j in range(lons)
    ]


def local(
    tracers,
    east_courant,
    north_courant,
    diffusivity,
    land_sea,
    fluxes,
    source_cell,
    link_weight,
    target_cell,
):
    _, levels, rows, cols = tracers.shape
    target = target_cell[0]
    cells, east, own, to_east, to_west, to_north, to_south, corner, own_links, own_rows = load(
        tracers, east_courant, north_courant, fluxes, source_cell[0], link_weight[0]
    )
    from_corner = lax.ppermute(corner, ("lat", "lon"), diagonal())
    from_south = lax.ppermute(to_north, "lat", ring("lat", 1))
    from_north = lax.ppermute(to_south, "lat", ring("lat", -1))
    from_west = lax.ppermute(to_east, "lon", ring("lon", 1))
    from_east = lax.ppermute(to_west, "lon", ring("lon", -1))
    advected, diff = interior(cells, east, north_courant, diffusivity)
    earlier = remap(
        target, [(0, own_links, 0), (2, from_south, 5 * levels), (3, from_corner, 0)], rows, cols
    )
    messages = (own, from_west, from_east, own_rows, from_south, from_north, earlier)
    return step(cells, advected, diff, land_sea, target, messages)


def solution(mesh):
    in_specs = (
        P(None, None, "lat", "lon"),
        P(None, "lat", "lon"),
        P(None, "lat", "lon"),
        P(None, "lat", "lon"),
        P("lat", "lon"),
        P(None, ("lat", "lon")),
        P(("lat", "lon"), None, None),
        P(("lat", "lon"), None, None),
        P(("lat", "lon"), None, None),
    )
    out_specs = P(None, None, "lat", "lon")
    return jax.shard_map(local, mesh=mesh, in_specs=in_specs, out_specs=out_specs, check_vma=False)
```

```python
import functools

import jax
import jax.numpy as jnp
import numpy as np
from jax import lax
from jax.experimental import pallas as pl
from jax.experimental.pallas import tpu as pltpu
from jax.sharding import PartitionSpec as P

F32 = jnp.float32
BF16 = jnp.bfloat16
LANES = 128
SUB = 8
TABLE_ROWS = 16
PARTS = 4
PACK = 16
LEVELS = 6
FORWARD = 4
BACKWARD = 4


def lane_of(shape):
    return lax.broadcasted_iota(jnp.int32, shape, len(shape) - 1)


def remap_rows(links):
    return 5 * TABLE_ROWS + 2 * (links // LANES)


def load_kernel(
    links,
    tracers,
    east_courant,
    north_courant,
    fluxes,
    source,
    weight,
    cells,
    east,
    own,
    east_msg,
    west_msg,
    north_msg,
    south_msg,
    corner_msg,
    own_msg,
    own_rows,
    flux_in,
    source_in,
    weight_in,
    first_north,
    last_north,
    sem,
):
    _, levels, rows, _ = tracers.shape
    lat = lax.axis_index("lat")
    has_north = (lat < lax.axis_size("lat") - 1).astype(F32)
    has_south = (lat > 0).astype(F32)
    part = levels // PARTS
    half = levels // 2
    small = [
        pltpu.make_async_copy(fluxes, flux_in, sem.at[0]),
        pltpu.make_async_copy(source, source_in, sem.at[1]),
        pltpu.make_async_copy(weight, weight_in, sem.at[2]),
        pltpu.make_async_copy(north_courant.at[:, pl.ds(rows - SUB, SUB), :], last_north, sem.at[3]),
        pltpu.make_async_copy(north_courant.at[:, pl.ds(0, SUB), :], first_north, sem.at[4 + 3 * PARTS]),
    ]
    large = []
    for q in range(PARTS):
        at = pl.ds(q * part, part)
        large.append(
            [
                pltpu.make_async_copy(tracers.at[0, at], cells.at[0, at], sem.at[4 + 3 * q]),
                pltpu.make_async_copy(tracers.at[1, at], cells.at[1, at], sem.at[5 + 3 * q]),
                pltpu.make_async_copy(east_courant.at[at], east.at[at], sem.at[6 + 3 * q]),
            ]
        )
    for copy in small:
        copy.start()
    for group in large:
        for copy in group:
            copy.start()
    for copy in small:
        copy.wait()
    quarter = fluxes.shape[1] // 4
    places = ((own_msg, 0), (east_msg, 2 * rows), (north_msg, 5 * levels), (corner_msg, 0))
    for n, (msg, base) in enumerate(places):
        for f in range(5):
            for u in range(TABLE_ROWS):
                cut = pl.ds(n * quarter + u * LANES, LANES)
                row = flux_in[f : f + 1, cut]
                if f == 1:
                    row = row + flux_in[5:6, cut]
                msg[pl.ds(base + f * TABLE_ROWS + u, 1), :] = row
        base = base + 5 * TABLE_ROWS
        for c in range(links // LANES):
            cut = pl.ds(c * LANES, LANES)
            msg[pl.ds(base + c, 1), :] = source_in[n : n + 1, cut].astype(F32)
            row = weight_in[n : n + 1, cut]
            msg[pl.ds(base + links // LANES + c, 1), :] = row * has_north if n >= 2 else row
    for k in range(levels):
        north_msg[pl.ds(4 * levels + k, 1), :] = last_north[k, SUB - 1 : SUB, :] * has_north
        own_rows[pl.ds(k, 1), :] = first_north[k, 0:1, :]
        own_rows[pl.ds(levels + k, 1), :] = last_north[k, SUB - 2 : SUB - 1, :]
        own_rows[pl.ds(2 * levels + k, 1), :] = last_north[k, SUB - 1 : SUB, :]

    lane = lane_of((SUB, LANES))
    group = lane // 4
    for q in range(PARTS):
        for copy in large[q]:
            copy.wait()
        side = q * part // half
        offset = q * part % half

        def pack(rb, carry):
            at = pl.ds(pl.multiple_of(rb * SUB, SUB), SUB)
            for slot, ref in ((side, cells.at[0]), (2 + side, cells.at[1]), (4 + side, east)):
                packed = own[slot, at, :] if offset else jnp.zeros((SUB, LANES), F32)
                for j in range(part):
                    moved = pltpu.roll(ref[q * part + j, at, :], 4 * (offset + j) + 2, 1)
                    packed = jnp.where(group == offset + j, moved, packed)
                own[slot, at, :] = packed
            return carry

        lax.fori_loop(0, rows // SUB, pack, 0, unroll=PACK)
        for t in range(2):
            for k in range(q * part, (q + 1) * part):
                for j in range(2):
                    at = pl.ds((2 * t + j) * levels + k, 1)
                    low = cells[t, k, j : j + 1, :]
                    high = cells[t, k, rows - 2 + j : rows - 1 + j, :]
                    south_msg[at, :] = low * has_south
                    north_msg[at, :] = high * has_north
                    own_rows[pl.ds((3 + 2 * t + j) * levels + k, 1), :] = low

    early = lane % 4 < 2
    spare = lane >= 2 * levels
    last_column = (4 * lane + 1) % LANES

    def messages(rb, carry):
        at = pl.ds(pl.multiple_of(rb * SUB, SUB), SUB)
        for t in range(2):
            first = own[2 * t, at, :]
            second = own[2 * t + 1, at, :]
            courant = jnp.take_along_axis(own[4 + t, at, :], last_column, axis=1, mode="promise_in_bounds")
            tails = jnp.where(early, first, pltpu.roll(second, 2, 1))
            place = pl.ds(pl.multiple_of(t * rows + rb * SUB, SUB), SUB)
            east_msg[place, :] = jnp.where(spare, courant, tails)
            west_msg[place, :] = jnp.where(early, pltpu.roll(first, LANES - 2, 1), second)
        return carry

    lax.fori_loop(0, rows // SUB, messages, 0, unroll=4)


def in_hbm(*arrays):
    return [pltpu.with_memory_space_constraint(a, pltpu.HBM) for a in arrays]


def load(tracers, east_courant, north_courant, fluxes, source, weight):
    _, levels, rows, cols = tracers.shape
    links = source.shape[1]
    remap = remap_rows(links)
    hbm = pl.BlockSpec(memory_space=pltpu.HBM)
    vmem = pl.BlockSpec(memory_space=pltpu.VMEM)
    shapes = [
        tracers.shape,
        east_courant.shape,
        (6, rows, cols),
        (2 * rows + remap, LANES),
        (2 * rows, LANES),
        (5 * levels + remap, LANES),
        (4 * levels, LANES),
        (remap, LANES),
        (remap, LANES),
        (7 * levels, LANES),
    ]
    return pl.pallas_call(
        functools.partial(load_kernel, links),
        in_specs=[hbm] * 6,
        out_specs=[vmem] * len(shapes),
        out_shape=[pltpu.VMEM(shape, F32) for shape in shapes],
        scratch_shapes=[
            pltpu.VMEM(fluxes.shape, F32),
            pltpu.VMEM(source.shape, jnp.int32),
            pltpu.VMEM(weight.shape, F32),
            pltpu.VMEM((levels, SUB, cols), F32),
            pltpu.VMEM((levels, SUB, cols), F32),
            pltpu.SemaphoreType.DMA((5 + 3 * PARTS,)),
        ],
        compiler_params=pltpu.CompilerParams(vmem_limit_bytes=16 << 20),
        name="load",
    )(*in_hbm(tracers, east_courant, north_courant, fluxes, source, weight))


def stencil_weights(cols):
    i = lax.broadcasted_iota(jnp.int32, (2 * cols, 2 * cols), 0) % cols
    j = lax.broadcasted_iota(jnp.int32, (2 * cols, 2 * cols), 1)
    face = j % cols - j // cols
    gap = i - face
    near = (gap == 0) | (gap == 1)
    far = (gap == -1) | (gap == 2)
    return jnp.where(near, 7.0, jnp.where(far, -1.0, 0.0)).astype(BF16)


def interior_kernel(
    cells,
    east,
    north_courant,
    diffusivity,
    advected,
    diff,
    weights,
    north,
    sem,
):
    _, levels, rows, cols = cells.shape
    weights[...] = stencil_weights(cols)
    part = levels // PARTS
    sub = lax.broadcasted_iota(jnp.int32, (SUB, LANES), 0)
    blocks = rows // SUB
    copies = []
    for q in range(PARTS):
        at = pl.ds(q * part, part)
        copies.append(pltpu.make_async_copy(north_courant.at[at], north.at[at], sem.at[q]))
    last = pltpu.make_async_copy(diffusivity, diff, sem.at[PARTS])
    for copy in copies:
        copy.start()
    last.start()

    def level(k, carry):
        west_courant = [pltpu.roll(east[k, i * SUB : (i + 1) * SUB, :], 1, 1) for i in range(blocks)]
        for t in range(2):
            whole = cells[t, k]
            high = whole.astype(BF16)
            low = (whole - high.astype(F32)).astype(BF16)
            faces = jnp.dot(
                jnp.concatenate([high, low], 1), weights[...], preferred_element_type=F32
            )
            south = jnp.zeros((SUB, LANES), F32)
            for i in range(blocks):
                r0 = i * SUB
                here = cells[t, k, r0 : r0 + SUB, :]
                east_flux = east[k, r0 : r0 + SUB, :] * faces[r0 : r0 + SUB, :cols]
                west_flux = west_courant[i] * faces[r0 : r0 + SUB, cols:]
                if i == 0:
                    low_one = jnp.where(sub == 0, 0.0, pltpu.roll(here, 1, 0))
                else:
                    low_one = cells[t, k, r0 - 1 : r0 - 1 + SUB, :]
                if i == blocks - 1:
                    up_one = jnp.where(sub == SUB - 1, 0.0, pltpu.roll(here, SUB - 1, 0))
                    up_two = jnp.where(sub >= SUB - 2, 0.0, pltpu.roll(here, SUB - 2, 0))
                else:
                    up_one = cells[t, k, r0 + 1 : r0 + 1 + SUB, :]
                    up_two = cells[t, k, r0 + 2 : r0 + 2 + SUB, :]
                face = 7.0 * (here + up_one) - (low_one + up_two)
                north_flux = north[k, r0 : r0 + SUB, :] * face
                moved = pltpu.roll(north_flux, 1, 0)
                south_flux = jnp.where(sub == 0, south, moved)
                south = moved
                change = (east_flux - west_flux) + (north_flux - south_flux)
                advected[t, k, r0 : r0 + SUB, :] = here - change * (1.0 / 12.0)
        return carry

    for q in range(PARTS):
        copies[q].wait()
        lax.fori_loop(q * part, (q + 1) * part, level, 0, unroll=LEVELS)
    last.wait()


def interior(cells, east, north_courant, diffusivity):
    _, levels, rows, cols = cells.shape
    hbm = pl.BlockSpec(memory_space=pltpu.HBM)
    vmem = pl.BlockSpec(memory_space=pltpu.VMEM)
    return pl.pallas_call(
        interior_kernel,
        in_specs=[vmem] * 2 + [hbm] * 2,
        out_specs=[vmem] * 2,
        out_shape=[pltpu.VMEM(cells.shape, F32), pltpu.VMEM(diffusivity.shape, F32)],
        scratch_shapes=[
            pltpu.VMEM((2 * cols, 2 * cols), BF16),
            pltpu.VMEM(north_courant.shape, F32),
            pltpu.SemaphoreType.DMA((PARTS + 1,)),
        ],
        compiler_params=pltpu.CompilerParams(vmem_limit_bytes=16 << 20),
        name="interior",
    )(cells, east, *in_hbm(north_courant, diffusivity))


def gather_links(msg, base, n, links, picked):
    rows = links // LANES
    for g in range(rows // SUB):
        cells = msg[pl.ds(base + 5 * TABLE_ROWS + g * SUB, SUB), :].astype(jnp.int32)
        weights = msg[pl.ds(base + 5 * TABLE_ROWS + rows + g * SUB, SUB), :]
        low = cells % LANES
        high = (cells // LANES) % TABLE_ROWS
        for f in range(5):
            total = jnp.zeros((SUB, LANES), F32)
            for u in range(TABLE_ROWS):
                row = jnp.broadcast_to(msg[pl.ds(base + f * TABLE_ROWS + u, 1), :], (SUB, LANES))
                found = jnp.take_along_axis(row, low, axis=1, mode="promise_in_bounds")
                total = jnp.where(high == u, found, total)
            picked[f, pl.ds(n * rows + g * SUB, SUB), :] = total * weights


def scatter_links(picked, target, n, links, rows, cols):
    half_rows = rows // 2
    half_cols = cols // 2
    count = links // LANES
    wide = 4 * half_cols
    short = half_rows // 4
    tall_iota = lax.broadcasted_iota(jnp.int32, (wide, LANES), 0).astype(jnp.int16)
    short_iota = lax.broadcasted_iota(jnp.int32, (short, LANES), 0)
    ones = jnp.ones((wide, LANES), BF16)
    total = jnp.zeros((wide, 10 * short), F32)
    group = count
    for g in range(count // group):
        lefts = []
        rights = []
        for c in range(g * group, (g + 1) * group):
            cell = target[n : n + 1, c * LANES : (c + 1) * LANES]
            row = cell // cols - (1 - n // 2) * half_rows
            col = cell % cols - (1 - n % 2) * half_cols
            short_at = jnp.broadcast_to(row % short, (short, LANES)) == short_iota
            place = (row // short * half_cols + col).astype(jnp.int16)
            wide_at = jnp.broadcast_to(place, (wide, LANES)) == tall_iota
            rights.append(jnp.where(wide_at, ones, jnp.zeros_like(ones)))
            pieces = []
            for f in range(5):
                value = picked[f, pl.ds(n * count + c, 1), :]
                high = value.astype(BF16).astype(F32)
                low = value - high
                for part in (high, low):
                    spread = jnp.broadcast_to(part, (short, LANES))
                    pieces.append(jnp.where(short_at, spread, 0.0).astype(BF16))
            lefts.append(jnp.concatenate(pieces, 0))
        left = jnp.concatenate(lefts, 1)
        right = jnp.concatenate(rights, 1)
        total = total + lax.dot_general(
            right, left, (((1,), (1,)), ((), ())), preferred_element_type=F32
        )
    return total.T


def remap_kernel(links, rows, cols, numbers, bases, target, *refs):
    count = len(numbers)
    quads, picked = refs[-2:]
    for i, (n, base) in enumerate(zip(numbers, bases)):
        gather_links(refs[i], base, n, links, picked)
        quads[i] = scatter_links(picked, target, n, links, rows, cols)


def remap(target, blocks, rows, cols, after=()):
    links = target.shape[1]
    numbers = tuple(n for n, _, _ in blocks)
    bases = tuple(base for _, _, base in blocks)
    vmem = pl.BlockSpec(memory_space=pltpu.VMEM)
    return pl.pallas_call(
        functools.partial(remap_kernel, links, rows, cols, numbers, bases),
        in_specs=[vmem] * (1 + len(blocks)) + [pl.BlockSpec(memory_space=pl.ANY)] * len(after),
        out_specs=vmem,
        out_shape=jax.ShapeDtypeStruct((len(blocks), 10 * rows // 8, 2 * cols), F32),
        scratch_shapes=[pltpu.VMEM((5, 4 * links // LANES, LANES), F32)],
        compiler_params=pltpu.CompilerParams(vmem_limit_bytes=16 << 20),
        name="remap",
    )(target, *[msg for _, msg, _ in blocks], *after)


def main_kernel(
    chunk_rows,
    tables,
    cells,
    advected,
    diff,
    land,
    own,
    from_west,
    from_east,
    own_rows,
    from_south,
    from_north,
    upper,
    lower,
    out,
    values,
    gains,
    surface,
    fix,
    row_fix,
    out_sem,
):
    _, levels, rows, cols = cells.shape
    chunks = rows // chunk_rows
    lane = lane_of((SUB, LANES))

    def store(c, q):
        part = pl.ds(c * chunk_rows, chunk_rows)
        at = pl.ds(q * (levels // PARTS), levels // PARTS)
        return pltpu.make_async_copy(
            values.at[:, at, part, :], out.at[:, at, part, :], out_sem.at[c, q]
        )

    quads = [upper[0], upper[1], lower[0], lower[1]]
    short = rows // 8
    for pair in range(2):
        left = quads[2 * pair + 1]
        right = quads[2 * pair]
        for f in range(5):
            at = 2 * f * short
            one = left[at : at + short] + left[at + short : at + 2 * short]
            two = right[at : at + short] + right[at + short : at + 2 * short]
            for g in range(4):
                half = slice(g // 2 * LANES, g // 2 * LANES + LANES)
                a = one[:, half]
                b = two[:, half]
                if g % 2:
                    a = pltpu.roll(a, LANES // 2, 1)
                else:
                    b = pltpu.roll(b, LANES // 2, 1)
                merged = jnp.where(lane_of((short, LANES)) < LANES // 2, a, b)
                base = (1 - pair) * (rows // 2) + g * short
                surface[f, base : base + short, :] = merged
    for rb in range(rows // SUB):
        at = pl.ds(rb * SUB, SUB)
        s3 = surface[3, at, :]
        s4 = surface[4, at, :]
        surface[3, at, :] = 2.0 * jnp.sqrt(s3 * s3 + s4 * s4)

    half = levels // 2
    place_in_group = lane % 4
    spread = (2 * levels + lane // 4) % LANES
    for side in range(2):

        def mend(rb, carry):
            at = pl.ds(pl.multiple_of(rb * SUB, SUB), SUB)
            msg_at = pl.ds(pl.multiple_of(side * rows + rb * SUB, SUB), SUB)
            courant = own[4 + side, at, :]
            courant_before = pltpu.roll(courant, 1, 1)
            west_courant = jnp.take_along_axis(
                from_west[msg_at, :], spread, axis=1, mode="promise_in_bounds"
            )
            for t in range(2):
                msg_at = pl.ds(pl.multiple_of(t * rows + rb * SUB, SUB), SUB)
                west = from_west[msg_at, :]
                right = from_east[msg_at, :]
                if side:
                    west = pltpu.roll(west, LANES - 2, 1)
                    right = pltpu.roll(right, LANES - 2, 1)
                inner = own[2 * t + side, at, :]
                inner_next = pltpu.roll(inner, LANES - 1, 1)
                west_one = pltpu.roll(west, 1, 1)
                west_two = pltpu.roll(west, 2, 1)
                product = courant * right
                second = courant * (7.0 * pltpu.roll(right, 1, 1)) - product + pltpu.roll(product, 1, 1)
                third = (
                    courant_before * (7.0 * inner - inner_next)
                    - courant * west_one
                    - west_courant * (7.0 * (west_one + inner) - (west_two + inner_next))
                )
                fourth = courant_before * west_two
                change = jnp.where(
                    place_in_group < 2,
                    jnp.where(place_in_group == 0, -product, second),
                    jnp.where(place_in_group == 2, third, fourth),
                )
                fix[t, side, at, :] = change * (-1.0 / 12.0)
            return carry

        lax.fori_loop(0, rows // SUB, mend, 0, unroll=4)

    def plane(msg, p):
        return msg[p * levels : (p + 1) * levels, :]

    for t in range(2):
        inner_one = plane(own_rows, 3 + 2 * t)
        inner_two = plane(own_rows, 4 + 2 * t)
        below_two = plane(from_south, 2 * t)
        below_one = plane(from_south, 2 * t + 1)
        above_one = plane(from_north, 2 * t)
        above_two = plane(from_north, 2 * t + 1)
        first = plane(own_rows, 0) * below_one
        entering = plane(from_south, 4) * (7.0 * (below_one + inner_one) - (below_two + inner_two))
        last = plane(own_rows, 1) * above_one
        top = plane(own_rows, 2) * (7.0 * above_one - above_two)
        for p, change in enumerate((-first - entering, first, -last, top + last)):
            row_fix[t, p] = change * (-1.0 / 12.0)

    at_edge = (lane >= LANES - 2) | (lane < 2)
    sub = lax.broadcasted_iota(jnp.int32, (SUB, LANES), 0)
    blocks = chunk_rows // SUB

    def row_pair(t, k, p, at):
        one = jnp.broadcast_to(row_fix[t, p, pl.ds(k, 1), :], (SUB, LANES))
        two = jnp.broadcast_to(row_fix[t, p + 1, pl.ds(k, 1), :], (SUB, LANES))
        return jnp.where(sub == at, one, jnp.where(sub == at + 1, two, 0.0))

    def advect(t, k, base):
        side = k // half
        shift = (2 * LANES - 2 - 4 * (k % half)) % LANES
        result = []
        for i in range(blocks):
            at = pl.ds(base + i * SUB, SUB)
            edge = pltpu.roll(fix[t, side, at, :], shift, 1)
            value = advected[t, k, at, :] + jnp.where(at_edge, edge, 0.0)
            if base + i * SUB == 0:
                value = value + row_pair(t, k, 0, 0)
            if base + (i + 1) * SUB == rows:
                value = value + row_pair(t, k, 2, SUB - 2)
            result.append(value)
        return result

    for c in range(chunks):
        base = c * chunk_rows

        def forward(k, carry, last=False):
            new = []
            heat_all = advect(0, k, base)
            salt_all = advect(1, k, base)
            for i in range(blocks):
                r0 = base + i * SUB
                above, lead, heat, salt = carry[4 * i : 4 * i + 4]
                heat_in = heat_all[i] + surface[2, r0 : r0 + SUB, :] * tables[0, k]
                salt_in = salt_all[i]
                if last:
                    inverse = 1.0 / lead
                    below = above
                else:
                    below = diff[k, r0 : r0 + SUB, :] + surface[3, r0 : r0 + SUB, :] * tables[1, k]
                    pivot = lead + below
                    rough = pl.reciprocal(pivot, approx=True)
                    inverse = rough * (2.0 - pivot * rough)
                heat = (heat_in + above * heat) * inverse
                salt = (salt_in + above * salt) * inverse
                values[0, k, r0 : r0 + SUB, :] = heat
                values[1, k, r0 : r0 + SUB, :] = salt
                if not last:
                    gains[k, i * SUB : (i + 1) * SUB, :] = below * inverse
                    lead = 1.0 + below * (lead * inverse)
                new += [below, lead, heat, salt]
            return tuple(new)

        carry = []
        for i in range(blocks):
            r0 = base + i * SUB
            one = jnp.ones((SUB, LANES), F32)
            carry += [one, one, 0.5 * surface[0, r0 : r0 + SUB, :], 0.5 * surface[1, r0 : r0 + SUB, :]]
        spare = (levels - 1) % FORWARD
        carry = lax.fori_loop(0, levels - 1 - spare, forward, tuple(carry), unroll=FORWARD)
        for k in range(levels - 1 - spare, levels - 1):
            carry = forward(k, carry)
        carry = forward(levels - 1, carry, True)

        def finish(k, i, heat, salt):
            r0 = base + i * SUB
            wet = land[r0 : r0 + SUB, :] == 1
            values[0, k, r0 : r0 + SUB, :] = jnp.where(wet, heat, cells[0, k, r0 : r0 + SUB, :])
            values[1, k, r0 : r0 + SUB, :] = jnp.where(wet, salt, cells[1, k, r0 : r0 + SUB, :])

        def backward(step, carry):
            k = levels - 2 - step
            new = []
            for i in range(blocks):
                r0 = base + i * SUB
                heat, salt = carry[2 * i : 2 * i + 2]
                gain = gains[k, i * SUB : (i + 1) * SUB, :]
                heat = values[0, k, r0 : r0 + SUB, :] + gain * heat
                salt = values[1, k, r0 : r0 + SUB, :] + gain * salt
                finish(k, i, heat, salt)
                new += [heat, salt]
            return tuple(new)

        ends = []
        for i in range(blocks):
            heat, salt = carry[4 * i + 2 : 4 * i + 4]
            finish(levels - 1, i, heat, salt)
            ends += [heat, salt]
        carry = backward(0, tuple(ends))
        done = 1
        for q in reversed(range(PARTS)):
            until = levels - 1 - q * (levels // PARTS)
            while (until - done) % BACKWARD:
                carry = backward(done, carry)
                done += 1
            carry = lax.fori_loop(done, until, backward, carry, unroll=BACKWARD)
            done = until
            store(c, q).start()
    for c in range(chunks):
        for q in range(PARTS):
            store(c, q).wait()


def step(cells, advected, diff, land, messages, chunk_rows=64):
    _, levels, rows, cols = cells.shape
    depth = np.arange(levels)
    decay = np.exp(-4.0 * depth / levels)
    absorb = decay - np.exp(-4.0 * (depth + 1.0) / levels)
    tables = jnp.asarray(np.stack([0.5 * absorb, decay]), F32)
    chunks = rows // chunk_rows
    hbm = pl.BlockSpec(memory_space=pl.ANY)
    vmem = pl.BlockSpec(memory_space=pltpu.VMEM)
    return pl.pallas_call(
        functools.partial(main_kernel, chunk_rows),
        in_specs=[pl.BlockSpec(memory_space=pltpu.SMEM)] + [vmem] * (4 + len(messages)),
        out_specs=hbm,
        out_shape=jax.ShapeDtypeStruct(cells.shape, F32),
        scratch_shapes=[
            pltpu.VMEM((2, levels, rows, cols), F32),
            pltpu.VMEM((levels, chunk_rows, cols), F32),
            pltpu.VMEM((5, rows, cols), F32),
            pltpu.VMEM((2, 2, rows, cols), F32),
            pltpu.VMEM((2, 4, levels, cols), F32),
            pltpu.SemaphoreType.DMA((chunks, PARTS)),
        ],
        compiler_params=pltpu.CompilerParams(vmem_limit_bytes=16 << 20),
        name="step",
    )(tables, cells, advected, diff, land, *messages)


def ring(axis, by):
    length = lax.axis_size(axis)
    return [(i, (i + by) % length) for i in range(length)]


def diagonal():
    lats = lax.axis_size("lat")
    lons = lax.axis_size("lon")
    return [
        (i * lons + j, (i + 1) % lats * lons + (j + 1) % lons) for i in range(lats) for j in range(lons)
    ]


def local(
    tracers,
    east_courant,
    north_courant,
    diffusivity,
    land_sea,
    fluxes,
    source_cell,
    link_weight,
    target_cell,
):
    _, levels, rows, cols = tracers.shape
    target = target_cell[0]
    cells, east, own, to_east, to_west, to_north, to_south, corner, own_links, own_rows = load(
        tracers, east_courant, north_courant, fluxes, source_cell[0], link_weight[0]
    )
    from_corner = lax.ppermute(corner, ("lat", "lon"), diagonal())
    from_south = lax.ppermute(to_north, "lat", ring("lat", 1))
    from_north = lax.ppermute(to_south, "lat", ring("lat", -1))
    from_west = lax.ppermute(to_east, "lon", ring("lon", 1))
    from_east = lax.ppermute(to_west, "lon", ring("lon", -1))
    advected, diff = interior(cells, east, north_courant, diffusivity)
    upper = remap(target, [(0, own_links, 0), (1, from_west, 2 * rows)], rows, cols)
    lower = remap(target, [(2, from_south, 5 * levels), (3, from_corner, 0)], rows, cols, [upper])
    messages = (own, from_west, from_east, own_rows, from_south, from_north, upper, lower)
    return step(cells, advected, diff, land_sea, messages)


def solution(mesh):
    in_specs = (
        P(None, None, "lat", "lon"),
        P(None, "lat", "lon"),
        P(None, "lat", "lon"),
        P(None, "lat", "lon"),
        P("lat", "lon"),
        P(None, ("lat", "lon")),
        P(("lat", "lon"), None, None),
        P(("lat", "lon"), None, None),
        P(("lat", "lon"), None, None),
    )
    out_specs = P(None, None, "lat", "lon")
    return jax.shard_map(local, mesh=mesh, in_specs=in_specs, out_specs=out_specs, check_vma=False)
```

```python
import functools

import jax
import jax.numpy as jnp
import numpy as np
from jax import lax
from jax.experimental import pallas as pl
from jax.experimental.pallas import tpu as pltpu
from jax.sharding import PartitionSpec as P

F32 = jnp.float32
BF16 = jnp.bfloat16
LANES = 128
SUB = 8
TABLE_ROWS = 16
PARTS = 4
PACK = 16
LEVELS = 12
FORWARD = 16
BACKWARD = 12


def lane_of(shape):
    return lax.broadcasted_iota(jnp.int32, shape, len(shape) - 1)


def remap_rows(links):
    return 5 * TABLE_ROWS + 2 * (links // LANES)


def load_kernel(
    links,
    tracers,
    east_courant,
    north_courant,
    fluxes,
    source,
    weight,
    cells,
    east,
    own,
    east_msg,
    west_msg,
    north_msg,
    south_msg,
    corner_msg,
    own_msg,
    own_rows,
    flux_in,
    source_in,
    weight_in,
    first_north,
    last_north,
    sem,
):
    _, levels, rows, _ = tracers.shape
    lat = lax.axis_index("lat")
    has_north = (lat < lax.axis_size("lat") - 1).astype(F32)
    has_south = (lat > 0).astype(F32)
    part = levels // PARTS
    half = levels // 2
    small = [
        pltpu.make_async_copy(fluxes, flux_in, sem.at[0]),
        pltpu.make_async_copy(source, source_in, sem.at[1]),
        pltpu.make_async_copy(weight, weight_in, sem.at[2]),
        pltpu.make_async_copy(north_courant.at[:, pl.ds(rows - SUB, SUB), :], last_north, sem.at[3]),
        pltpu.make_async_copy(north_courant.at[:, pl.ds(0, SUB), :], first_north, sem.at[4 + 3 * PARTS]),
    ]
    large = []
    for q in range(PARTS):
        at = pl.ds(q * part, part)
        large.append(
            [
                pltpu.make_async_copy(tracers.at[0, at], cells.at[0, at], sem.at[4 + 3 * q]),
                pltpu.make_async_copy(tracers.at[1, at], cells.at[1, at], sem.at[5 + 3 * q]),
                pltpu.make_async_copy(east_courant.at[at], east.at[at], sem.at[6 + 3 * q]),
            ]
        )
    for copy in small:
        copy.start()
    for group in large:
        for copy in group:
            copy.start()
    for copy in small:
        copy.wait()
    quarter = fluxes.shape[1] // 4
    places = ((own_msg, 0), (east_msg, 2 * rows), (north_msg, 5 * levels), (corner_msg, 0))
    for n, (msg, base) in enumerate(places):
        for f in range(5):
            for u in range(TABLE_ROWS):
                cut = pl.ds(n * quarter + u * LANES, LANES)
                row = flux_in[f : f + 1, cut]
                if f == 1:
                    row = row + flux_in[5:6, cut]
                msg[pl.ds(base + f * TABLE_ROWS + u, 1), :] = row
        base = base + 5 * TABLE_ROWS
        for c in range(links // LANES):
            cut = pl.ds(c * LANES, LANES)
            msg[pl.ds(base + c, 1), :] = source_in[n : n + 1, cut].astype(F32)
            row = weight_in[n : n + 1, cut]
            msg[pl.ds(base + links // LANES + c, 1), :] = row * has_north if n >= 2 else row
    for k in range(levels):
        north_msg[pl.ds(4 * levels + k, 1), :] = last_north[k, SUB - 1 : SUB, :] * has_north
        own_rows[pl.ds(k, 1), :] = first_north[k, 0:1, :]
        own_rows[pl.ds(levels + k, 1), :] = last_north[k, SUB - 2 : SUB - 1, :]
        own_rows[pl.ds(2 * levels + k, 1), :] = last_north[k, SUB - 1 : SUB, :]

    lane = lane_of((SUB, LANES))
    group = lane // 4
    for q in range(PARTS):
        for copy in large[q]:
            copy.wait()
        side = q * part // half
        offset = q * part % half

        def pack(rb, carry):
            at = pl.ds(pl.multiple_of(rb * SUB, SUB), SUB)
            for slot, ref in ((side, cells.at[0]), (2 + side, cells.at[1]), (4 + side, east)):
                packed = own[slot, at, :] if offset else jnp.zeros((SUB, LANES), F32)
                for j in range(part):
                    moved = pltpu.roll(ref[q * part + j, at, :], 4 * (offset + j) + 2, 1)
                    packed = jnp.where(group == offset + j, moved, packed)
                own[slot, at, :] = packed
            return carry

        lax.fori_loop(0, rows // SUB, pack, 0, unroll=PACK)
        for t in range(2):
            for k in range(q * part, (q + 1) * part):
                for j in range(2):
                    at = pl.ds((2 * t + j) * levels + k, 1)
                    low = cells[t, k, j : j + 1, :]
                    high = cells[t, k, rows - 2 + j : rows - 1 + j, :]
                    south_msg[at, :] = low * has_south
                    north_msg[at, :] = high * has_north
                    own_rows[pl.ds((3 + 2 * t + j) * levels + k, 1), :] = low

    early = lane % 4 < 2
    spare = lane >= 2 * levels
    last_column = (4 * lane + 1) % LANES

    def messages(rb, carry):
        at = pl.ds(pl.multiple_of(rb * SUB, SUB), SUB)
        for t in range(2):
            first = own[2 * t, at, :]
            second = own[2 * t + 1, at, :]
            courant = jnp.take_along_axis(own[4 + t, at, :], last_column, axis=1, mode="promise_in_bounds")
            tails = jnp.where(early, first, pltpu.roll(second, 2, 1))
            place = pl.ds(pl.multiple_of(t * rows + rb * SUB, SUB), SUB)
            east_msg[place, :] = jnp.where(spare, courant, tails)
            west_msg[place, :] = jnp.where(early, pltpu.roll(first, LANES - 2, 1), second)
        return carry

    lax.fori_loop(0, rows // SUB, messages, 0, unroll=4)


def in_hbm(*arrays):
    return [pltpu.with_memory_space_constraint(a, pltpu.HBM) for a in arrays]


def load(tracers, east_courant, north_courant, fluxes, source, weight):
    _, levels, rows, cols = tracers.shape
    links = source.shape[1]
    remap = remap_rows(links)
    hbm = pl.BlockSpec(memory_space=pltpu.HBM)
    vmem = pl.BlockSpec(memory_space=pltpu.VMEM)
    shapes = [
        tracers.shape,
        east_courant.shape,
        (6, rows, cols),
        (2 * rows + remap, LANES),
        (2 * rows, LANES),
        (5 * levels + remap, LANES),
        (4 * levels, LANES),
        (remap, LANES),
        (remap, LANES),
        (7 * levels, LANES),
    ]
    return pl.pallas_call(
        functools.partial(load_kernel, links),
        in_specs=[hbm] * 6,
        out_specs=[vmem] * len(shapes),
        out_shape=[pltpu.VMEM(shape, F32) for shape in shapes],
        scratch_shapes=[
            pltpu.VMEM(fluxes.shape, F32),
            pltpu.VMEM(source.shape, jnp.int32),
            pltpu.VMEM(weight.shape, F32),
            pltpu.VMEM((levels, SUB, cols), F32),
            pltpu.VMEM((levels, SUB, cols), F32),
            pltpu.SemaphoreType.DMA((5 + 3 * PARTS,)),
        ],
        compiler_params=pltpu.CompilerParams(vmem_limit_bytes=16 << 20),
        name="load",
    )(*in_hbm(tracers, east_courant, north_courant, fluxes, source, weight))


def stencil_weights(cols):
    i = lax.broadcasted_iota(jnp.int32, (2 * cols, 2 * cols), 0) % cols
    j = lax.broadcasted_iota(jnp.int32, (2 * cols, 2 * cols), 1)
    face = j % cols - j // cols
    gap = i - face
    near = (gap == 0) | (gap == 1)
    far = (gap == -1) | (gap == 2)
    return jnp.where(near, 7.0, jnp.where(far, -1.0, 0.0)).astype(BF16)


def interior_kernel(
    cells,
    east,
    north_courant,
    diffusivity,
    advected,
    diff,
    weights,
    north,
    sem,
):
    _, levels, rows, cols = cells.shape
    weights[...] = stencil_weights(cols)
    part = levels // PARTS
    sub = lax.broadcasted_iota(jnp.int32, (SUB, LANES), 0)
    blocks = rows // SUB
    copies = []
    for q in range(PARTS):
        at = pl.ds(q * part, part)
        copies.append(pltpu.make_async_copy(north_courant.at[at], north.at[at], sem.at[q]))
    last = pltpu.make_async_copy(diffusivity, diff, sem.at[PARTS])
    for copy in copies:
        copy.start()
    last.start()

    def level(k, carry):
        west_courant = [pltpu.roll(east[k, i * SUB : (i + 1) * SUB, :], 1, 1) for i in range(blocks)]
        for t in range(2):
            whole = cells[t, k]
            high = whole.astype(BF16)
            low = (whole - high.astype(F32)).astype(BF16)
            faces = jnp.dot(
                jnp.concatenate([high, low], 1), weights[...], preferred_element_type=F32
            )
            south = jnp.zeros((SUB, LANES), F32)
            for i in range(blocks):
                r0 = i * SUB
                here = cells[t, k, r0 : r0 + SUB, :]
                east_flux = east[k, r0 : r0 + SUB, :] * faces[r0 : r0 + SUB, :cols]
                west_flux = west_courant[i] * faces[r0 : r0 + SUB, cols:]
                if i == 0:
                    low_one = jnp.where(sub == 0, 0.0, pltpu.roll(here, 1, 0))
                else:
                    low_one = cells[t, k, r0 - 1 : r0 - 1 + SUB, :]
                if i == blocks - 1:
                    up_one = jnp.where(sub == SUB - 1, 0.0, pltpu.roll(here, SUB - 1, 0))
                    up_two = jnp.where(sub >= SUB - 2, 0.0, pltpu.roll(here, SUB - 2, 0))
                else:
                    up_one = cells[t, k, r0 + 1 : r0 + 1 + SUB, :]
                    up_two = cells[t, k, r0 + 2 : r0 + 2 + SUB, :]
                face = 7.0 * (here + up_one) - (low_one + up_two)
                north_flux = north[k, r0 : r0 + SUB, :] * face
                moved = pltpu.roll(north_flux, 1, 0)
                south_flux = jnp.where(sub == 0, south, moved)
                south = moved
                change = (east_flux - west_flux) + (north_flux - south_flux)
                advected[t, k, r0 : r0 + SUB, :] = here - change * (1.0 / 12.0)
        return carry

    for q in range(PARTS):
        copies[q].wait()
        lax.fori_loop(q * part, (q + 1) * part, level, 0, unroll=LEVELS)
    last.wait()


def interior(cells, east, north_courant, diffusivity):
    _, levels, rows, cols = cells.shape
    hbm = pl.BlockSpec(memory_space=pltpu.HBM)
    vmem = pl.BlockSpec(memory_space=pltpu.VMEM)
    return pl.pallas_call(
        interior_kernel,
        in_specs=[vmem] * 2 + [hbm] * 2,
        out_specs=[vmem] * 2,
        out_shape=[pltpu.VMEM(cells.shape, F32), pltpu.VMEM(diffusivity.shape, F32)],
        scratch_shapes=[
            pltpu.VMEM((2 * cols, 2 * cols), BF16),
            pltpu.VMEM(north_courant.shape, F32),
            pltpu.SemaphoreType.DMA((PARTS + 1,)),
        ],
        compiler_params=pltpu.CompilerParams(vmem_limit_bytes=16 << 20),
        name="interior",
    )(cells, east, *in_hbm(north_courant, diffusivity))


def gather_links(msg, base, n, links, picked):
    rows = links // LANES
    for g in range(rows // SUB):
        cells = msg[pl.ds(base + 5 * TABLE_ROWS + g * SUB, SUB), :].astype(jnp.int32)
        weights = msg[pl.ds(base + 5 * TABLE_ROWS + rows + g * SUB, SUB), :]
        low = cells % LANES
        high = (cells // LANES) % TABLE_ROWS
        for f in range(5):
            total = jnp.zeros((SUB, LANES), F32)
            for u in range(TABLE_ROWS):
                row = jnp.broadcast_to(msg[pl.ds(base + f * TABLE_ROWS + u, 1), :], (SUB, LANES))
                found = jnp.take_along_axis(row, low, axis=1, mode="promise_in_bounds")
                total = jnp.where(high == u, found, total)
            picked[f, pl.ds(n * rows + g * SUB, SUB), :] = total * weights


def scatter_links(picked, target, n, links, rows, cols):
    half_rows = rows // 2
    half_cols = cols // 2
    count = links // LANES
    wide = 4 * half_cols
    short = half_rows // 4
    tall_iota = lax.broadcasted_iota(jnp.int32, (wide, LANES), 0).astype(jnp.int16)
    short_iota = lax.broadcasted_iota(jnp.int32, (short, LANES), 0)
    ones = jnp.ones((wide, LANES), BF16)
    total = jnp.zeros((wide, 10 * short), F32)
    group = count
    for g in range(count // group):
        lefts = []
        rights = []
        for c in range(g * group, (g + 1) * group):
            cell = target[n : n + 1, c * LANES : (c + 1) * LANES]
            row = cell // cols - (1 - n // 2) * half_rows
            col = cell % cols - (1 - n % 2) * half_cols
            short_at = jnp.broadcast_to(row % short, (short, LANES)) == short_iota
            place = (row // short * half_cols + col).astype(jnp.int16)
            wide_at = jnp.broadcast_to(place, (wide, LANES)) == tall_iota
            rights.append(jnp.where(wide_at, ones, jnp.zeros_like(ones)))
            pieces = []
            for f in range(5):
                value = picked[f, pl.ds(n * count + c, 1), :]
                high = value.astype(BF16).astype(F32)
                low = value - high
                for part in (high, low):
                    spread = jnp.broadcast_to(part, (short, LANES))
                    pieces.append(jnp.where(short_at, spread, 0.0).astype(BF16))
            lefts.append(jnp.concatenate(pieces, 0))
        left = jnp.concatenate(lefts, 1)
        right = jnp.concatenate(rights, 1)
        total = total + lax.dot_general(
            right, left, (((1,), (1,)), ((), ())), preferred_element_type=F32
        )
    return total.T


def remap_kernel(links, rows, cols, numbers, bases, target, *refs):
    count = len(numbers)
    quads, picked = refs[-2:]
    for i, (n, base) in enumerate(zip(numbers, bases)):
        gather_links(refs[i], base, n, links, picked)
        quads[i] = scatter_links(picked, target, n, links, rows, cols)


def remap(target, blocks, rows, cols, after=()):
    links = target.shape[1]
    numbers = tuple(n for n, _, _ in blocks)
    bases = tuple(base for _, _, base in blocks)
    vmem = pl.BlockSpec(memory_space=pltpu.VMEM)
    return pl.pallas_call(
        functools.partial(remap_kernel, links, rows, cols, numbers, bases),
        in_specs=[vmem] * (1 + len(blocks)) + [pl.BlockSpec(memory_space=pl.ANY)] * len(after),
        out_specs=vmem,
        out_shape=jax.ShapeDtypeStruct((len(blocks), 10 * rows // 8, 2 * cols), F32),
        scratch_shapes=[pltpu.VMEM((5, 4 * links // LANES, LANES), F32)],
        compiler_params=pltpu.CompilerParams(vmem_limit_bytes=16 << 20),
        name="remap",
    )(target, *[msg for _, msg, _ in blocks], *after)


def main_kernel(
    chunk_rows,
    tables,
    cells,
    advected,
    diff,
    land,
    own,
    from_west,
    from_east,
    own_rows,
    from_south,
    from_north,
    upper,
    lower,
    out,
    values,
    gains,
    surface,
    fix,
    row_fix,
    out_sem,
):
    _, levels, rows, cols = cells.shape
    chunks = rows // chunk_rows
    lane = lane_of((SUB, LANES))

    def store(c, q):
        part = pl.ds(c * chunk_rows, chunk_rows)
        at = pl.ds(q * (levels // PARTS), levels // PARTS)
        return pltpu.make_async_copy(
            values.at[:, at, part, :], out.at[:, at, part, :], out_sem.at[c, q]
        )

    quads = [upper[0], upper[1], lower[0], lower[1]]
    short = rows // 8
    for pair in range(2):
        left = quads[2 * pair + 1]
        right = quads[2 * pair]
        for f in range(5):
            at = 2 * f * short
            one = left[at : at + short] + left[at + short : at + 2 * short]
            two = right[at : at + short] + right[at + short : at + 2 * short]
            for g in range(4):
                half = slice(g // 2 * LANES, g // 2 * LANES + LANES)
                a = one[:, half]
                b = two[:, half]
                if g % 2:
                    a = pltpu.roll(a, LANES // 2, 1)
                else:
                    b = pltpu.roll(b, LANES // 2, 1)
                merged = jnp.where(lane_of((short, LANES)) < LANES // 2, a, b)
                base = (1 - pair) * (rows // 2) + g * short
                surface[f, base : base + short, :] = merged
    for rb in range(rows // SUB):
        at = pl.ds(rb * SUB, SUB)
        s3 = surface[3, at, :]
        s4 = surface[4, at, :]
        surface[3, at, :] = 2.0 * jnp.sqrt(s3 * s3 + s4 * s4)

    half = levels // 2
    place_in_group = lane % 4
    spread = (2 * levels + lane // 4) % LANES
    for side in range(2):

        def mend(rb, carry):
            at = pl.ds(pl.multiple_of(rb * SUB, SUB), SUB)
            msg_at = pl.ds(pl.multiple_of(side * rows + rb * SUB, SUB), SUB)
            courant = own[4 + side, at, :]
            courant_before = pltpu.roll(courant, 1, 1)
            west_courant = jnp.take_along_axis(
                from_west[msg_at, :], spread, axis=1, mode="promise_in_bounds"
            )
            for t in range(2):
                msg_at = pl.ds(pl.multiple_of(t * rows + rb * SUB, SUB), SUB)
                west = from_west[msg_at, :]
                right = from_east[msg_at, :]
                if side:
                    west = pltpu.roll(west, LANES - 2, 1)
                    right = pltpu.roll(right, LANES - 2, 1)
                inner = own[2 * t + side, at, :]
                inner_next = pltpu.roll(inner, LANES - 1, 1)
                west_one = pltpu.roll(west, 1, 1)
                west_two = pltpu.roll(west, 2, 1)
                product = courant * right
                second = courant * (7.0 * pltpu.roll(right, 1, 1)) - product + pltpu.roll(product, 1, 1)
                third = (
                    courant_before * (7.0 * inner - inner_next)
                    - courant * west_one
                    - west_courant * (7.0 * (west_one + inner) - (west_two + inner_next))
                )
                fourth = courant_before * west_two
                change = jnp.where(
                    place_in_group < 2,
                    jnp.where(place_in_group == 0, -product, second),
                    jnp.where(place_in_group == 2, third, fourth),
                )
                fix[t, side, at, :] = change * (-1.0 / 12.0)
            return carry

        lax.fori_loop(0, rows // SUB, mend, 0, unroll=8)

    def plane(msg, p):
        return msg[p * levels : (p + 1) * levels, :]

    for t in range(2):
        inner_one = plane(own_rows, 3 + 2 * t)
        inner_two = plane(own_rows, 4 + 2 * t)
        below_two = plane(from_south, 2 * t)
        below_one = plane(from_south, 2 * t + 1)
        above_one = plane(from_north, 2 * t)
        above_two = plane(from_north, 2 * t + 1)
        first = plane(own_rows, 0) * below_one
        entering = plane(from_south, 4) * (7.0 * (below_one + inner_one) - (below_two + inner_two))
        last = plane(own_rows, 1) * above_one
        top = plane(own_rows, 2) * (7.0 * above_one - above_two)
        for p, change in enumerate((-first - entering, first, -last, top + last)):
            row_fix[t, p] = change * (-1.0 / 12.0)

    at_edge = (lane >= LANES - 2) | (lane < 2)
    sub = lax.broadcasted_iota(jnp.int32, (SUB, LANES), 0)
    blocks = chunk_rows // SUB

    def row_pair(t, k, p, at):
        one = jnp.broadcast_to(row_fix[t, p, pl.ds(k, 1), :], (SUB, LANES))
        two = jnp.broadcast_to(row_fix[t, p + 1, pl.ds(k, 1), :], (SUB, LANES))
        return jnp.where(sub == at, one, jnp.where(sub == at + 1, two, 0.0))

    def advect(t, k, base):
        side = k // half
        shift = (2 * LANES - 2 - 4 * (k % half)) % LANES
        result = []
        for i in range(blocks):
            at = pl.ds(base + i * SUB, SUB)
            edge = pltpu.roll(fix[t, side, at, :], shift, 1)
            value = advected[t, k, at, :] + jnp.where(at_edge, edge, 0.0)
            if base + i * SUB == 0:
                value = value + row_pair(t, k, 0, 0)
            if base + (i + 1) * SUB == rows:
                value = value + row_pair(t, k, 2, SUB - 2)
            result.append(value)
        return result

    for c in range(chunks):
        base = c * chunk_rows

        def forward(k, carry, last=False):
            new = []
            heat_all = advect(0, k, base)
            salt_all = advect(1, k, base)
            for i in range(blocks):
                r0 = base + i * SUB
                above, lead, heat, salt = carry[4 * i : 4 * i + 4]
                heat_in = heat_all[i] + surface[2, r0 : r0 + SUB, :] * tables[0, k]
                salt_in = salt_all[i]
                if last:
                    inverse = 1.0 / lead
                    below = above
                else:
                    below = diff[k, r0 : r0 + SUB, :] + surface[3, r0 : r0 + SUB, :] * tables[1, k]
                    pivot = lead + below
                    rough = pl.reciprocal(pivot, approx=True)
                    inverse = rough * (2.0 - pivot * rough)
                heat = (heat_in + above * heat) * inverse
                salt = (salt_in + above * salt) * inverse
                values[0, k, r0 : r0 + SUB, :] = heat
                values[1, k, r0 : r0 + SUB, :] = salt
                if not last:
                    gains[k, i * SUB : (i + 1) * SUB, :] = below * inverse
                    lead = 1.0 + below * (lead * inverse)
                new += [below, lead, heat, salt]
            return tuple(new)

        carry = []
        for i in range(blocks):
            r0 = base + i * SUB
            one = jnp.ones((SUB, LANES), F32)
            carry += [one, one, 0.5 * surface[0, r0 : r0 + SUB, :], 0.5 * surface[1, r0 : r0 + SUB, :]]
        spare = (levels - 1) % FORWARD
        carry = lax.fori_loop(0, levels - 1 - spare, forward, tuple(carry), unroll=FORWARD)
        for k in range(levels - 1 - spare, levels - 1):
            carry = forward(k, carry)
        carry = forward(levels - 1, carry, True)

        def finish(k, i, heat, salt):
            r0 = base + i * SUB
            wet = land[r0 : r0 + SUB, :] == 1
            values[0, k, r0 : r0 + SUB, :] = jnp.where(wet, heat, cells[0, k, r0 : r0 + SUB, :])
            values[1, k, r0 : r0 + SUB, :] = jnp.where(wet, salt, cells[1, k, r0 : r0 + SUB, :])

        def backward(step, carry):
            k = levels - 2 - step
            new = []
            for i in range(blocks):
                r0 = base + i * SUB
                heat, salt = carry[2 * i : 2 * i + 2]
                gain = gains[k, i * SUB : (i + 1) * SUB, :]
                heat = values[0, k, r0 : r0 + SUB, :] + gain * heat
                salt = values[1, k, r0 : r0 + SUB, :] + gain * salt
                finish(k, i, heat, salt)
                new += [heat, salt]
            return tuple(new)

        ends = []
        for i in range(blocks):
            heat, salt = carry[4 * i + 2 : 4 * i + 4]
            finish(levels - 1, i, heat, salt)
            ends += [heat, salt]
        carry = backward(0, tuple(ends))
        done = 1
        for q in reversed(range(PARTS)):
            until = levels - 1 - q * (levels // PARTS)
            while (until - done) % BACKWARD:
                carry = backward(done, carry)
                done += 1
            carry = lax.fori_loop(done, until, backward, carry, unroll=BACKWARD)
            done = until
            store(c, q).start()
    for c in range(chunks):
        for q in range(PARTS):
            store(c, q).wait()


def step(cells, advected, diff, land, messages, chunk_rows=64):
    _, levels, rows, cols = cells.shape
    depth = np.arange(levels)
    decay = np.exp(-4.0 * depth / levels)
    absorb = decay - np.exp(-4.0 * (depth + 1.0) / levels)
    tables = jnp.asarray(np.stack([0.5 * absorb, decay]), F32)
    chunks = rows // chunk_rows
    hbm = pl.BlockSpec(memory_space=pl.ANY)
    vmem = pl.BlockSpec(memory_space=pltpu.VMEM)
    return pl.pallas_call(
        functools.partial(main_kernel, chunk_rows),
        in_specs=[pl.BlockSpec(memory_space=pltpu.SMEM)] + [vmem] * (4 + len(messages)),
        out_specs=hbm,
        out_shape=jax.ShapeDtypeStruct(cells.shape, F32),
        scratch_shapes=[
            pltpu.VMEM((2, levels, rows, cols), F32),
            pltpu.VMEM((levels, chunk_rows, cols), F32),
            pltpu.VMEM((5, rows, cols), F32),
            pltpu.VMEM((2, 2, rows, cols), F32),
            pltpu.VMEM((2, 4, levels, cols), F32),
            pltpu.SemaphoreType.DMA((chunks, PARTS)),
        ],
        compiler_params=pltpu.CompilerParams(vmem_limit_bytes=16 << 20),
        name="step",
    )(tables, cells, advected, diff, land, *messages)


def ring(axis, by):
    length = lax.axis_size(axis)
    return [(i, (i + by) % length) for i in range(length)]


def diagonal():
    lats = lax.axis_size("lat")
    lons = lax.axis_size("lon")
    return [
        (i * lons + j, (i + 1) % lats * lons + (j + 1) % lons) for i in range(lats) for j in range(lons)
    ]


def local(
    tracers,
    east_courant,
    north_courant,
    diffusivity,
    land_sea,
    fluxes,
    source_cell,
    link_weight,
    target_cell,
):
    _, levels, rows, cols = tracers.shape
    target = target_cell[0]
    cells, east, own, to_east, to_west, to_north, to_south, corner, own_links, own_rows = load(
        tracers, east_courant, north_courant, fluxes, source_cell[0], link_weight[0]
    )
    from_corner = lax.ppermute(corner, ("lat", "lon"), diagonal())
    from_south = lax.ppermute(to_north, "lat", ring("lat", 1))
    from_north = lax.ppermute(to_south, "lat", ring("lat", -1))
    from_west = lax.ppermute(to_east, "lon", ring("lon", 1))
    from_east = lax.ppermute(to_west, "lon", ring("lon", -1))
    advected, diff = interior(cells, east, north_courant, diffusivity)
    upper = remap(target, [(0, own_links, 0), (1, from_west, 2 * rows)], rows, cols)
    lower = remap(target, [(2, from_south, 5 * levels), (3, from_corner, 0)], rows, cols, [upper])
    messages = (own, from_west, from_east, own_rows, from_south, from_north, upper, lower)
    return step(cells, advected, diff, land_sea, messages)


def solution(mesh):
    in_specs = (
        P(None, None, "lat", "lon"),
        P(None, "lat", "lon"),
        P(None, "lat", "lon"),
        P(None, "lat", "lon"),
        P("lat", "lon"),
        P(None, ("lat", "lon")),
        P(("lat", "lon"), None, None),
        P(("lat", "lon"), None, None),
        P(("lat", "lon"), None, None),
    )
    out_specs = P(None, None, "lat", "lon")
    return jax.shard_map(local, mesh=mesh, in_specs=in_specs, out_specs=out_specs, check_vma=False)
```

```python
import functools

import jax
import jax.numpy as jnp
import numpy as np
from jax import lax
from jax.experimental import pallas as pl
from jax.experimental.pallas import tpu as pltpu
from jax.sharding import PartitionSpec as P

F32 = jnp.float32
BF16 = jnp.bfloat16
LANES = 128
SUB = 8
TABLE_ROWS = 16
PARTS = 4
PACK = 16
LEVELS = 12
FORWARD = 16
BACKWARD = 12


def lane_of(shape):
    return lax.broadcasted_iota(jnp.int32, shape, len(shape) - 1)


def remap_rows(links):
    return 5 * TABLE_ROWS + 2 * (links // LANES)


def load_kernel(
    links,
    tracers,
    east_courant,
    north_courant,
    fluxes,
    source,
    weight,
    cells,
    east,
    own,
    east_msg,
    west_msg,
    north_msg,
    south_msg,
    corner_msg,
    own_msg,
    own_rows,
    flux_in,
    source_in,
    weight_in,
    first_north,
    last_north,
    sem,
):
    _, levels, rows, _ = tracers.shape
    lat = lax.axis_index("lat")
    has_north = (lat < lax.axis_size("lat") - 1).astype(F32)
    has_south = (lat > 0).astype(F32)
    part = levels // PARTS
    half = levels // 2
    small = [
        pltpu.make_async_copy(fluxes, flux_in, sem.at[0]),
        pltpu.make_async_copy(source, source_in, sem.at[1]),
        pltpu.make_async_copy(weight, weight_in, sem.at[2]),
        pltpu.make_async_copy(north_courant.at[:, pl.ds(rows - SUB, SUB), :], last_north, sem.at[3]),
        pltpu.make_async_copy(north_courant.at[:, pl.ds(0, SUB), :], first_north, sem.at[4 + 3 * PARTS]),
    ]
    large = []
    for q in range(PARTS):
        at = pl.ds(q * part, part)
        large.append(
            [
                pltpu.make_async_copy(tracers.at[0, at], cells.at[0, at], sem.at[4 + 3 * q]),
                pltpu.make_async_copy(tracers.at[1, at], cells.at[1, at], sem.at[5 + 3 * q]),
                pltpu.make_async_copy(east_courant.at[at], east.at[at], sem.at[6 + 3 * q]),
            ]
        )
    for copy in small:
        copy.start()
    for group in large:
        for copy in group:
            copy.start()
    for copy in small:
        copy.wait()
    quarter = fluxes.shape[1] // 4
    places = ((own_msg, 0), (east_msg, 2 * rows), (north_msg, 5 * levels), (corner_msg, 0))
    for n, (msg, base) in enumerate(places):
        for f in range(5):
            for u in range(TABLE_ROWS):
                cut = pl.ds(n * quarter + u * LANES, LANES)
                row = flux_in[f : f + 1, cut]
                if f == 1:
                    row = row + flux_in[5:6, cut]
                msg[pl.ds(base + f * TABLE_ROWS + u, 1), :] = row
        base = base + 5 * TABLE_ROWS
        for c in range(links // LANES):
            cut = pl.ds(c * LANES, LANES)
            msg[pl.ds(base + c, 1), :] = source_in[n : n + 1, cut].astype(F32)
            row = weight_in[n : n + 1, cut]
            msg[pl.ds(base + links // LANES + c, 1), :] = row * has_north if n >= 2 else row
    for k in range(levels):
        north_msg[pl.ds(4 * levels + k, 1), :] = last_north[k, SUB - 1 : SUB, :] * has_north
        own_rows[pl.ds(k, 1), :] = first_north[k, 0:1, :]
        own_rows[pl.ds(levels + k, 1), :] = last_north[k, SUB - 2 : SUB - 1, :]
        own_rows[pl.ds(2 * levels + k, 1), :] = last_north[k, SUB - 1 : SUB, :]

    lane = lane_of((SUB, LANES))
    group = lane // 4
    for q in range(PARTS):
        for copy in large[q]:
            copy.wait()
        side = q * part // half
        offset = q * part % half

        def pack(rb, carry):
            at = pl.ds(pl.multiple_of(rb * SUB, SUB), SUB)
            for slot, ref in ((side, cells.at[0]), (2 + side, cells.at[1]), (4 + side, east)):
                packed = own[slot, at, :] if offset else jnp.zeros((SUB, LANES), F32)
                for j in range(part):
                    moved = pltpu.roll(ref[q * part + j, at, :], 4 * (offset + j) + 2, 1)
                    packed = jnp.where(group == offset + j, moved, packed)
                own[slot, at, :] = packed
            return carry

        lax.fori_loop(0, rows // SUB, pack, 0, unroll=PACK)
        for t in range(2):
            for k in range(q * part, (q + 1) * part):
                for j in range(2):
                    at = pl.ds((2 * t + j) * levels + k, 1)
                    low = cells[t, k, j : j + 1, :]
                    high = cells[t, k, rows - 2 + j : rows - 1 + j, :]
                    south_msg[at, :] = low * has_south
                    north_msg[at, :] = high * has_north
                    own_rows[pl.ds((3 + 2 * t + j) * levels + k, 1), :] = low

    early = lane % 4 < 2
    spare = lane >= 2 * levels
    last_column = (4 * lane + 1) % LANES

    def messages(rb, carry):
        at = pl.ds(pl.multiple_of(rb * SUB, SUB), SUB)
        for t in range(2):
            first = own[2 * t, at, :]
            second = own[2 * t + 1, at, :]
            courant = jnp.take_along_axis(own[4 + t, at, :], last_column, axis=1, mode="promise_in_bounds")
            tails = jnp.where(early, first, pltpu.roll(second, 2, 1))
            place = pl.ds(pl.multiple_of(t * rows + rb * SUB, SUB), SUB)
            east_msg[place, :] = jnp.where(spare, courant, tails)
            west_msg[place, :] = jnp.where(early, pltpu.roll(first, LANES - 2, 1), second)
        return carry

    lax.fori_loop(0, rows // SUB, messages, 0, unroll=4)


def in_hbm(*arrays):
    return [pltpu.with_memory_space_constraint(a, pltpu.HBM) for a in arrays]


def load(tracers, east_courant, north_courant, fluxes, source, weight):
    _, levels, rows, cols = tracers.shape
    links = source.shape[1]
    remap = remap_rows(links)
    hbm = pl.BlockSpec(memory_space=pltpu.HBM)
    vmem = pl.BlockSpec(memory_space=pltpu.VMEM)
    shapes = [
        tracers.shape,
        east_courant.shape,
        (6, rows, cols),
        (2 * rows + remap, LANES),
        (2 * rows, LANES),
        (5 * levels + remap, LANES),
        (4 * levels, LANES),
        (remap, LANES),
        (remap, LANES),
        (7 * levels, LANES),
    ]
    return pl.pallas_call(
        functools.partial(load_kernel, links),
        in_specs=[hbm] * 6,
        out_specs=[vmem] * len(shapes),
        out_shape=[pltpu.VMEM(shape, F32) for shape in shapes],
        scratch_shapes=[
            pltpu.VMEM(fluxes.shape, F32),
            pltpu.VMEM(source.shape, jnp.int32),
            pltpu.VMEM(weight.shape, F32),
            pltpu.VMEM((levels, SUB, cols), F32),
            pltpu.VMEM((levels, SUB, cols), F32),
            pltpu.SemaphoreType.DMA((5 + 3 * PARTS,)),
        ],
        compiler_params=pltpu.CompilerParams(vmem_limit_bytes=16 << 20),
        name="load",
    )(*in_hbm(tracers, east_courant, north_courant, fluxes, source, weight))


def stencil_weights(cols):
    i = lax.broadcasted_iota(jnp.int32, (2 * cols, 2 * cols), 0) % cols
    j = lax.broadcasted_iota(jnp.int32, (2 * cols, 2 * cols), 1)
    face = j % cols - j // cols
    gap = i - face
    near = (gap == 0) | (gap == 1)
    far = (gap == -1) | (gap == 2)
    return jnp.where(near, 7.0, jnp.where(far, -1.0, 0.0)).astype(BF16)


def interior_kernel(
    cells,
    east,
    north_courant,
    diffusivity,
    advected,
    diff,
    weights,
    north,
    sem,
):
    _, levels, rows, cols = cells.shape
    weights[...] = stencil_weights(cols)
    part = levels // PARTS
    sub = lax.broadcasted_iota(jnp.int32, (SUB, LANES), 0)
    blocks = rows // SUB
    copies = []
    for q in range(PARTS):
        at = pl.ds(q * part, part)
        copies.append(pltpu.make_async_copy(north_courant.at[at], north.at[at], sem.at[q]))
    last = pltpu.make_async_copy(diffusivity, diff, sem.at[PARTS])
    for copy in copies:
        copy.start()
    last.start()

    def level(k, carry):
        west_courant = [pltpu.roll(east[k, i * SUB : (i + 1) * SUB, :], 1, 1) for i in range(blocks)]
        for t in range(2):
            whole = cells[t, k]
            high = whole.astype(BF16)
            low = (whole - high.astype(F32)).astype(BF16)
            faces = jnp.dot(
                jnp.concatenate([high, low], 1), weights[...], preferred_element_type=F32
            )
            south = jnp.zeros((SUB, LANES), F32)
            for i in range(blocks):
                r0 = i * SUB
                here = cells[t, k, r0 : r0 + SUB, :]
                east_flux = east[k, r0 : r0 + SUB, :] * faces[r0 : r0 + SUB, :cols]
                west_flux = west_courant[i] * faces[r0 : r0 + SUB, cols:]
                if i == 0:
                    low_one = jnp.where(sub == 0, 0.0, pltpu.roll(here, 1, 0))
                else:
                    low_one = cells[t, k, r0 - 1 : r0 - 1 + SUB, :]
                if i == blocks - 1:
                    up_one = jnp.where(sub == SUB - 1, 0.0, pltpu.roll(here, SUB - 1, 0))
                    up_two = jnp.where(sub >= SUB - 2, 0.0, pltpu.roll(here, SUB - 2, 0))
                else:
                    up_one = cells[t, k, r0 + 1 : r0 + 1 + SUB, :]
                    up_two = cells[t, k, r0 + 2 : r0 + 2 + SUB, :]
                face = 7.0 * (here + up_one) - (low_one + up_two)
                north_flux = north[k, r0 : r0 + SUB, :] * face
                moved = pltpu.roll(north_flux, 1, 0)
                south_flux = jnp.where(sub == 0, south, moved)
                south = moved
                change = (east_flux - west_flux) + (north_flux - south_flux)
                advected[t, k, r0 : r0 + SUB, :] = here - change * (1.0 / 12.0)
        return carry

    for q in range(PARTS):
        copies[q].wait()
        lax.fori_loop(q * part, (q + 1) * part, level, 0, unroll=LEVELS)
    last.wait()


def interior(cells, east, north_courant, diffusivity):
    _, levels, rows, cols = cells.shape
    hbm = pl.BlockSpec(memory_space=pltpu.HBM)
    vmem = pl.BlockSpec(memory_space=pltpu.VMEM)
    return pl.pallas_call(
        interior_kernel,
        in_specs=[vmem] * 2 + [hbm] * 2,
        out_specs=[vmem] * 2,
        out_shape=[pltpu.VMEM(cells.shape, F32), pltpu.VMEM(diffusivity.shape, F32)],
        scratch_shapes=[
            pltpu.VMEM((2 * cols, 2 * cols), BF16),
            pltpu.VMEM(north_courant.shape, F32),
            pltpu.SemaphoreType.DMA((PARTS + 1,)),
        ],
        compiler_params=pltpu.CompilerParams(vmem_limit_bytes=16 << 20),
        name="interior",
    )(cells, east, *in_hbm(north_courant, diffusivity))


def gather_links(msg, base, n, links, picked):
    rows = links // LANES
    for g in range(rows // SUB):
        cells = msg[pl.ds(base + 5 * TABLE_ROWS + g * SUB, SUB), :].astype(jnp.int32)
        weights = msg[pl.ds(base + 5 * TABLE_ROWS + rows + g * SUB, SUB), :]
        low = cells % LANES
        high = (cells // LANES) % TABLE_ROWS
        for f in range(5):
            total = jnp.zeros((SUB, LANES), F32)
            for u in range(TABLE_ROWS):
                row = jnp.broadcast_to(msg[pl.ds(base + f * TABLE_ROWS + u, 1), :], (SUB, LANES))
                found = jnp.take_along_axis(row, low, axis=1, mode="promise_in_bounds")
                total = jnp.where(high == u, found, total)
            picked[f, pl.ds(n * rows + g * SUB, SUB), :] = total * weights


def scatter_links(picked, target, n, links, rows, cols):
    half_rows = rows // 2
    half_cols = cols // 2
    count = links // LANES
    wide = 4 * half_cols
    short = half_rows // 4
    tall_iota = lax.broadcasted_iota(jnp.int32, (wide, LANES), 0).astype(jnp.int16)
    short_iota = lax.broadcasted_iota(jnp.int32, (short, LANES), 0)
    ones = jnp.ones((wide, LANES), BF16)
    total = jnp.zeros((wide, 10 * short), F32)
    group = count
    for g in range(count // group):
        lefts = []
        rights = []
        for c in range(g * group, (g + 1) * group):
            cell = target[n : n + 1, c * LANES : (c + 1) * LANES]
            row = cell // cols - (1 - n // 2) * half_rows
            col = cell % cols - (1 - n % 2) * half_cols
            short_at = jnp.broadcast_to(row % short, (short, LANES)) == short_iota
            place = (row // short * half_cols + col).astype(jnp.int16)
            wide_at = jnp.broadcast_to(place, (wide, LANES)) == tall_iota
            rights.append(jnp.where(wide_at, ones, jnp.zeros_like(ones)))
            pieces = []
            for f in range(5):
                value = picked[f, pl.ds(n * count + c, 1), :]
                high = value.astype(BF16).astype(F32)
                low = value - high
                for part in (high, low):
                    spread = jnp.broadcast_to(part, (short, LANES))
                    pieces.append(jnp.where(short_at, spread, 0.0).astype(BF16))
            lefts.append(jnp.concatenate(pieces, 0))
        left = jnp.concatenate(lefts, 1)
        right = jnp.concatenate(rights, 1)
        total = total + lax.dot_general(
            right, left, (((1,), (1,)), ((), ())), preferred_element_type=F32
        )
    return total.T


def remap_kernel(links, rows, cols, numbers, bases, target, *refs):
    count = len(numbers)
    quads, picked = refs[-2:]
    for i, (n, base) in enumerate(zip(numbers, bases)):
        gather_links(refs[i], base, n, links, picked)
        quads[i] = scatter_links(picked, target, n, links, rows, cols)


def remap(target, blocks, rows, cols, after=()):
    links = target.shape[1]
    numbers = tuple(n for n, _, _ in blocks)
    bases = tuple(base for _, _, base in blocks)
    vmem = pl.BlockSpec(memory_space=pltpu.VMEM)
    return pl.pallas_call(
        functools.partial(remap_kernel, links, rows, cols, numbers, bases),
        in_specs=[vmem] * (1 + len(blocks)) + [pl.BlockSpec(memory_space=pl.ANY)] * len(after),
        out_specs=vmem,
        out_shape=jax.ShapeDtypeStruct((len(blocks), 10 * rows // 8, 2 * cols), F32),
        scratch_shapes=[pltpu.VMEM((5, 4 * links // LANES, LANES), F32)],
        compiler_params=pltpu.CompilerParams(vmem_limit_bytes=16 << 20),
        name="remap",
    )(target, *[msg for _, msg, _ in blocks], *after)


def column_kernel(levels, own, from_west, from_east, fix):
    _, rows, _ = own.shape
    lane = lane_of((SUB, LANES))
    place_in_group = lane % 4
    spread = (2 * levels + lane // 4) % LANES
    for side in range(2):

        def mend(rb, carry):
            at = pl.ds(pl.multiple_of(rb * SUB, SUB), SUB)
            msg_at = pl.ds(pl.multiple_of(side * rows + rb * SUB, SUB), SUB)
            courant = own[4 + side, at, :]
            courant_before = pltpu.roll(courant, 1, 1)
            west_courant = jnp.take_along_axis(
                from_west[msg_at, :], spread, axis=1, mode="promise_in_bounds"
            )
            for t in range(2):
                msg_at = pl.ds(pl.multiple_of(t * rows + rb * SUB, SUB), SUB)
                west = from_west[msg_at, :]
                right = from_east[msg_at, :]
                if side:
                    west = pltpu.roll(west, LANES - 2, 1)
                    right = pltpu.roll(right, LANES - 2, 1)
                inner = own[2 * t + side, at, :]
                inner_next = pltpu.roll(inner, LANES - 1, 1)
                west_one = pltpu.roll(west, 1, 1)
                west_two = pltpu.roll(west, 2, 1)
                product = courant * right
                second = courant * (7.0 * pltpu.roll(right, 1, 1)) - product + pltpu.roll(product, 1, 1)
                third = (
                    courant_before * (7.0 * inner - inner_next)
                    - courant * west_one
                    - west_courant * (7.0 * (west_one + inner) - (west_two + inner_next))
                )
                fourth = courant_before * west_two
                change = jnp.where(
                    place_in_group < 2,
                    jnp.where(place_in_group == 0, -product, second),
                    jnp.where(place_in_group == 2, third, fourth),
                )
                fix[t, side, at, :] = change * (-1.0 / 12.0)
            return carry

        lax.fori_loop(0, rows // SUB, mend, 0, unroll=8)


def column_fix(levels, own, from_west, from_east):
    _, rows, cols = own.shape
    vmem = pl.BlockSpec(memory_space=pltpu.VMEM)
    return pl.pallas_call(
        functools.partial(column_kernel, levels),
        in_specs=[vmem] * 3,
        out_specs=vmem,
        out_shape=pltpu.VMEM((2, 2, rows, cols), F32),
        compiler_params=pltpu.CompilerParams(vmem_limit_bytes=16 << 20),
        name="column_fix",
    )(own, from_west, from_east)


def main_kernel(
    chunk_rows,
    tables,
    cells,
    advected,
    diff,
    land,
    fix,
    own_rows,
    from_south,
    from_north,
    upper,
    lower,
    out,
    values,
    gains,
    surface,
    row_fix,
    out_sem,
):
    _, levels, rows, cols = cells.shape
    chunks = rows // chunk_rows
    lane = lane_of((SUB, LANES))

    def store(c, q):
        part = pl.ds(c * chunk_rows, chunk_rows)
        at = pl.ds(q * (levels // PARTS), levels // PARTS)
        return pltpu.make_async_copy(
            values.at[:, at, part, :], out.at[:, at, part, :], out_sem.at[c, q]
        )

    quads = [upper[0], upper[1], lower[0], lower[1]]
    short = rows // 8
    for pair in range(2):
        left = quads[2 * pair + 1]
        right = quads[2 * pair]
        for f in range(5):
            at = 2 * f * short
            one = left[at : at + short] + left[at + short : at + 2 * short]
            two = right[at : at + short] + right[at + short : at + 2 * short]
            for g in range(4):
                half = slice(g // 2 * LANES, g // 2 * LANES + LANES)
                a = one[:, half]
                b = two[:, half]
                if g % 2:
                    a = pltpu.roll(a, LANES // 2, 1)
                else:
                    b = pltpu.roll(b, LANES // 2, 1)
                merged = jnp.where(lane_of((short, LANES)) < LANES // 2, a, b)
                base = (1 - pair) * (rows // 2) + g * short
                surface[f, base : base + short, :] = merged
    for rb in range(rows // SUB):
        at = pl.ds(rb * SUB, SUB)
        s3 = surface[3, at, :]
        s4 = surface[4, at, :]
        surface[3, at, :] = 2.0 * jnp.sqrt(s3 * s3 + s4 * s4)

    half = levels // 2

    def plane(msg, p):
        return msg[p * levels : (p + 1) * levels, :]

    for t in range(2):
        inner_one = plane(own_rows, 3 + 2 * t)
        inner_two = plane(own_rows, 4 + 2 * t)
        below_two = plane(from_south, 2 * t)
        below_one = plane(from_south, 2 * t + 1)
        above_one = plane(from_north, 2 * t)
        above_two = plane(from_north, 2 * t + 1)
        first = plane(own_rows, 0) * below_one
        entering = plane(from_south, 4) * (7.0 * (below_one + inner_one) - (below_two + inner_two))
        last = plane(own_rows, 1) * above_one
        top = plane(own_rows, 2) * (7.0 * above_one - above_two)
        for p, change in enumerate((-first - entering, first, -last, top + last)):
            row_fix[t, p] = change * (-1.0 / 12.0)

    at_edge = (lane >= LANES - 2) | (lane < 2)
    sub = lax.broadcasted_iota(jnp.int32, (SUB, LANES), 0)
    blocks = chunk_rows // SUB

    def row_pair(t, k, p, at):
        one = jnp.broadcast_to(row_fix[t, p, pl.ds(k, 1), :], (SUB, LANES))
        two = jnp.broadcast_to(row_fix[t, p + 1, pl.ds(k, 1), :], (SUB, LANES))
        return jnp.where(sub == at, one, jnp.where(sub == at + 1, two, 0.0))

    def advect(t, k, base):
        side = k // half
        shift = (2 * LANES - 2 - 4 * (k % half)) % LANES
        result = []
        for i in range(blocks):
            at = pl.ds(base + i * SUB, SUB)
            edge = pltpu.roll(fix[t, side, at, :], shift, 1)
            value = advected[t, k, at, :] + jnp.where(at_edge, edge, 0.0)
            if base + i * SUB == 0:
                value = value + row_pair(t, k, 0, 0)
            if base + (i + 1) * SUB == rows:
                value = value + row_pair(t, k, 2, SUB - 2)
            result.append(value)
        return result

    for c in range(chunks):
        base = c * chunk_rows

        def forward(k, carry, last=False):
            new = []
            heat_all = advect(0, k, base)
            salt_all = advect(1, k, base)
            for i in range(blocks):
                r0 = base + i * SUB
                above, lead, heat, salt = carry[4 * i : 4 * i + 4]
                heat_in = heat_all[i] + surface[2, r0 : r0 + SUB, :] * tables[0, k]
                salt_in = salt_all[i]
                if last:
                    inverse = 1.0 / lead
                    below = above
                else:
                    below = diff[k, r0 : r0 + SUB, :] + surface[3, r0 : r0 + SUB, :] * tables[1, k]
                    pivot = lead + below
                    rough = pl.reciprocal(pivot, approx=True)
                    inverse = rough * (2.0 - pivot * rough)
                heat = (heat_in + above * heat) * inverse
                salt = (salt_in + above * salt) * inverse
                values[0, k, r0 : r0 + SUB, :] = heat
                values[1, k, r0 : r0 + SUB, :] = salt
                if not last:
                    gains[k, i * SUB : (i + 1) * SUB, :] = below * inverse
                    lead = 1.0 + below * (lead * inverse)
                new += [below, lead, heat, salt]
            return tuple(new)

        carry = []
        for i in range(blocks):
            r0 = base + i * SUB
            one = jnp.ones((SUB, LANES), F32)
            carry += [one, one, 0.5 * surface[0, r0 : r0 + SUB, :], 0.5 * surface[1, r0 : r0 + SUB, :]]
        spare = (levels - 1) % FORWARD
        carry = lax.fori_loop(0, levels - 1 - spare, forward, tuple(carry), unroll=FORWARD)
        for k in range(levels - 1 - spare, levels - 1):
            carry = forward(k, carry)
        carry = forward(levels - 1, carry, True)

        def finish(k, i, heat, salt):
            r0 = base + i * SUB
            wet = land[r0 : r0 + SUB, :] == 1
            values[0, k, r0 : r0 + SUB, :] = jnp.where(wet, heat, cells[0, k, r0 : r0 + SUB, :])
            values[1, k, r0 : r0 + SUB, :] = jnp.where(wet, salt, cells[1, k, r0 : r0 + SUB, :])

        def backward(step, carry):
            k = levels - 2 - step
            new = []
            for i in range(blocks):
                r0 = base + i * SUB
                heat, salt = carry[2 * i : 2 * i + 2]
                gain = gains[k, i * SUB : (i + 1) * SUB, :]
                heat = values[0, k, r0 : r0 + SUB, :] + gain * heat
                salt = values[1, k, r0 : r0 + SUB, :] + gain * salt
                finish(k, i, heat, salt)
                new += [heat, salt]
            return tuple(new)

        ends = []
        for i in range(blocks):
            heat, salt = carry[4 * i + 2 : 4 * i + 4]
            finish(levels - 1, i, heat, salt)
            ends += [heat, salt]
        carry = backward(0, tuple(ends))
        done = 1
        for q in reversed(range(PARTS)):
            until = levels - 1 - q * (levels // PARTS)
            while (until - done) % BACKWARD:
                carry = backward(done, carry)
                done += 1
            carry = lax.fori_loop(done, until, backward, carry, unroll=BACKWARD)
            done = until
            store(c, q).start()
    for c in range(chunks):
        for q in range(PARTS):
            store(c, q).wait()


def step(cells, advected, diff, land, messages, chunk_rows=64):
    _, levels, rows, cols = cells.shape
    depth = np.arange(levels)
    decay = np.exp(-4.0 * depth / levels)
    absorb = decay - np.exp(-4.0 * (depth + 1.0) / levels)
    tables = jnp.asarray(np.stack([0.5 * absorb, decay]), F32)
    chunks = rows // chunk_rows
    hbm = pl.BlockSpec(memory_space=pl.ANY)
    vmem = pl.BlockSpec(memory_space=pltpu.VMEM)
    return pl.pallas_call(
        functools.partial(main_kernel, chunk_rows),
        in_specs=[pl.BlockSpec(memory_space=pltpu.SMEM)] + [vmem] * (4 + len(messages)),
        out_specs=hbm,
        out_shape=jax.ShapeDtypeStruct(cells.shape, F32),
        scratch_shapes=[
            pltpu.VMEM((2, levels, rows, cols), F32),
            pltpu.VMEM((levels, chunk_rows, cols), F32),
            pltpu.VMEM((5, rows, cols), F32),
            pltpu.VMEM((2, 4, levels, cols), F32),
            pltpu.SemaphoreType.DMA((chunks, PARTS)),
        ],
        compiler_params=pltpu.CompilerParams(vmem_limit_bytes=16 << 20),
        name="step",
    )(tables, cells, advected, diff, land, *messages)


def ring(axis, by):
    length = lax.axis_size(axis)
    return [(i, (i + by) % length) for i in range(length)]


def diagonal():
    lats = lax.axis_size("lat")
    lons = lax.axis_size("lon")
    return [
        (i * lons + j, (i + 1) % lats * lons + (j + 1) % lons) for i in range(lats) for j in range(lons)
    ]


def local(
    tracers,
    east_courant,
    north_courant,
    diffusivity,
    land_sea,
    fluxes,
    source_cell,
    link_weight,
    target_cell,
):
    _, levels, rows, cols = tracers.shape
    target = target_cell[0]
    cells, east, own, to_east, to_west, to_north, to_south, corner, own_links, own_rows = load(
        tracers, east_courant, north_courant, fluxes, source_cell[0], link_weight[0]
    )
    from_corner = lax.ppermute(corner, ("lat", "lon"), diagonal())
    from_south = lax.ppermute(to_north, "lat", ring("lat", 1))
    from_north = lax.ppermute(to_south, "lat", ring("lat", -1))
    from_west = lax.ppermute(to_east, "lon", ring("lon", 1))
    from_east = lax.ppermute(to_west, "lon", ring("lon", -1))
    advected, diff = interior(cells, east, north_courant, diffusivity)
    upper = remap(target, [(0, own_links, 0), (1, from_west, 2 * rows)], rows, cols)
    fix = column_fix(levels, own, from_west, from_east)
    lower = remap(target, [(2, from_south, 5 * levels), (3, from_corner, 0)], rows, cols, [upper, fix])
    messages = (fix, own_rows, from_south, from_north, upper, lower)
    return step(cells, advected, diff, land_sea, messages)


def solution(mesh):
    in_specs = (
        P(None, None, "lat", "lon"),
        P(None, "lat", "lon"),
        P(None, "lat", "lon"),
        P(None, "lat", "lon"),
        P("lat", "lon"),
        P(None, ("lat", "lon")),
        P(("lat", "lon"), None, None),
        P(("lat", "lon"), None, None),
        P(("lat", "lon"), None, None),
    )
    out_specs = P(None, None, "lat", "lon")
    return jax.shard_map(local, mesh=mesh, in_specs=in_specs, out_specs=out_specs, check_vma=False)
```

```python
import functools

import jax
import jax.numpy as jnp
import numpy as np
from jax import lax
from jax.experimental import pallas as pl
from jax.experimental.pallas import tpu as pltpu
from jax.sharding import PartitionSpec as P

F32 = jnp.float32
BF16 = jnp.bfloat16
LANES = 128
SUB = 8
TABLE_ROWS = 16
PARTS = 4
PACK = 16
LEVELS = 12
FORWARD = 16
BACKWARD = 12


def lane_of(shape):
    return lax.broadcasted_iota(jnp.int32, shape, len(shape) - 1)


def remap_rows(links):
    return 5 * TABLE_ROWS + 2 * (links // LANES)


def load_kernel(
    links,
    tracers,
    east_courant,
    north_courant,
    fluxes,
    source,
    weight,
    cells,
    east,
    own,
    east_msg,
    west_msg,
    north_msg,
    south_msg,
    corner_msg,
    own_msg,
    own_rows,
    flux_in,
    source_in,
    weight_in,
    first_north,
    last_north,
    sem,
):
    _, levels, rows, _ = tracers.shape
    lat = lax.axis_index("lat")
    has_north = (lat < lax.axis_size("lat") - 1).astype(F32)
    has_south = (lat > 0).astype(F32)
    part = levels // PARTS
    half = levels // 2
    small = [
        pltpu.make_async_copy(fluxes, flux_in, sem.at[0]),
        pltpu.make_async_copy(source, source_in, sem.at[1]),
        pltpu.make_async_copy(weight, weight_in, sem.at[2]),
        pltpu.make_async_copy(north_courant.at[:, pl.ds(rows - SUB, SUB), :], last_north, sem.at[3]),
        pltpu.make_async_copy(north_courant.at[:, pl.ds(0, SUB), :], first_north, sem.at[4 + 3 * PARTS]),
    ]
    large = []
    for q in range(PARTS):
        at = pl.ds(q * part, part)
        large.append(
            [
                pltpu.make_async_copy(tracers.at[0, at], cells.at[0, at], sem.at[4 + 3 * q]),
                pltpu.make_async_copy(tracers.at[1, at], cells.at[1, at], sem.at[5 + 3 * q]),
                pltpu.make_async_copy(east_courant.at[at], east.at[at], sem.at[6 + 3 * q]),
            ]
        )
    for copy in small:
        copy.start()
    for group in large:
        for copy in group:
            copy.start()
    for copy in small:
        copy.wait()
    quarter = fluxes.shape[1] // 4
    places = ((own_msg, 0), (east_msg, 2 * rows), (north_msg, 5 * levels), (corner_msg, 0))
    for n, (msg, base) in enumerate(places):
        for f in range(5):
            for u in range(TABLE_ROWS):
                cut = pl.ds(n * quarter + u * LANES, LANES)
                row = flux_in[f : f + 1, cut]
                if f == 1:
                    row = row + flux_in[5:6, cut]
                msg[pl.ds(base + f * TABLE_ROWS + u, 1), :] = row
        base = base + 5 * TABLE_ROWS
        for c in range(links // LANES):
            cut = pl.ds(c * LANES, LANES)
            msg[pl.ds(base + c, 1), :] = source_in[n : n + 1, cut].astype(F32)
            row = weight_in[n : n + 1, cut]
            msg[pl.ds(base + links // LANES + c, 1), :] = row * has_north if n >= 2 else row
    for k in range(levels):
        north_msg[pl.ds(4 * levels + k, 1), :] = last_north[k, SUB - 1 : SUB, :] * has_north
        own_rows[pl.ds(k, 1), :] = first_north[k, 0:1, :]
        own_rows[pl.ds(levels + k, 1), :] = last_north[k, SUB - 2 : SUB - 1, :]
        own_rows[pl.ds(2 * levels + k, 1), :] = last_north[k, SUB - 1 : SUB, :]

    lane = lane_of((SUB, LANES))
    group = lane // 4
    for q in range(PARTS):
        for copy in large[q]:
            copy.wait()
        side = q * part // half
        offset = q * part % half

        def pack(rb, carry):
            at = pl.ds(pl.multiple_of(rb * SUB, SUB), SUB)
            for slot, ref in ((side, cells.at[0]), (2 + side, cells.at[1]), (4 + side, east)):
                packed = own[slot, at, :] if offset else jnp.zeros((SUB, LANES), F32)
                for j in range(part):
                    moved = pltpu.roll(ref[q * part + j, at, :], 4 * (offset + j) + 2, 1)
                    packed = jnp.where(group == offset + j, moved, packed)
                own[slot, at, :] = packed
            return carry

        lax.fori_loop(0, rows // SUB, pack, 0, unroll=PACK)
        for t in range(2):
            for k in range(q * part, (q + 1) * part):
                for j in range(2):
                    at = pl.ds((2 * t + j) * levels + k, 1)
                    low = cells[t, k, j : j + 1, :]
                    high = cells[t, k, rows - 2 + j : rows - 1 + j, :]
                    south_msg[at, :] = low * has_south
                    north_msg[at, :] = high * has_north
                    own_rows[pl.ds((3 + 2 * t + j) * levels + k, 1), :] = low

    early = lane % 4 < 2
    spare = lane >= 2 * levels
    last_column = (4 * lane + 1) % LANES

    def messages(rb, carry):
        at = pl.ds(pl.multiple_of(rb * SUB, SUB), SUB)
        for t in range(2):
            first = own[2 * t, at, :]
            second = own[2 * t + 1, at, :]
            courant = jnp.take_along_axis(own[4 + t, at, :], last_column, axis=1, mode="promise_in_bounds")
            tails = jnp.where(early, first, pltpu.roll(second, 2, 1))
            place = pl.ds(pl.multiple_of(t * rows + rb * SUB, SUB), SUB)
            east_msg[place, :] = jnp.where(spare, courant, tails)
            west_msg[place, :] = jnp.where(early, pltpu.roll(first, LANES - 2, 1), second)
        return carry

    lax.fori_loop(0, rows // SUB, messages, 0, unroll=8)


def in_hbm(*arrays):
    return [pltpu.with_memory_space_constraint(a, pltpu.HBM) for a in arrays]


def load(tracers, east_courant, north_courant, fluxes, source, weight):
    _, levels, rows, cols = tracers.shape
    links = source.shape[1]
    remap = remap_rows(links)
    hbm = pl.BlockSpec(memory_space=pltpu.HBM)
    vmem = pl.BlockSpec(memory_space=pltpu.VMEM)
    shapes = [
        tracers.shape,
        east_courant.shape,
        (6, rows, cols),
        (2 * rows + remap, LANES),
        (2 * rows, LANES),
        (5 * levels + remap, LANES),
        (4 * levels, LANES),
        (remap, LANES),
        (remap, LANES),
        (7 * levels, LANES),
    ]
    return pl.pallas_call(
        functools.partial(load_kernel, links),
        in_specs=[hbm] * 6,
        out_specs=[vmem] * len(shapes),
        out_shape=[pltpu.VMEM(shape, F32) for shape in shapes],
        scratch_shapes=[
            pltpu.VMEM(fluxes.shape, F32),
            pltpu.VMEM(source.shape, jnp.int32),
            pltpu.VMEM(weight.shape, F32),
            pltpu.VMEM((levels, SUB, cols), F32),
            pltpu.VMEM((levels, SUB, cols), F32),
            pltpu.SemaphoreType.DMA((5 + 3 * PARTS,)),
        ],
        compiler_params=pltpu.CompilerParams(vmem_limit_bytes=16 << 20),
        name="load",
    )(*in_hbm(tracers, east_courant, north_courant, fluxes, source, weight))


def stencil_weights(cols):
    i = lax.broadcasted_iota(jnp.int32, (2 * cols, 2 * cols), 0) % cols
    j = lax.broadcasted_iota(jnp.int32, (2 * cols, 2 * cols), 1)
    face = j % cols - j // cols
    gap = i - face
    near = (gap == 0) | (gap == 1)
    far = (gap == -1) | (gap == 2)
    return jnp.where(near, 7.0, jnp.where(far, -1.0, 0.0)).astype(BF16)


def interior_kernel(
    cells,
    east,
    north_courant,
    diffusivity,
    advected,
    diff,
    weights,
    north,
    sem,
):
    _, levels, rows, cols = cells.shape
    weights[...] = stencil_weights(cols)
    part = levels // PARTS
    sub = lax.broadcasted_iota(jnp.int32, (SUB, LANES), 0)
    blocks = rows // SUB
    copies = []
    for q in range(PARTS):
        at = pl.ds(q * part, part)
        copies.append(pltpu.make_async_copy(north_courant.at[at], north.at[at], sem.at[q]))
    last = pltpu.make_async_copy(diffusivity, diff, sem.at[PARTS])
    for copy in copies:
        copy.start()
    last.start()

    def level(k, carry):
        west_courant = [pltpu.roll(east[k, i * SUB : (i + 1) * SUB, :], 1, 1) for i in range(blocks)]
        for t in range(2):
            whole = cells[t, k]
            high = whole.astype(BF16)
            low = (whole - high.astype(F32)).astype(BF16)
            faces = jnp.dot(
                jnp.concatenate([high, low], 1), weights[...], preferred_element_type=F32
            )
            south = jnp.zeros((SUB, LANES), F32)
            for i in range(blocks):
                r0 = i * SUB
                here = cells[t, k, r0 : r0 + SUB, :]
                east_flux = east[k, r0 : r0 + SUB, :] * faces[r0 : r0 + SUB, :cols]
                west_flux = west_courant[i] * faces[r0 : r0 + SUB, cols:]
                if i == 0:
                    low_one = jnp.where(sub == 0, 0.0, pltpu.roll(here, 1, 0))
                else:
                    low_one = cells[t, k, r0 - 1 : r0 - 1 + SUB, :]
                if i == blocks - 1:
                    up_one = jnp.where(sub == SUB - 1, 0.0, pltpu.roll(here, SUB - 1, 0))
                    up_two = jnp.where(sub >= SUB - 2, 0.0, pltpu.roll(here, SUB - 2, 0))
                else:
                    up_one = cells[t, k, r0 + 1 : r0 + 1 + SUB, :]
                    up_two = cells[t, k, r0 + 2 : r0 + 2 + SUB, :]
                face = 7.0 * (here + up_one) - (low_one + up_two)
                north_flux = north[k, r0 : r0 + SUB, :] * face
                moved = pltpu.roll(north_flux, 1, 0)
                south_flux = jnp.where(sub == 0, south, moved)
                south = moved
                change = (east_flux - west_flux) + (north_flux - south_flux)
                advected[t, k, r0 : r0 + SUB, :] = here - change * (1.0 / 12.0)
        return carry

    for q in range(PARTS):
        copies[q].wait()
        lax.fori_loop(q * part, (q + 1) * part, level, 0, unroll=LEVELS)
    last.wait()


def interior(cells, east, north_courant, diffusivity):
    _, levels, rows, cols = cells.shape
    hbm = pl.BlockSpec(memory_space=pltpu.HBM)
    vmem = pl.BlockSpec(memory_space=pltpu.VMEM)
    return pl.pallas_call(
        interior_kernel,
        in_specs=[vmem] * 2 + [hbm] * 2,
        out_specs=[vmem] * 2,
        out_shape=[pltpu.VMEM(cells.shape, F32), pltpu.VMEM(diffusivity.shape, F32)],
        scratch_shapes=[
            pltpu.VMEM((2 * cols, 2 * cols), BF16),
            pltpu.VMEM(north_courant.shape, F32),
            pltpu.SemaphoreType.DMA((PARTS + 1,)),
        ],
        compiler_params=pltpu.CompilerParams(vmem_limit_bytes=16 << 20),
        name="interior",
    )(cells, east, *in_hbm(north_courant, diffusivity))


def gather_links(msg, base, n, links, picked):
    rows = links // LANES
    for g in range(rows // SUB):
        cells = msg[pl.ds(base + 5 * TABLE_ROWS + g * SUB, SUB), :].astype(jnp.int32)
        weights = msg[pl.ds(base + 5 * TABLE_ROWS + rows + g * SUB, SUB), :]
        low = cells % LANES
        high = (cells // LANES) % TABLE_ROWS
        for f in range(5):
            total = jnp.zeros((SUB, LANES), F32)
            for u in range(TABLE_ROWS):
                row = jnp.broadcast_to(msg[pl.ds(base + f * TABLE_ROWS + u, 1), :], (SUB, LANES))
                found = jnp.take_along_axis(row, low, axis=1, mode="promise_in_bounds")
                total = jnp.where(high == u, found, total)
            picked[f, pl.ds(n * rows + g * SUB, SUB), :] = total * weights


def scatter_links(picked, target, n, links, rows, cols):
    half_rows = rows // 2
    half_cols = cols // 2
    count = links // LANES
    wide = 4 * half_cols
    short = half_rows // 4
    tall_iota = lax.broadcasted_iota(jnp.int32, (wide, LANES), 0).astype(jnp.int16)
    short_iota = lax.broadcasted_iota(jnp.int32, (short, LANES), 0)
    ones = jnp.ones((wide, LANES), BF16)
    total = jnp.zeros((wide, 10 * short), F32)
    group = count
    for g in range(count // group):
        lefts = []
        rights = []
        for c in range(g * group, (g + 1) * group):
            cell = target[n : n + 1, c * LANES : (c + 1) * LANES]
            row = cell // cols - (1 - n // 2) * half_rows
            col = cell % cols - (1 - n % 2) * half_cols
            short_at = jnp.broadcast_to(row % short, (short, LANES)) == short_iota
            place = (row // short * half_cols + col).astype(jnp.int16)
            wide_at = jnp.broadcast_to(place, (wide, LANES)) == tall_iota
            rights.append(jnp.where(wide_at, ones, jnp.zeros_like(ones)))
            pieces = []
            for f in range(5):
                value = picked[f, pl.ds(n * count + c, 1), :]
                high = value.astype(BF16).astype(F32)
                low = value - high
                for part in (high, low):
                    spread = jnp.broadcast_to(part, (short, LANES))
                    pieces.append(jnp.where(short_at, spread, 0.0).astype(BF16))
            lefts.append(jnp.concatenate(pieces, 0))
        left = jnp.concatenate(lefts, 1)
        right = jnp.concatenate(rights, 1)
        total = total + lax.dot_general(
            right, left, (((1,), (1,)), ((), ())), preferred_element_type=F32
        )
    return total.T


def remap_kernel(links, rows, cols, numbers, bases, target, *refs):
    count = len(numbers)
    quads, picked = refs[-2:]
    for i, (n, base) in enumerate(zip(numbers, bases)):
        gather_links(refs[i], base, n, links, picked)
        quads[i] = scatter_links(picked, target, n, links, rows, cols)


def remap(target, blocks, rows, cols, after=()):
    links = target.shape[1]
    numbers = tuple(n for n, _, _ in blocks)
    bases = tuple(base for _, _, base in blocks)
    vmem = pl.BlockSpec(memory_space=pltpu.VMEM)
    return pl.pallas_call(
        functools.partial(remap_kernel, links, rows, cols, numbers, bases),
        in_specs=[vmem] * (1 + len(blocks)) + [pl.BlockSpec(memory_space=pl.ANY)] * len(after),
        out_specs=vmem,
        out_shape=jax.ShapeDtypeStruct((len(blocks), 10 * rows // 8, 2 * cols), F32),
        scratch_shapes=[pltpu.VMEM((5, 4 * links // LANES, LANES), F32)],
        compiler_params=pltpu.CompilerParams(vmem_limit_bytes=16 << 20),
        name="remap",
    )(target, *[msg for _, msg, _ in blocks], *after)


def column_kernel(levels, own, from_west, from_east, fix):
    _, rows, _ = own.shape
    lane = lane_of((SUB, LANES))
    place_in_group = lane % 4
    spread = (2 * levels + lane // 4) % LANES
    for side in range(2):

        def mend(rb, carry):
            at = pl.ds(pl.multiple_of(rb * SUB, SUB), SUB)
            msg_at = pl.ds(pl.multiple_of(side * rows + rb * SUB, SUB), SUB)
            courant = own[4 + side, at, :]
            courant_before = pltpu.roll(courant, 1, 1)
            west_courant = jnp.take_along_axis(
                from_west[msg_at, :], spread, axis=1, mode="promise_in_bounds"
            )
            for t in range(2):
                msg_at = pl.ds(pl.multiple_of(t * rows + rb * SUB, SUB), SUB)
                west = from_west[msg_at, :]
                right = from_east[msg_at, :]
                if side:
                    west_one = pltpu.roll(west, LANES - 1, 1)
                    west_two = west
                    right_before = pltpu.roll(right, LANES - 1, 1)
                    right = pltpu.roll(right, LANES - 2, 1)
                else:
                    west_one = pltpu.roll(west, 1, 1)
                    west_two = pltpu.roll(west, 2, 1)
                    right_before = pltpu.roll(right, 1, 1)
                inner = own[2 * t + side, at, :]
                inner_next = pltpu.roll(inner, LANES - 1, 1)
                product = courant * right
                second = courant * (7.0 * right_before) - product + pltpu.roll(product, 1, 1)
                third = (
                    courant_before * (7.0 * inner - inner_next)
                    - courant * west_one
                    - west_courant * (7.0 * (west_one + inner) - (west_two + inner_next))
                )
                fourth = courant_before * west_two
                change = jnp.where(
                    place_in_group < 2,
                    jnp.where(place_in_group == 0, -product, second),
                    jnp.where(place_in_group == 2, third, fourth),
                )
                fix[t, side, at, :] = change * (-1.0 / 12.0)
            return carry

        lax.fori_loop(0, rows // SUB, mend, 0, unroll=8)


def column_fix(levels, own, from_west, from_east):
    _, rows, cols = own.shape
    vmem = pl.BlockSpec(memory_space=pltpu.VMEM)
    return pl.pallas_call(
        functools.partial(column_kernel, levels),
        in_specs=[vmem] * 3,
        out_specs=vmem,
        out_shape=pltpu.VMEM((2, 2, rows, cols), F32),
        compiler_params=pltpu.CompilerParams(vmem_limit_bytes=16 << 20),
        name="column_fix",
    )(own, from_west, from_east)


def main_kernel(
    chunk_rows,
    tables,
    cells,
    advected,
    diff,
    land,
    fix,
    own_rows,
    from_south,
    from_north,
    upper,
    lower,
    out,
    values,
    gains,
    surface,
    row_fix,
    out_sem,
):
    _, levels, rows, cols = cells.shape
    chunks = rows // chunk_rows
    lane = lane_of((SUB, LANES))

    def store(c, q):
        part = pl.ds(c * chunk_rows, chunk_rows)
        at = pl.ds(q * (levels // PARTS), levels // PARTS)
        return pltpu.make_async_copy(
            values.at[:, at, part, :], out.at[:, at, part, :], out_sem.at[c, q]
        )

    quads = [upper[0], upper[1], lower[0], lower[1]]
    short = rows // 8
    for pair in range(2):
        left = quads[2 * pair + 1]
        right = quads[2 * pair]
        for f in range(5):
            at = 2 * f * short
            one = left[at : at + short] + left[at + short : at + 2 * short]
            two = right[at : at + short] + right[at + short : at + 2 * short]
            for g in range(4):
                half = slice(g // 2 * LANES, g // 2 * LANES + LANES)
                a = one[:, half]
                b = two[:, half]
                if g % 2:
                    a = pltpu.roll(a, LANES // 2, 1)
                else:
                    b = pltpu.roll(b, LANES // 2, 1)
                merged = jnp.where(lane_of((short, LANES)) < LANES // 2, a, b)
                base = (1 - pair) * (rows // 2) + g * short
                surface[f, base : base + short, :] = merged
    for rb in range(rows // SUB):
        at = pl.ds(rb * SUB, SUB)
        s3 = surface[3, at, :]
        s4 = surface[4, at, :]
        surface[3, at, :] = 2.0 * jnp.sqrt(s3 * s3 + s4 * s4)

    half = levels // 2

    def plane(msg, p):
        return msg[p * levels : (p + 1) * levels, :]

    for t in range(2):
        inner_one = plane(own_rows, 3 + 2 * t)
        inner_two = plane(own_rows, 4 + 2 * t)
        below_two = plane(from_south, 2 * t)
        below_one = plane(from_south, 2 * t + 1)
        above_one = plane(from_north, 2 * t)
        above_two = plane(from_north, 2 * t + 1)
        first = plane(own_rows, 0) * below_one
        entering = plane(from_south, 4) * (7.0 * (below_one + inner_one) - (below_two + inner_two))
        last = plane(own_rows, 1) * above_one
        top = plane(own_rows, 2) * (7.0 * above_one - above_two)
        for p, change in enumerate((-first - entering, first, -last, top + last)):
            row_fix[t, p] = change * (-1.0 / 12.0)

    at_edge = (lane >= LANES - 2) | (lane < 2)
    sub = lax.broadcasted_iota(jnp.int32, (SUB, LANES), 0)
    blocks = chunk_rows // SUB

    def row_pair(t, k, p, at):
        one = jnp.broadcast_to(row_fix[t, p, pl.ds(k, 1), :], (SUB, LANES))
        two = jnp.broadcast_to(row_fix[t, p + 1, pl.ds(k, 1), :], (SUB, LANES))
        return jnp.where(sub == at, one, jnp.where(sub == at + 1, two, 0.0))

    def advect(t, k, base):
        side = k // half
        shift = (2 * LANES - 2 - 4 * (k % half)) % LANES
        result = []
        for i in range(blocks):
            at = pl.ds(base + i * SUB, SUB)
            edge = pltpu.roll(fix[t, side, at, :], shift, 1)
            value = advected[t, k, at, :] + jnp.where(at_edge, edge, 0.0)
            if base + i * SUB == 0:
                value = value + row_pair(t, k, 0, 0)
            if base + (i + 1) * SUB == rows:
                value = value + row_pair(t, k, 2, SUB - 2)
            result.append(value)
        return result

    for c in range(chunks):
        base = c * chunk_rows

        def forward(k, carry, last=False):
            new = []
            heat_all = advect(0, k, base)
            salt_all = advect(1, k, base)
            for i in range(blocks):
                r0 = base + i * SUB
                above, lead, heat, salt = carry[4 * i : 4 * i + 4]
                heat_in = heat_all[i] + surface[2, r0 : r0 + SUB, :] * tables[0, k]
                salt_in = salt_all[i]
                if last:
                    inverse = 1.0 / lead
                    below = above
                else:
                    below = diff[k, r0 : r0 + SUB, :] + surface[3, r0 : r0 + SUB, :] * tables[1, k]
                    pivot = lead + below
                    rough = pl.reciprocal(pivot, approx=True)
                    inverse = rough * (2.0 - pivot * rough)
                heat = (heat_in + above * heat) * inverse
                salt = (salt_in + above * salt) * inverse
                values[0, k, r0 : r0 + SUB, :] = heat
                values[1, k, r0 : r0 + SUB, :] = salt
                if not last:
                    gains[k, i * SUB : (i + 1) * SUB, :] = below * inverse
                    lead = 1.0 + below * (lead * inverse)
                new += [below, lead, heat, salt]
            return tuple(new)

        carry = []
        for i in range(blocks):
            r0 = base + i * SUB
            one = jnp.ones((SUB, LANES), F32)
            carry += [one, one, 0.5 * surface[0, r0 : r0 + SUB, :], 0.5 * surface[1, r0 : r0 + SUB, :]]
        spare = (levels - 1) % FORWARD
        carry = lax.fori_loop(0, levels - 1 - spare, forward, tuple(carry), unroll=FORWARD)
        for k in range(levels - 1 - spare, levels - 1):
            carry = forward(k, carry)
        carry = forward(levels - 1, carry, True)

        def finish(k, i, heat, salt):
            r0 = base + i * SUB
            wet = land[r0 : r0 + SUB, :] == 1
            values[0, k, r0 : r0 + SUB, :] = jnp.where(wet, heat, cells[0, k, r0 : r0 + SUB, :])
            values[1, k, r0 : r0 + SUB, :] = jnp.where(wet, salt, cells[1, k, r0 : r0 + SUB, :])

        def backward(step, carry):
            k = levels - 2 - step
            new = []
            for i in range(blocks):
                r0 = base + i * SUB
                heat, salt = carry[2 * i : 2 * i + 2]
                gain = gains[k, i * SUB : (i + 1) * SUB, :]
                heat = values[0, k, r0 : r0 + SUB, :] + gain * heat
                salt = values[1, k, r0 : r0 + SUB, :] + gain * salt
                finish(k, i, heat, salt)
                new += [heat, salt]
            return tuple(new)

        ends = []
        for i in range(blocks):
            heat, salt = carry[4 * i + 2 : 4 * i + 4]
            finish(levels - 1, i, heat, salt)
            ends += [heat, salt]
        carry = backward(0, tuple(ends))
        done = 1
        for q in reversed(range(PARTS)):
            until = levels - 1 - q * (levels // PARTS)
            while (until - done) % BACKWARD:
                carry = backward(done, carry)
                done += 1
            carry = lax.fori_loop(done, until, backward, carry, unroll=BACKWARD)
            done = until
            store(c, q).start()
    for c in range(chunks):
        for q in range(PARTS):
            store(c, q).wait()


def step(cells, advected, diff, land, messages, chunk_rows=64):
    _, levels, rows, cols = cells.shape
    depth = np.arange(levels)
    decay = np.exp(-4.0 * depth / levels)
    absorb = decay - np.exp(-4.0 * (depth + 1.0) / levels)
    tables = jnp.asarray(np.stack([0.5 * absorb, decay]), F32)
    chunks = rows // chunk_rows
    hbm = pl.BlockSpec(memory_space=pl.ANY)
    vmem = pl.BlockSpec(memory_space=pltpu.VMEM)
    return pl.pallas_call(
        functools.partial(main_kernel, chunk_rows),
        in_specs=[pl.BlockSpec(memory_space=pltpu.SMEM)] + [vmem] * (4 + len(messages)),
        out_specs=hbm,
        out_shape=jax.ShapeDtypeStruct(cells.shape, F32),
        scratch_shapes=[
            pltpu.VMEM((2, levels, rows, cols), F32),
            pltpu.VMEM((levels, chunk_rows, cols), F32),
            pltpu.VMEM((5, rows, cols), F32),
            pltpu.VMEM((2, 4, levels, cols), F32),
            pltpu.SemaphoreType.DMA((chunks, PARTS)),
        ],
        compiler_params=pltpu.CompilerParams(vmem_limit_bytes=16 << 20),
        name="step",
    )(tables, cells, advected, diff, land, *messages)


def ring(axis, by):
    length = lax.axis_size(axis)
    return [(i, (i + by) % length) for i in range(length)]


def diagonal():
    lats = lax.axis_size("lat")
    lons = lax.axis_size("lon")
    return [
        (i * lons + j, (i + 1) % lats * lons + (j + 1) % lons) for i in range(lats) for j in range(lons)
    ]


def local(
    tracers,
    east_courant,
    north_courant,
    diffusivity,
    land_sea,
    fluxes,
    source_cell,
    link_weight,
    target_cell,
):
    _, levels, rows, cols = tracers.shape
    target = target_cell[0]
    cells, east, own, to_east, to_west, to_north, to_south, corner, own_links, own_rows = load(
        tracers, east_courant, north_courant, fluxes, source_cell[0], link_weight[0]
    )
    from_corner = lax.ppermute(corner, ("lat", "lon"), diagonal())
    from_south = lax.ppermute(to_north, "lat", ring("lat", 1))
    from_north = lax.ppermute(to_south, "lat", ring("lat", -1))
    from_west = lax.ppermute(to_east, "lon", ring("lon", 1))
    from_east = lax.ppermute(to_west, "lon", ring("lon", -1))
    advected, diff = interior(cells, east, north_courant, diffusivity)
    upper = remap(target, [(0, own_links, 0), (1, from_west, 2 * rows)], rows, cols)
    fix = column_fix(levels, own, from_west, from_east)
    lower = remap(target, [(2, from_south, 5 * levels), (3, from_corner, 0)], rows, cols, [upper, fix])
    messages = (fix, own_rows, from_south, from_north, upper, lower)
    return step(cells, advected, diff, land_sea, messages)


def solution(mesh):
    in_specs = (
        P(None, None, "lat", "lon"),
        P(None, "lat", "lon"),
        P(None, "lat", "lon"),
        P(None, "lat", "lon"),
        P("lat", "lon"),
        P(None, ("lat", "lon")),
        P(("lat", "lon"), None, None),
        P(("lat", "lon"), None, None),
        P(("lat", "lon"), None, None),
    )
    out_specs = P(None, None, "lat", "lon")
    return jax.shard_map(local, mesh=mesh, in_specs=in_specs, out_specs=out_specs, check_vma=False)
```
